32 devices in a mesh: dp: 8 (over z, x), mp: 4 (over y, core).
Axes of the slice: x: 2, y: 2, z: 4, core: 2. Of those that a mesh axis runs over, the one named last changes fastest.
Arguments:
- patches: bfloat16 [64, 206, 768], P(('dp', 'mp')), may hold values from -9 to 9
- lengths: int32 [64], P(('dp', 'mp')), may hold values from 98 to 197, as said below
- tasks: int32 [64, 1], P(('dp', 'mp')), may hold values from 0 to 7
- prompt_master: float32 [8, 38400], P(None, ('dp', 'mp')), may hold values from -6 to 6
- first_moment: float32 [8, 38400], P(None, ('dp', 'mp')), may hold values from -0.0029296875 to 0.0029296875
- second_moment: float32 [8, 38400], P(None, ('dp', 'mp')), may hold values from 3.2552083e-09 to 1.3020833e-08
- gain_one: float32 [768], replicated, may hold values from 0.1 to 1.9
- gain_two: float32 [768], replicated, may hold values from 0.1 to 1.9
- w_qkv: bfloat16 [768, 3, 768], P('dp', None, 'mp'), may hold values from -0.21875 to 0.21875
- w_out: bfloat16 [768, 768], P('mp', 'dp'), may hold values from -0.875 to 0.875
- w_up: bfloat16 [768, 3072], P('dp', 'mp'), may hold values from -0.21875 to 0.21875
- w_down: bfloat16 [3072, 768], P('mp', 'dp'), may hold values from -0.109375 to 0.109375
- cotangent: bfloat16 [64, 256, 768], P('dp'), may hold values from -7.5 to 7.5
Outputs:
- block_out: bfloat16 [64, 256, 768], P(('dp', 'mp'))
- patch_grad: bfloat16 [64, 206, 768], P(('dp', 'mp'))
- prompt_grad: float32 [8, 38400], P(None, ('dp', 'mp'))
- grad_norm: float32 [], replicated
- new_first: float32 [8, 38400], P(None, ('dp', 'mp'))
- new_second: float32 [8, 38400], P(None, ('dp', 'mp'))
- new_master: float32 [8, 38400], P(None, ('dp', 'mp'))
- new_copy: bfloat16 [8, 38400], P(None, ('dp', 'mp'))
- rms_stats: float32 [3], replicated
The draws below stay inside these ranges and needn't reach their ends.
Inputs may be any that keep to these rules, and one draw needn't show every extreme that they name: `lengths`: some image has 197 valid patch rows. `tasks`: every prompt set is used by some image.
All inputs are finite; a program needn't handle non-finite values.
Results may differ from the reference program's by a relative error of at most 0.017.
Values may be sent and summed in bfloat16 or wider, within the bound.
A program may use at most 128 MiB of HBM per device.

```python
import math
import jax
import jax.numpy as jnp
from jax import lax

D = 768
HEADS = 12
HEAD_DIM = 64
FF = 3072
PROMPTS = 50
TASKS = 8
ROWS = 256
PATCH_TOKENS = 197
STEP = 10
PATCH = 206
IMAGES = 64


def draw_patches(key, part):
    key = jax.random.fold_in(key, 5)
    first_key, second_key = jax.random.split(key)
    place = jnp.arange(IMAGES, dtype=jnp.float32) / max(IMAGES - 1, 1)
    base = jnp.clip(jax.random.normal(first_key, (IMAGES, PATCH, D), jnp.float32), -4.0, 4.0)
    level = 0.6 + 1.2 * place
    rough = jax.random.uniform(second_key, (IMAGES, 1, 1), jnp.float32, 0.8, 1.25)
    return (base * level[:, None, None] * rough).astype(jnp.bfloat16)


def draw_lengths(key, part):
    key = jax.random.fold_in(key, 11)
    first_key, second_key = jax.random.split(key)
    base = jax.random.randint(first_key, (IMAGES,), PATCH_TOKENS // 2, PATCH_TOKENS + 1, dtype=jnp.int32)
    chosen_spot = jax.random.randint(second_key, (), 0, IMAGES, dtype=jnp.int32)
    return base.at[chosen_spot].set(PATCH_TOKENS)


def draw_cotangent(key, part):
    key = jax.random.fold_in(key, 17)
    place = jnp.arange(ROWS, dtype=jnp.float32) / max(PROMPTS - 1, 1)
    lead_mask = jnp.arange(ROWS) < PROMPTS
    base = jnp.clip(jax.random.normal(key, (IMAGES, ROWS, D), jnp.float32), -4.0, 4.0)
    level = jnp.where(lead_mask, 0.6 + 1.2 * place, 1.0)
    return (base * level[None, :, None]).astype(jnp.bfloat16)


def level_of(own_key, shape, pieces, low, top_value):
    loudness = 1.0
    for position, shards_of in pieces:
        draws = jax.random.uniform(jax.random.fold_in(jax.random.fold_in(own_key, 6), position), (shards_of,), jnp.float32, low / len(pieces), top_value / len(pieces))
        loudness = loudness * jnp.repeat(jnp.exp(draws), shape[position] // shards_of).reshape((-1,) + (1,) * (len(shape) - 1 - position))
    return loudness


def choose_distinct(stream_key, rows, number_of, top, lift):
    ranking = jax.random.permutation(jax.random.fold_in(stream_key, 1), number_of)
    favour = ranking
    for power in range(3):
        favour = favour * favour // number_of
    favour = favour * lift // number_of
    lots = jax.random.randint(jax.random.fold_in(stream_key, 2), (rows, number_of), 0, 4096) + favour
    fixed_rows = jax.random.permutation(jax.random.fold_in(stream_key, 3), rows)[jnp.arange(number_of) % rows]
    lots = jnp.where(jnp.arange(rows)[:, None] == fixed_rows[None, :], 1 << 14, lots)
    score = lots * number_of + jnp.arange(number_of)
    return lax.top_k(score.astype(jnp.int32), top)[1].astype(jnp.int32)


def normal_values(own_key, dims, width, bound, pieces=(), kind=jnp.bfloat16):
    entries = width * jax.random.normal(own_key, dims, jnp.float32)
    if pieces:
        entries = entries * level_of(own_key, dims, pieces, -0.22, 0.18)
    return jnp.clip(entries, -bound, bound).astype(kind)


def setup_inputs(seed: int = 0) -> dict:
    seeds = jax.random.split(jax.random.key(seed), 14)
    return {
        "patches": draw_patches(jax.random.fold_in(seeds[13], 71), 0),
        "lengths": draw_lengths(jax.random.fold_in(seeds[13], 71), 0),
        "tasks": choose_distinct(seeds[2], IMAGES, TASKS, 1, 2048),
        "prompt_master": normal_values(seeds[3], (TASKS, PROMPTS * D), 1.0, 6.0, ((1, 32),), jnp.float32),
        "first_moment": normal_values(seeds[4], (TASKS, PROMPTS * D), (0.11 / (TASKS * PROMPTS * D) ** 0.5), 0.0029296875, ((1, 32),), jnp.float32),
        "second_moment": jnp.clip(jnp.exp(math.log(1.302083330045889e-08) - 1.3862944 * jax.random.uniform(seeds[5], (TASKS, PROMPTS * D), jnp.float32) ** level_of(seeds[5], (TASKS, PROMPTS * D), ((1, 32),), -0.2, 0.2)), 3.2552083251147224e-09, 1.302083330045889e-08),
        "gain_one": jnp.clip(1.0 + 0.18 * jax.random.normal(seeds[6], (D,), jnp.float32), 0.1, 1.9),
        "gain_two": jnp.clip(1.0 + 0.18 * jax.random.normal(seeds[7], (D,), jnp.float32), 0.1, 1.9),
        "w_qkv": normal_values(seeds[8], (D, 3, D), D ** -0.5, 0.21875, ((0, 8), (2, 4))),
        "w_out": normal_values(seeds[9], (D, D), (D // 16) ** -0.5, 0.875, ((0, 4), (1, 8))),
        "w_up": normal_values(seeds[10], (D, FF), D ** -0.5, 0.21875, ((0, 8), (1, 4))),
        "w_down": normal_values(seeds[11], (FF, D), FF ** -0.5, 0.109375, ((0, 4), (1, 8))),
        "cotangent": draw_cotangent(jax.random.fold_in(seeds[13], 71), 0),
    }


@jax.custom_vjp
def low(v):
    return lax.optimization_barrier(v.astype(jnp.bfloat16)).astype(jnp.float32)

@jax.custom_vjp
def low_back(v):
    return v

def low_keep(v):
    return (low(v), None)

def low_pass(kept, grad):
    return (grad,)

def back_keep(v):
    return (v, None)

def back_low(kept, grad):
    return (low(grad),)
low.defvjp(low_keep, low_pass)
low_back.defvjp(back_keep, back_low)
highest = lax.Precision.HIGHEST
eps_norm = 1e-06
clip_level = 1.0
beta_one = 0.9
beta_two = 0.999
learn_rate = 3.0
decay_rate = 0.05
adam_eps = 1e-08

def layer_norm(values, gain):
    centre = lax.optimization_barrier(jnp.mean(values, axis=-1, keepdims=True))
    shifted = values - centre
    spread = lax.optimization_barrier(jnp.mean(shifted * shifted, axis=-1, keepdims=True))
    return shifted * lax.rsqrt(spread + eps_norm) * gain

def block_forward(patch_rows, prompt_table, chosen, key_mask, w_mix, w_proj, w_expand, w_reduce, gain_one, gain_two):
    block_count = patch_rows.shape[0]
    lead_part = jnp.einsum('bt,tpd->bpd', chosen, prompt_table, precision=highest)
    residual = jnp.concatenate([lead_part, patch_rows], axis=1)
    normed = low(layer_norm(residual, gain_one))
    mixed_qkv = low_back(low(jnp.einsum('brd,dce->brce', normed, w_mix, precision=highest)))
    split_heads = mixed_qkv.reshape(block_count, ROWS, 3, HEADS, HEAD_DIM)
    queries = split_heads[:, :, 0]
    keys_all = split_heads[:, :, 1]
    values = split_heads[:, :, 2]
    scores = jnp.einsum('bqhe,bkhe->bhqk', queries, keys_all, precision=highest) * (1.0 / math.sqrt(HEAD_DIM))
    scores = low_back(scores)
    scores = jnp.where(key_mask[:, None, None, :], scores, -1e+30)
    row_top = lax.optimization_barrier(jnp.max(scores, axis=-1, keepdims=True))
    exponent = jnp.exp(scores - row_top)
    attend_weights = low(exponent / lax.optimization_barrier(jnp.sum(exponent, axis=-1, keepdims=True)))
    context = jnp.einsum('bhqk,bkhe->bqhe', attend_weights, values, precision=highest).reshape(block_count, ROWS, D)
    context = low_back(low(context))
    attn_out = low_back(jnp.einsum('brc,cd->brd', context, w_proj, precision=highest))
    residual_two = residual + attn_out
    normed_two = low(layer_norm(residual_two, gain_two))
    upward = low_back(jnp.einsum('brd,df->brf', normed_two, w_expand, precision=highest))
    act_units = low(jax.nn.gelu(upward, approximate=False))
    mlp_out = low_back(jnp.einsum('brf,fd->brd', act_units, w_reduce, precision=highest))
    return (residual_two + mlp_out, attn_out, mlp_out)

def reference(patches, lengths, tasks, prompt_master, first_moment, second_moment, gain_one, gain_two, w_qkv, w_out, w_up, w_down, cotangent):
    prompt_table = lax.optimization_barrier(prompt_master.astype(jnp.bfloat16)).astype(jnp.float32)
    prompt_table = prompt_table.reshape(TASKS, PROMPTS, D)
    w_mix = w_qkv.astype(jnp.float32)
    w_proj = w_out.astype(jnp.float32)
    w_expand = w_up.astype(jnp.float32)
    w_reduce = w_down.astype(jnp.float32)
    block_images = math.gcd(IMAGES, max(1, 4096 // ROWS))

    def one_block(carry, block_index):
        grad_table, square_sums = carry
        first_row = block_index * block_images
        patch_part = lax.dynamic_slice_in_dim(patches, first_row, block_images, 0).astype(jnp.float32)
        length_part = lax.dynamic_slice_in_dim(lengths, first_row, block_images, 0)
        task_part = lax.dynamic_slice_in_dim(tasks, first_row, block_images, 0)
        grad_part = lax.dynamic_slice_in_dim(cotangent, first_row, block_images, 0).astype(jnp.float32)
        key_mask = jnp.arange(ROWS, dtype=jnp.int32)[None, :] < (PROMPTS + length_part)[:, None]
        chosen = (task_part[:, 0:1] == jnp.arange(TASKS, dtype=jnp.int32)[None, :]).astype(jnp.float32)

        def forward(rows_in, table_in):
            return block_forward(rows_in, table_in, chosen, key_mask, w_mix, w_proj, w_expand, w_reduce, gain_one, gain_two)
        (block_sum, attn_out, mlp_out), pull = jax.vjp(forward, patch_part, prompt_table)
        grad_patch, grad_prompt = pull((grad_part, jnp.zeros_like(attn_out), jnp.zeros_like(mlp_out)))
        live_rows = key_mask.astype(jnp.float32)[:, :, None]
        part_sums = jnp.stack([jnp.sum(block_sum * block_sum * live_rows), jnp.sum(attn_out * attn_out * live_rows), jnp.sum(mlp_out * mlp_out * live_rows)])
        return ((grad_table + grad_prompt, square_sums + part_sums), (block_sum.astype(jnp.bfloat16), grad_patch.astype(jnp.bfloat16)))
    start_carry = (jnp.zeros((TASKS, PROMPTS, D), jnp.float32), jnp.zeros((3,), jnp.float32))
    (grad_table, square_sums), (outs_all, grads_all) = lax.scan(one_block, start_carry, jnp.arange(IMAGES // block_images, dtype=jnp.int32))
    block_out = outs_all.reshape(IMAGES, ROWS, D)
    patch_grad = grads_all.reshape(IMAGES, PATCH, D)
    task_grad = grad_table.reshape(TASKS, PROMPTS * D)
    grad_norm = jnp.sqrt(jnp.sum(task_grad * task_grad))
    prompt_grad = task_grad * (clip_level / jnp.maximum(grad_norm, clip_level))
    new_first = beta_one * first_moment + (1.0 - beta_one) * prompt_grad
    new_second = beta_two * second_moment + (1.0 - beta_two) * prompt_grad * prompt_grad
    step_size = new_first / (1.0 - beta_one ** STEP) / (jnp.sqrt(new_second / (1.0 - beta_two ** STEP)) + adam_eps)
    new_master = prompt_master - learn_rate * (step_size + decay_rate * prompt_master)
    live_count = jnp.sum(PROMPTS + lengths).astype(jnp.float32)
    rms_stats = jnp.sqrt(square_sums / (live_count * D))
    return (block_out, patch_grad, prompt_grad, grad_norm, new_first, new_second, new_master, new_master.astype(jnp.bfloat16), rms_stats)
```

```python
import functools
import math

import jax
import jax.numpy as jnp
from jax import lax
from jax.experimental import pallas as pl
from jax.experimental.pallas import tpu as pltpu
from jax.sharding import PartitionSpec as P

HEAD_DIM = 64
STEP = 10
MESH = pl.DeviceIdType.MESH
F32 = jnp.float32
BF16 = jnp.bfloat16

eps_norm = 1e-06
clip_level = 1.0
beta_one = 0.9
beta_two = 0.999
learn_rate = 3.0
decay_rate = 0.05
adam_eps = 1e-08

D = 768
ROWS = 256
LEAD = 50
PATCH = 206
IMGS = 2
TASKS = 8
PART = 1200
PADP = 1280
NDEV = 32
CHUNK = 256
CHUNKS = 3
RING = 24


def run_if(cond, f):
    if cond is None:
        f()
    else:
        pl.when(cond())(f)


def both(*conds):
    conds = [c for c in conds if c is not None]
    if not conds:
        return None

    def value():
        out = conds[0]()
        for c in conds[1:]:
            out = jnp.logical_and(out, c())
        return out

    return value


class Net:
    def __init__(self, send_sem, recv_sem):
        self.send_sem, self.recv_sem = send_sem, recv_sem
        self.sent = self.used = 0
        dp, mp = lax.axis_index("dp"), lax.axis_index("mp")
        z, x, y, c = dp // 2, dp % 2, mp // 2, mp % 2
        self.z, self.x, self.y, self.c = z, x, y, c
        self.dp, self.mp = dp, mp
        self.peer = {
            "x": (2 * z + 1 - x, mp),
            "y": (dp, (1 - y) * 2 + c),
            "c": (dp, 2 * y + 1 - c),
            "u": (jnp.minimum(2 * z + 2 + x, 6 + x), mp),
            "d": (jnp.maximum(2 * z - 2 + x, x), mp),
        }
        self.ring = [None] * RING

    def alloc(self, n):
        first = self.used
        self.used += n
        return first

    def send(self, way, view, sem, cond=None):
        i = self.sent % RING
        self.sent += 1
        if self.ring[i] is not None:
            self.wait_sent(i)

        def copy():
            v = view()
            return pltpu.make_async_remote_copy(
                src_ref=v,
                dst_ref=v,
                send_sem=self.send_sem.at[i],
                recv_sem=self.recv_sem.at[sem()],
                device_id=self.peer[way],
                device_id_type=MESH,
            )

        run_if(cond, lambda: copy().start())
        self.ring[i] = (cond, copy)

    def wait_sent(self, i):
        cond, copy = self.ring[i]
        run_if(cond, lambda: copy().wait_send())
        self.ring[i] = None

    def recv(self, view, sem, cond=None):
        def wait():
            v = view()
            pltpu.make_async_copy(v, v, self.recv_sem.at[sem()]).wait()

        run_if(cond, wait)

    def finish(self):
        for i in range(RING):
            if self.ring[i] is not None:
                self.wait_sent(i)


def gather_events(net, G, W, off, split):
    z, x, y, c = net.z, net.x, net.y, net.c
    r1, r2, r3, rows = split
    f_sem, zs_sem, zp_sem, m_sem, l_sem, c_sem = (net.alloc(n) for n in (1, 4, 4, 4, 4, 4))
    not_top, not_low = (lambda: z < 3), (lambda: z > 0)
    every = slice(None)

    def V(yy, d, first, last, other=False):
        def view():
            core = (1 - c) if other else c
            cols = pl.ds(pl.multiple_of(core * W, 128), W)
            return G.at[:, yy, d() if callable(d) else d, pl.ds(first, last - first), cols]

        return view

    def two(p):
        return lambda: pl.ds(2 * p(), 2)

    def one(p):
        return lambda: 2 * p() + x

    def at(sem, p):
        return lambda: sem + p()

    own = lambda: z

    def send(way, yy, d, first, last, sem, cond=None):
        if last > first:
            net.send(way, V(yy, d, first, last), sem, cond)

    def planes(k):
        if k == 0:
            return [(own, None)]
        return [(lambda: z - k, lambda: z >= k), (lambda: z + k, lambda: z + k <= 3)]

    def middle(p, cond):
        send("x", y, one(p), r1, r2, at(m_sem, p), cond)
        send("y", y, one(p), r2, r3, at(m_sem, p), cond)

    def start():
        send("x", y, one(own), 0, r1, lambda: f_sem)
        send("y", y, one(own), r3, rows, lambda: f_sem)
        send("u", y, one(own), r1, r3, at(zs_sem, own), not_top)
        send("d", y, one(own), r1, r3, at(zs_sem, own), not_low)
        middle(own, None)

    def pair(way, p, cond):
        send(way, y, two(p), 0, r1, at(zp_sem, p), cond)
        send(way, every, one(p), r3, rows, at(zp_sem, p), cond)

    def first_hop():
        net.recv(V(y, one(own), 0, r1 + rows - r3), lambda: f_sem)
        pair("u", own, not_top)
        pair("d", own, not_low)

    def ways(k):
        return [(p, cond, w, far) for (p, cond), w, far in zip(planes(k), "ud", (not_top, not_low))]

    def single_hop(k):
        for p, cond, way, far in ways(k):
            net.recv(V(y, one(p), r1, r3), at(zs_sem, p), cond)
            if k < 3:
                send(way, y, one(p), r1, r3, at(zs_sem, p), both(cond, far))
            middle(p, cond)

    def pair_hop(k):
        for p, cond, way, far in ways(k):
            net.recv(V(y, two(p), 0, r1 + rows - r3), at(zp_sem, p), cond)
            if k < 3:
                pair(way, p, both(cond, far))

    def last_hop(k):
        for p, cond in planes(k):
            if r3 > r1:
                net.recv(V(y, one(p), r1, r3), at(m_sem, p), cond)
            send("y", y, two(p), 0, r2, at(l_sem, p), cond)
            send("x", every, one(p), r2, rows, at(l_sem, p), cond)

    def to_core(k):
        for p, cond in planes(k):
            net.recv(V(y, two(p), 0, rows), at(l_sem, p), cond)
            send("c", every, two(p), 0, rows, at(c_sem, p), cond)

    def from_core(k):
        for p, cond in planes(k):
            net.recv(V(every, two(p), 0, rows, other=True), at(c_sem, p), cond)

    ev = [(off, start), (off + 1, first_hop)]
    for k in (1, 2, 3):
        if r3 > r1:
            ev.append((off + k, functools.partial(single_hop, k)))
        ev.append((off + 1 + k, functools.partial(pair_hop, k)))
    for k in (0, 1, 2, 3):
        ev.append((off + 1 + k + 0.5, functools.partial(last_hop, k)))
        ev.append((off + 2 + k + 0.3, functools.partial(to_core, k)))
        ev.append((off + 3 + k + 0.6, functools.partial(from_core, k)))
    return ev


class Events:
    def __init__(self, items):
        self.items = sorted(items, key=lambda e: e[0])

    def take(self, limit):
        out = []
        while self.items and self.items[0][0] <= limit:
            out.append(self.items.pop(0)[1])
        return out

    def run(self, limit):
        for f in self.take(limit):
            f()


def at_step(t, groups):
    for j, group in enumerate(groups):
        if group:

            def go(group=group):
                for f in group:
                    f()

            pl.when(t == j)(go)


def nn(a, b):
    return lax.dot_general(a, b, (((1,), (0,)), ((), ())), preferred_element_type=F32)


def nt(a, b):
    return lax.dot_general(a, b, (((1,), (1,)), ((), ())), preferred_element_type=F32)


def tn(a, b):
    return lax.dot_general(a, b, (((0,), (0,)), ((), ())), preferred_element_type=F32)


def norm_parts(v):
    centre = jnp.mean(v, axis=-1, keepdims=True)
    shifted = v - centre
    spread = jnp.mean(shifted * shifted, axis=-1, keepdims=True)
    scaled = lax.rsqrt(spread + eps_norm)
    return shifted * scaled, scaled


def norm_back(v, gain, upstream):
    normal, scaled = norm_parts(v)
    weighted = upstream * gain
    return scaled * (
        weighted
        - jnp.mean(weighted, axis=-1, keepdims=True)
        - normal * jnp.mean(weighted * normal, axis=-1, keepdims=True)
    )


def keep(lanes, low, high):
    return jnp.where(lanes, low, high)


def layer_kernel(
    patches, lengths, tasks, master, gain_one, gain_two, a_in, u_in, d_in, cot_hbm,
    out_block, out_patch, out_task, out_stats,
    GP, GA, GM, LOC, SEL, RES, N1, QKV, PT, CTX, RES2, N2, COT, ACT, GU, MACC, GACC, G2B, DM, LEADR,
    SEND, RECV, ONEHOT, SREC, STSUM, local_sem, send_sem, recv_sem, all_sem,
):
    net = Net(send_sem, recv_sem)
    z, x, y, c, dp, mp = net.z, net.x, net.y, net.c, net.dp, net.mp
    device = dp * 4 + mp

    def own_cols(w):
        return pl.ds(pl.multiple_of(c * w, 128), w)

    cot_copy = pltpu.make_async_copy(cot_hbm.at[pl.ds(mp * IMGS, IMGS)], COT, local_sem.at[0])
    cot_copy.start()
    copies = [pltpu.make_async_copy(a_in, GA.at[0, y, dp, :, own_cols(D)], local_sem.at[1])]
    for i in range(CHUNKS):
        for j, w in enumerate((u_in, d_in)):
            copies.append(
                pltpu.make_async_copy(
                    w.at[:, pl.ds(CHUNK * i, CHUNK)],
                    GM.at[i, j, y, dp, :, own_cols(CHUNK)],
                    local_sem.at[2 + 2 * i + j],
                )
            )
    for copy in copies:
        copy.start()
    barrier = pltpu.get_barrier_semaphore()
    for i in range(8):
        for j in range(4):
            @pl.when(jnp.logical_or(dp != i, mp != j))
            def _():
                pl.semaphore_signal(barrier, inc=1, device_id=(i, j), device_id_type=MESH)

    LOC[:, 0:PART] = master[...]
    lane = lax.broadcasted_iota(jnp.int32, (TASKS, PADP - PART), 1)
    LOC[:, PART:PADP] = jnp.where(
        lane == 0, tasks[0, 0].astype(F32), jnp.where(lane == 1, tasks[1, 0].astype(F32), 0.0)
    )
    half = PADP // 2
    GP[0, pl.ds(y, 1), pl.ds(dp, 1), :, own_cols(half)] = (
        jnp.concatenate([LOC[:, 0:half], LOC[:, half:PADP]], axis=0).astype(BF16)[None, None]
    )
    for copy in copies:
        copy.wait()
    pl.semaphore_wait(barrier, NDEV - 1)

    split = (32, 48, 64, 96)
    ev = gather_events(net, GP, half, -0.5, (16, 16, 16, 16))
    ev += gather_events(net, GA, D, 0.0, split)
    for i in range(CHUNKS):
        ev += gather_events(net, GM.at[i], CHUNK, 1.51 * (i + 1), split)
    ev = [(-1 + 0.01 * k if f.__name__ == "start" else k, f) if hasattr(f, "__name__") else (k, f) for k, f in ev]
    events = Events(ev)

    g1 = gain_one[...]
    g2 = gain_two[...]
    limits = [lengths[b] + LEAD for b in range(IMGS)]
    live = [
        (lax.broadcasted_iota(jnp.int32, (ROWS, 1), 0) < limits[b]).astype(F32) for b in range(IMGS)
    ]

    events.run(0.5)
    for b in range(IMGS):
        RES[b, LEAD:ROWS, :] = patches[b].astype(F32)
    MACC[...] = jnp.zeros_like(MACC)
    GACC[...] = jnp.zeros_like(GACC)
    SEND[...] = jnp.zeros_like(SEND)
    events.run(6.11)

    task_rows = lax.broadcasted_iota(jnp.int32, (TASKS, 1), 0)

    def pick(d, _):
        dd, mm = d // 4, d % 4
        raw = GP[0, mm // 2, dd, :, pl.ds(pl.multiple_of((mm % 2) * half, 128), half)].astype(F32)
        low, high = raw[0:8], raw[8:16]
        rep, j = d // 16, d % 16
        for b in range(IMGS):
            hot = (task_rows == tasks[b, 0]).astype(F32)
            row = 2 * rep + b
            SEL[j, pl.ds(row, 1), 0:half] = jnp.sum(low * hot, axis=0, keepdims=True)
            SEL[j, pl.ds(row, 1), half:PADP] = jnp.sum(high * hot, axis=0, keepdims=True)
        base = PART - half
        for b in range(IMGS):
            which = high[0:1, base + b : base + b + 1]
            ONEHOT[d, b] = (
                lax.broadcasted_iota(jnp.int32, (TASKS, 128), 0).astype(F32) == which
            ).astype(F32)
        return 0

    lax.fori_loop(0, NDEV, pick, 0)
    wide = lax.broadcasted_iota(jnp.int32, (4, D), 1)
    for r in range(25):
        j, off = (D * r) // PART, (D * r) % PART
        first = min(D, PART - off)
        low = SEL[j, 0:4, :]
        seg = (pltpu.roll(low, PADP - off, 1) if off else low)[:, 0:D]
        if first < D:
            seg = jnp.where(wide < first, seg, pltpu.roll(SEL[j + 1, 0:4, :], first, 1)[:, 0:D])
        for rep in range(2):
            for b in range(IMGS):
                RES[b, 25 * rep + r : 25 * rep + r + 1, :] = seg[2 * rep + b : 2 * rep + b + 1]

    for b in range(IMGS):
        N1[b] = (norm_parts(RES[b])[0] * g1).astype(BF16)
    events.run(6.61)

    def weight(ref, core, first, width, span):
        cols = pl.ds(pl.multiple_of(core * span + first, 128), width)
        return ref[:, :, cols].reshape(D, width)

    left = lax.broadcasted_iota(jnp.int32, (ROWS, 128), 1) < HEAD_DIM
    scale = 1.0 / math.sqrt(HEAD_DIM)
    wide = lax.broadcasted_iota(jnp.int32, (1, 640), 1)
    q_scale = jnp.where((wide < 128) | ((wide >= 384) & (wide < 448)), scale, 1.0)

    def split_keys(first, step, n):
        return [events.take(first + step * (j + 1)) for j in range(n)]

    groups = split_keys(6.61, 0.15, 4)

    def project(t, _):
        at_step(t, groups)
        w = weight(GA.at[0, t // 2], t % 2, 0, 640, D)
        mixed = nn(N1[...].reshape(IMGS * ROWS, D), w).astype(BF16).astype(F32) * q_scale
        QKV[t] = mixed.astype(BF16).reshape(IMGS, ROWS, 640)
        return 0

    lax.fori_loop(0, 4, project, 0)

    key_rows = lax.broadcasted_iota(jnp.int32, (ROWS, ROWS), 0)
    zero = jnp.zeros((), BF16)
    groups_a = split_keys(7.2, 0.15, 8)

    def attend(t, _):
        at_step(t, groups_a)
        b, m = t // 4, t % 4
        tile = lambda i: QKV[m, b, :, 128 * i : 128 * i + 128]
        q01, k01, v01, q2v2, k2 = (tile(i) for i in range(5))
        mask = key_rows < (lengths[b] + LEAD)

        def soft(keys, queries):
            s = jnp.where(mask, nt(keys, queries), -1e30)
            e = jnp.exp(s - jnp.max(s, axis=0, keepdims=True))
            return (e * (1.0 / jnp.sum(e, axis=0, keepdims=True))).astype(BF16)

        p0 = soft(k01, keep(left, q01, zero))
        p1 = soft(k01, keep(left, zero, q01))
        p2 = soft(k2, keep(left, q2v2, zero))
        PT[t, 0], PT[t, 1], PT[t, 2] = p0, p1, p2
        CTX[b, :, pl.ds(pl.multiple_of(m * 256, 128), 128)] = keep(left, 0.0, tn(p2, q2v2)).astype(BF16)
        CTX[b, :, pl.ds(pl.multiple_of(m * 256 + 128, 128), 128)] = keep(
            left, tn(p0, v01), tn(p1, v01)
        ).astype(BF16)
        return 0

    lax.fori_loop(0, 8, attend, 0)

    sums = [jnp.zeros((1, 1), F32) for _ in range(3)]

    def total(v):
        return jnp.sum(jnp.sum(v, axis=0, keepdims=True), axis=1, keepdims=True)

    for b in range(IMGS):
        events.run(8.4 + 0.2 * (b + 1))
        attn = jnp.zeros((ROWS, D), F32)
        for m in range(4):
            attn += nt(CTX[b, :, 256 * m : 256 * m + 256], weight(GA.at[0, m // 2], m % 2, 512, 256, D))
        sums[1] += total(attn * attn * live[b])
        res2 = RES[b] + attn
        RES2[b] = res2
        N2[b] = (norm_parts(res2)[0] * g2).astype(BF16)
    cot_copy.wait()

    done = [1.51 * (i + 1) + 6.61 for i in range(CHUNKS)]
    groups_m = [[], [], [], [], [], []]
    for i in range(CHUNKS):
        groups_m[2 * i] = events.take(done[i])
        groups_m[2 * i + 1] = events.take(done[i] + 0.6)

    def feed(t, _):
        at_step(t, groups_m)
        i, yy = t // 2, t % 2
        rows2 = N2[...].reshape(IMGS * ROWS, D)
        cot = COT[...].reshape(IMGS * ROWS, D)
        for core in range(2):
            up = nn(rows2, weight(GM.at[i, 0, yy], core, 0, CHUNK, CHUNK))
            back = nn(cot, weight(GM.at[i, 1, yy], core, 0, CHUNK, CHUNK))
            cumul = 0.5 * (1.0 + lax.erf(up * 0.7071067811865476))
            density = jnp.exp(-0.5 * up * up) * 0.3989422804014327
            ACT[:, CHUNK * core : CHUNK * (core + 1)] = (up * cumul).astype(BF16)
            GU[:, CHUNK * core : CHUNK * (core + 1)] = (back * (cumul + up * density)).astype(BF16)
        wide_d = weight(GM.at[i, 1, yy], 0, 0, 2 * CHUNK, CHUNK)
        MACC[...] += nt(ACT[...], wide_d).reshape(IMGS, ROWS, D)
        wide_u = weight(GM.at[i, 0, yy], 0, 0, 2 * CHUNK, CHUNK)
        GACC[...] += nt(GU[...], wide_u).reshape(IMGS, ROWS, D)
        return 0

    lax.fori_loop(0, 2 * CHUNKS, feed, 0)
    events.run(1e9)

    for b in range(IMGS):
        mlp = MACC[b]
        block = RES2[b] + mlp
        out_block[b] = block.astype(BF16)
        sums[0] += total(block * block * live[b])
        sums[2] += total(mlp * mlp * live[b])
        g = COT[b].astype(F32) + norm_back(RES2[b], g2, GACC[b])
        MACC[b] = g
        G2B[b] = g.astype(BF16)

    def attend_back(t, _):
        b, m = t // 4, t % 4
        tile = lambda i: QKV[m, b, :, 128 * i : 128 * i + 128]
        q01, k01, v01, q2v2, k2 = (tile(i) for i in range(5))
        cols = pl.ds(pl.multiple_of((m % 2) * D + 512, 128), 256)
        w = GA[0, m // 2, :, :, cols].reshape(D, 256)
        dctx = nn(G2B[b], w).astype(BF16)
        c2, c01 = dctx[:, 0:128], dctx[:, 128:256]

        def back(p, v, grad):
            pf = p.astype(F32)
            dp_ = nt(v, grad)
            inner = jnp.sum(pf * dp_, axis=0, keepdims=True)
            return (pf * (dp_ - inner)).astype(BF16)

        p0, p1, p2 = PT[t, 0], PT[t, 1], PT[t, 2]
        s0 = back(p0, keep(left, v01, zero), c01)
        s1 = back(p1, keep(left, zero, v01), c01)
        s2 = back(p2, keep(left, zero, q2v2), c2)
        DM[m, b, :, 0:128] = (keep(left, tn(s0, k01), tn(s1, k01)) * scale).astype(BF16)
        DM[m, b, :, 128:256] = keep(left, nn(s0, q01), nn(s1, q01)).astype(BF16)
        DM[m, b, :, 256:384] = keep(left, nn(p0, c01), nn(p1, c01)).astype(BF16)
        DM[m, b, :, 384:512] = keep(left, tn(s2, k2) * scale, nn(p2, c2)).astype(BF16)
        DM[m, b, :, 512:640] = keep(left, nn(s2, q2v2), 0.0).astype(BF16)
        return 0

    lax.fori_loop(0, 8, attend_back, 0)

    for b in range(IMGS):
        grad = jnp.zeros((ROWS, D), F32)
        for m in range(4):
            grad += nt(DM[m, b], weight(GA.at[0, m // 2], m % 2, 0, 640, D))
        grad = MACC[b] + norm_back(RES[b], g1, grad)
        GACC[b] = grad
        out_patch[b] = GACC[b, LEAD:ROWS, :].astype(BF16)

    for rep in range(2):
        for b in range(IMGS):
            LEADR[:, 2 * rep + b : 2 * rep + b + 1, :] = GACC[b, 25 * rep : 25 * rep + 25, :][:, None, :]
    wide = lax.broadcasted_iota(jnp.int32, (4, PADP), 1)
    for q in range(16):
        r, off = (PART * q) // D, (PART * q) % D
        msg, have = None, -off
        while have < PART:
            row = jnp.concatenate([LEADR[r, 0:4, :], jnp.zeros((4, PADP - D), F32)], axis=1)
            moved = pltpu.roll(row, have % PADP, 1) if have % PADP else row
            msg = moved if msg is None else jnp.where(wide < have, msg, moved)
            have += D
            r += 1
        msg = jnp.where(wide < PART, msg, 0.0)
        SEND[q] = msg[0:2]
        SEND[16 + q] = msg[2:4]

    def swap(d, what, start):
        i, j = d // 4, d % 4

        @pl.when(d != device)
        def _():
            pltpu.make_async_remote_copy(
                src_ref=what(d, True),
                dst_ref=what(device, False),
                send_sem=all_sem.at[2 * start],
                recv_sem=all_sem.at[2 * start + 1],
                device_id=(i, j),
                device_id_type=MESH,
            ).start()

    def to_owner(d, _):
        swap(d, lambda k, mine: SEND.at[k] if mine else RECV.at[k], 0)
        return 0

    lax.fori_loop(0, NDEV, to_owner, 0)
    RECV[pl.ds(device, 1)] = SEND[pl.ds(device, 1)]
    others = RECV.at[pl.ds(0, NDEV - 1)]
    pltpu.make_async_copy(others, others, all_sem.at[1]).wait()

    def add(s, acc):
        acc = acc + jnp.concatenate([ONEHOT[s, 0]] * (PADP // 128), axis=1) * RECV[s, 0:1, :]
        return acc + jnp.concatenate([ONEHOT[s, 1]] * (PADP // 128), axis=1) * RECV[s, 1:2, :]

    task_grad = lax.fori_loop(0, NDEV, add, jnp.zeros((TASKS, PADP), F32))
    square = total(task_grad * task_grad)
    lane = lax.broadcasted_iota(jnp.int32, (8, 128), 1)
    count = (limits[0] + limits[1]).astype(F32)
    stats = jnp.where(lane == 0, square, jnp.where(lane == 1, sums[0], jnp.where(lane == 2, sums[1], jnp.where(
        lane == 3, sums[2], jnp.where(lane == 4, count, 0.0)))))
    STSUM[...] = stats
    SREC[pl.ds(device, 1)] = stats[None]

    def to_all(d, _):
        swap(d, lambda k, mine: STSUM if mine else SREC.at[k], 1)
        return 0

    lax.fori_loop(0, NDEV, to_all, 0)
    out_task[...] = task_grad[:, 0:PART]
    others2 = SREC.at[pl.ds(0, NDEV - 1)]
    pltpu.make_async_copy(others2, others2, all_sem.at[3]).wait()
    out_stats[...] = jnp.sum(SREC[...], axis=0)
    pltpu.make_async_copy(others, others, all_sem.at[0]).wait()
    pltpu.make_async_copy(others2, others2, all_sem.at[2]).wait()
    net.finish()


def update_kernel(
    task_grad, stats, master, first_moment, second_moment, block_in, patch_in,
    out_grad, out_first, out_second, out_master, out_copy, out_small, block_out, patch_out,
):
    block_out[...] = block_in[...]
    patch_out[...] = patch_in[...]
    st = stats[0:1, :]
    square = st[0:1, 0:1]
    norm = jnp.sqrt(square)
    grad = task_grad[...] * (clip_level / jnp.maximum(norm, clip_level))
    first = beta_one * first_moment[...] + (1.0 - beta_one) * grad
    second = beta_two * second_moment[...] + (1.0 - beta_two) * grad * grad
    step_size = (
        first / (1.0 - beta_one**STEP) / (jnp.sqrt(second / (1.0 - beta_two**STEP)) + adam_eps)
    )
    old = master[...]
    new = old - learn_rate * (step_size + decay_rate * old)
    out_grad[...] = grad
    out_first[...] = first
    out_second[...] = second
    out_master[...] = new
    out_copy[...] = new.astype(BF16)
    lane = lax.broadcasted_iota(jnp.int32, (1, 128), 1)
    inside = jnp.where(lane == 0, square, st / (st[0:1, 4:5] * D))
    out_small[...] = jnp.sqrt(inside)


def fast_body(
    patches, lengths, tasks, prompt_master, first_moment, second_moment,
    gain_one, gain_two, w_qkv, w_out, w_up, w_down, cotangent,
):
    heads = w_qkv.reshape(96, 3, 3, HEAD_DIM)
    outs = w_out.T.reshape(96, 3, HEAD_DIM)
    order = [heads[:, 0, 0], heads[:, 0, 1], heads[:, 1, 0], heads[:, 1, 1], heads[:, 2, 0], heads[:, 2, 1],
             heads[:, 0, 2], heads[:, 2, 2], heads[:, 1, 2], outs[:, 2], outs[:, 0], outs[:, 1]]
    a_in = jnp.concatenate(order, axis=1)
    d_in = w_down.T
    vmem = pl.BlockSpec(memory_space=pltpu.VMEM)
    smem = pl.BlockSpec(memory_space=pltpu.SMEM)
    anywhere = pl.BlockSpec(memory_space=pl.ANY)
    V = pltpu.VMEM
    block, patch, task, stats = pl.pallas_call(
        layer_kernel,
        out_shape=[
            jax.ShapeDtypeStruct((IMGS, ROWS, D), BF16),
            jax.ShapeDtypeStruct((IMGS, PATCH, D), BF16),
            jax.ShapeDtypeStruct((TASKS, PART), F32),
            jax.ShapeDtypeStruct((8, 128), F32),
        ],
        in_specs=[vmem, smem, smem, vmem, vmem, vmem, vmem, vmem, vmem, anywhere],
        out_specs=[vmem] * 4,
        scratch_shapes=[
            V((1, 2, 8, 16, PADP), BF16),
            V((1, 2, 8, 96, 2 * D), BF16),
            V((CHUNKS, 2, 2, 8, 96, 2 * CHUNK), BF16),
            V((TASKS, PADP), F32),
            V((16, 4, PADP), F32),
            V((IMGS, ROWS, D), F32),
            V((IMGS, ROWS, D), BF16),
            V((4, IMGS, ROWS, 640), BF16),
            V((8, 3, ROWS, ROWS), BF16),
            V((IMGS, ROWS, 1024), BF16),
            V((IMGS, ROWS, D), F32),
            V((IMGS, ROWS, D), BF16),
            V((IMGS, ROWS, D), BF16),
            V((IMGS * ROWS, 2 * CHUNK), BF16),
            V((IMGS * ROWS, 2 * CHUNK), BF16),
            V((IMGS, ROWS, D), F32),
            V((IMGS, ROWS, D), F32),
            V((IMGS, ROWS, D), BF16),
            V((4, IMGS, ROWS, 640), BF16),
            V((25, 4, D), F32),
            V((NDEV, IMGS, PADP), F32),
            V((NDEV, IMGS, PADP), F32),
            V((NDEV, IMGS, TASKS, 128), F32),
            V((NDEV, 8, 128), F32),
            V((8, 128), F32),
            pltpu.SemaphoreType.DMA((8,)),
            pltpu.SemaphoreType.DMA((RING,)),
            pltpu.SemaphoreType.DMA((21 * (2 + CHUNKS),)),
            pltpu.SemaphoreType.DMA((4,)),
        ],
        compiler_params=pltpu.CompilerParams(
            collective_id=0, has_side_effects=True, vmem_limit_bytes=58 << 20
        ),
    )(patches, lengths, tasks, prompt_master, gain_one[None, :], gain_two[None, :], a_in, w_up, d_in, cotangent)
    grad, first, second, master, copy, small, block_out, patch_out = pl.pallas_call(
        update_kernel,
        out_shape=[jax.ShapeDtypeStruct((TASKS, PART), F32)] * 4
        + [
            jax.ShapeDtypeStruct((TASKS, PART), BF16),
            jax.ShapeDtypeStruct((1, 128), F32),
            jax.ShapeDtypeStruct((IMGS, ROWS, D), BF16),
            jax.ShapeDtypeStruct((IMGS, PATCH, D), BF16),
        ],
        in_specs=[vmem] * 7,
        out_specs=[vmem] * 8,
    )(task, stats, prompt_master, first_moment, second_moment, block, patch)
    return block_out, patch_out, grad, small[0, 0], first, second, master, copy, small[0, 1:4]


def layer_norm(values, gain):
    centre = jnp.mean(values, axis=-1, keepdims=True)
    shifted = values - centre
    spread = jnp.mean(shifted * shifted, axis=-1, keepdims=True)
    return shifted * lax.rsqrt(spread + eps_norm) * gain


def whole_norm_back(values, gain, upstream):
    centre = jnp.mean(values, axis=-1, keepdims=True)
    shifted = values - centre
    spread = jnp.mean(shifted * shifted, axis=-1, keepdims=True)
    scaled = lax.rsqrt(spread + eps_norm)
    normal_part = shifted * scaled
    weighted = upstream * gain
    return scaled * (
        weighted
        - jnp.mean(weighted, axis=-1, keepdims=True)
        - normal_part * jnp.mean(weighted * normal_part, axis=-1, keepdims=True)
    )


def gelu_slope(upward):
    cumul = 0.5 * (1.0 + lax.erf(upward * 0.7071067811865476))
    density = jnp.exp(-0.5 * upward * upward) * 0.3989422804014327
    return cumul + upward * density


def attend_forward(group_normed, group_limit, w_mix, block_images):
    group_size, row_count, feature_count = group_normed.shape
    lane_width = w_mix.shape[2]
    head_count = lane_width // HEAD_DIM
    scale = 1.0 / math.sqrt(HEAD_DIM)
    mask_all = jnp.arange(row_count, dtype=jnp.int32)[None, :] < group_limit[:, None]

    def one_block(block_index):
        first_row = block_index * block_images
        block_in = lax.dynamic_slice_in_dim(group_normed, first_row, block_images, 0)
        key_mask = lax.dynamic_slice_in_dim(mask_all, first_row, block_images, 0)
        mixed_qkv = jnp.einsum(
            "brd,dce->brce", block_in, w_mix, preferred_element_type=jnp.float32
        ).astype(jnp.bfloat16)
        split_heads = mixed_qkv.reshape(block_images, row_count, 3, head_count, HEAD_DIM)
        scores = (
            jnp.einsum(
                "bqhe,bkhe->bhqk",
                split_heads[:, :, 0],
                split_heads[:, :, 1],
                preferred_element_type=jnp.float32,
            )
            * scale
        )
        scores = jnp.where(key_mask[:, None, None, :], scores, -1e30)
        row_top = jnp.max(scores, axis=-1, keepdims=True)
        exponent = jnp.exp(scores - row_top)
        row_total = jnp.sum(exponent, axis=-1, keepdims=True)
        attend_weights = (exponent / row_total).astype(jnp.bfloat16)
        context = jnp.einsum(
            "bhqk,bkhe->bqhe",
            attend_weights,
            split_heads[:, :, 2],
            preferred_element_type=jnp.float32,
        )
        context = context.astype(jnp.bfloat16).reshape(block_images, row_count, lane_width)
        return (mixed_qkv, context, (row_top + jnp.log(row_total))[..., 0])

    mixed_qkv, context, logsums = lax.map(
        one_block, jnp.arange(group_size // block_images, dtype=jnp.int32)
    )
    return (
        mixed_qkv.reshape(group_size, row_count, 3, lane_width),
        context.reshape(group_size, row_count, lane_width),
        logsums.reshape(group_size, head_count, row_count),
    )


def attend_back(mixed_qkv, logsums, group_limit, grad_context, block_images):
    group_size, row_count, three_parts, lane_width = mixed_qkv.shape
    head_count = lane_width // HEAD_DIM
    scale = 1.0 / math.sqrt(HEAD_DIM)
    mask_all = jnp.arange(row_count, dtype=jnp.int32)[None, :] < group_limit[:, None]

    def one_block(block_index):
        first_row = block_index * block_images
        split_heads = lax.dynamic_slice_in_dim(mixed_qkv, first_row, block_images, 0).reshape(
            block_images, row_count, 3, head_count, HEAD_DIM
        )
        queries = split_heads[:, :, 0]
        keys_all = split_heads[:, :, 1]
        values = split_heads[:, :, 2]
        key_mask = lax.dynamic_slice_in_dim(mask_all, first_row, block_images, 0)
        logsum = lax.dynamic_slice_in_dim(logsums, first_row, block_images, 0)
        grad_out = lax.dynamic_slice_in_dim(grad_context, first_row, block_images, 0).reshape(
            block_images, row_count, head_count, HEAD_DIM
        )
        scores = (
            jnp.einsum("bqhe,bkhe->bhqk", queries, keys_all, preferred_element_type=jnp.float32)
            * scale
        )
        scores = jnp.where(key_mask[:, None, None, :], scores, -1e30)
        attend_weights = jnp.exp(scores - logsum[..., None])
        grad_weights = jnp.einsum(
            "bqhe,bkhe->bhqk", grad_out, values, preferred_element_type=jnp.float32
        )
        row_inner = jnp.sum(attend_weights * grad_weights, axis=-1, keepdims=True)
        grad_scores = (attend_weights * (grad_weights - row_inner)).astype(jnp.bfloat16)
        grad_query = (
            jnp.einsum("bhqk,bkhe->bqhe", grad_scores, keys_all, preferred_element_type=jnp.float32)
            * scale
        )
        grad_key = (
            jnp.einsum("bhqk,bqhe->bkhe", grad_scores, queries, preferred_element_type=jnp.float32)
            * scale
        )
        grad_value = jnp.einsum(
            "bhqk,bqhe->bkhe",
            attend_weights.astype(jnp.bfloat16),
            grad_out,
            preferred_element_type=jnp.float32,
        )
        stacked = jnp.stack([grad_query, grad_key, grad_value], axis=2).astype(jnp.bfloat16)
        return stacked.reshape(block_images, row_count, 3, lane_width)

    grad_mixed = lax.map(one_block, jnp.arange(group_size // block_images, dtype=jnp.int32))
    return grad_mixed.reshape(group_size, row_count, 3, lane_width)


def expand_units(group_two, w_expand, block_images):
    group_size, row_count, feature_count = group_two.shape

    def one_block(block_index):
        block_in = lax.dynamic_slice_in_dim(group_two, block_index * block_images, block_images, 0)
        upward = jnp.einsum("brd,df->brf", block_in, w_expand, preferred_element_type=jnp.float32)
        return jax.nn.gelu(upward, approximate=False).astype(jnp.bfloat16)

    act_units = lax.map(one_block, jnp.arange(group_size // block_images, dtype=jnp.int32))
    return act_units.reshape(group_size, row_count, w_expand.shape[1])


def units_back(grad_group, group_two, w_expand, w_reduce, block_images):
    group_size, row_count, feature_count = group_two.shape

    def one_block(block_index):
        first_row = block_index * block_images
        grad_in = lax.dynamic_slice_in_dim(grad_group, first_row, block_images, 0)
        norm_in = lax.dynamic_slice_in_dim(group_two, first_row, block_images, 0)
        back_units = jnp.einsum(
            "brd,fd->brf", grad_in, w_reduce, preferred_element_type=jnp.float32
        )
        upward = jnp.einsum("brd,df->brf", norm_in, w_expand, preferred_element_type=jnp.float32)
        return (back_units * gelu_slope(upward)).astype(jnp.bfloat16)

    grad_units = lax.map(one_block, jnp.arange(group_size // block_images, dtype=jnp.int32))
    return grad_units.reshape(group_size, row_count, w_expand.shape[1])


def rows_term(source, weight, form):
    return jnp.einsum(form, source, weight, preferred_element_type=jnp.float32)


def body(
    patches,
    lengths,
    tasks,
    prompt_master,
    first_moment,
    second_moment,
    gain_one,
    gain_two,
    w_qkv,
    w_out,
    w_up,
    w_down,
    cotangent,
):
    held_count, patch_count, feature_count = patches.shape
    row_count = cotangent.shape[1]
    lead_count = row_count - patch_count
    task_count = prompt_master.shape[0]
    prompt_table = lax.all_gather(
        prompt_master.astype(jnp.bfloat16), ("dp", "mp"), axis=1, tiled=True
    )
    chosen = tasks == jnp.arange(task_count, dtype=jnp.int32)[None, :]
    lead_part = jnp.dot(
        chosen.astype(jnp.bfloat16), prompt_table, preferred_element_type=jnp.float32
    )
    residual = jnp.concatenate(
        [lead_part.reshape(held_count, lead_count, feature_count), patches.astype(jnp.float32)],
        axis=1,
    )
    row_limit = lengths + lead_count
    w_mix, w_expand, w_reduce, w_rows = (
        lax.all_gather(w_qkv, "dp", axis=0, tiled=True),
        lax.all_gather(w_up, "dp", axis=0, tiled=True),
        lax.all_gather(w_down, "dp", axis=1, tiled=True),
        lax.all_gather(w_out, "dp", axis=1, tiled=True),
    )
    normed = layer_norm(residual, gain_one).astype(jnp.bfloat16)
    mp_rank = lax.axis_index("mp")
    group_normed, group_bound = (
        lax.all_gather(normed, "mp", axis=0, tiled=True),
        lax.all_gather(row_limit.astype(jnp.bfloat16), "mp", axis=0, tiled=True),
    )
    group_limit = group_bound.astype(jnp.int32)
    mixed_qkv, context, logsums = attend_forward(group_normed, group_limit, w_mix, held_count)
    attn_out = lax.psum_scatter(
        rows_term(context, w_rows, "brc,cd->brd"), "mp", scatter_dimension=0, tiled=True
    )
    residual_two = residual + attn_out
    normed_two = layer_norm(residual_two, gain_two).astype(jnp.bfloat16)
    group_two = lax.all_gather(normed_two, "mp", axis=0, tiled=True)
    act_units = expand_units(group_two, w_expand, held_count)
    mlp_out = lax.psum_scatter(
        rows_term(act_units, w_reduce, "brf,fd->brd").astype(jnp.bfloat16),
        "mp",
        scatter_dimension=0,
        tiled=True,
    ).astype(jnp.float32)
    block_sum = residual_two + mlp_out
    live_rows = (jnp.arange(row_count, dtype=jnp.int32)[None, :] < row_limit[:, None]).astype(
        jnp.float32
    )[:, :, None]
    square_sums = jnp.stack(
        [
            jnp.sum(block_sum * block_sum * live_rows),
            jnp.sum(attn_out * attn_out * live_rows),
            jnp.sum(mlp_out * mlp_out * live_rows),
        ]
    )
    live_count = jnp.sum(row_limit).astype(jnp.float32)
    w_mix, w_expand, w_reduce, w_rows = (
        lax.all_gather(w_qkv, "dp", axis=0, tiled=True),
        lax.all_gather(w_up, "dp", axis=0, tiled=True),
        lax.all_gather(w_down, "dp", axis=1, tiled=True),
        lax.all_gather(w_out, "dp", axis=1, tiled=True),
    )
    grad_held = lax.dynamic_slice_in_dim(cotangent, mp_rank * held_count, held_count, 0)
    grad_units = units_back(cotangent, group_two, w_expand, w_reduce, held_count)
    grad_normed_two = lax.psum_scatter(
        rows_term(grad_units, w_expand, "brf,df->brd"), "mp", scatter_dimension=0, tiled=True
    )
    grad_two = grad_held.astype(jnp.float32) + whole_norm_back(residual_two, gain_two, grad_normed_two)
    grad_low = grad_two.astype(jnp.bfloat16)
    grad_context = jnp.einsum(
        "brd,cd->brc",
        lax.all_gather(grad_low, "mp", axis=0, tiled=True),
        w_rows,
        preferred_element_type=jnp.float32,
    ).astype(jnp.bfloat16)
    grad_mixed = attend_back(mixed_qkv, logsums, group_limit, grad_context, held_count)
    grad_normed = lax.psum_scatter(
        rows_term(grad_mixed, w_mix, "brce,dce->brd").astype(jnp.bfloat16),
        "mp",
        scatter_dimension=0,
        tiled=True,
    ).astype(jnp.float32)
    grad_residual = grad_two + whole_norm_back(residual, gain_one, grad_normed)
    patch_grad = grad_residual[:, lead_count:].astype(jnp.bfloat16)
    lead_grad = grad_residual[:, :lead_count].reshape(held_count, lead_count * feature_count)
    task_term = jnp.dot(
        chosen.astype(jnp.float32).T,
        lead_grad,
        precision=lax.Precision.HIGHEST,
        preferred_element_type=jnp.float32,
    )
    task_grad = lax.psum_scatter(task_term, ("dp", "mp"), scatter_dimension=1, tiled=True)
    square = jnp.sum(task_grad * task_grad)
    square, square_sums, live_count = lax.psum((square, square_sums, live_count), ("dp", "mp"))
    grad_norm = jnp.sqrt(square)
    prompt_grad = task_grad * (clip_level / jnp.maximum(grad_norm, clip_level))
    new_first = beta_one * first_moment + (1.0 - beta_one) * prompt_grad
    new_second = beta_two * second_moment + (1.0 - beta_two) * prompt_grad * prompt_grad
    step_size = (
        new_first
        / (1.0 - beta_one**STEP)
        / (jnp.sqrt(new_second / (1.0 - beta_two**STEP)) + adam_eps)
    )
    new_master = prompt_master - learn_rate * (step_size + decay_rate * prompt_master)
    rms_stats = jnp.sqrt(square_sums / (live_count * feature_count))
    return (
        block_sum.astype(jnp.bfloat16),
        patch_grad,
        prompt_grad,
        grad_norm,
        new_first,
        new_second,
        new_master,
        new_master.astype(jnp.bfloat16),
        rms_stats,
    )


def solution(mesh):
    small = mesh.shape["dp"] == 8 and mesh.shape["mp"] == 4
    return jax.shard_map(
        fast_body if small else body,
        mesh=mesh,
        in_specs=(
            P(("dp", "mp"), None, None),
            P(("dp", "mp")),
            P(("dp", "mp"), None),
            P(None, ("dp", "mp")),
            P(None, ("dp", "mp")),
            P(None, ("dp", "mp")),
            P(),
            P(),
            P("dp", None, "mp"),
            P("mp", "dp"),
            P("dp", "mp"),
            P("mp", "dp"),
            P("dp", None, None),
        ),
        out_specs=(
            P(("dp", "mp"), None, None),
            P(("dp", "mp"), None, None),
            P(None, ("dp", "mp")),
            P(),
            P(None, ("dp", "mp")),
            P(None, ("dp", "mp")),
            P(None, ("dp", "mp")),
            P(None, ("dp", "mp")),
            P(),
        ),
        check_vma=False,
    )
```

```python
import functools
import math

import jax
import jax.numpy as jnp
from jax import lax
from jax.experimental import pallas as pl
from jax.experimental.pallas import tpu as pltpu
from jax.sharding import PartitionSpec as P

HEAD_DIM = 64
STEP = 10
MESH = pl.DeviceIdType.MESH
F32 = jnp.float32
BF16 = jnp.bfloat16

eps_norm = 1e-06
clip_level = 1.0
beta_one = 0.9
beta_two = 0.999
learn_rate = 3.0
decay_rate = 0.05
adam_eps = 1e-08

D = 768
ROWS = 256
LEAD = 50
PATCH = 206
IMGS = 2
TASKS = 8
PART = 1200
PADP = 1280
NDEV = 32
CHUNKS = (256, 256, 256)
ORDER = (
    (0, 28, 112, 84, 56, 4, 32, 37, 44,),
    (13, 17, 16, 60, 72, 14, 18, 48, 41, 38, 65, 20, 45, 22, 15, 21, 93, 19, 42, 46, 52, 39, 23, 69, 26, 25, 66, 73, 27, 24,),
    (49, 88,),
    (43, 47, 67, 94, 70, 121, 53, 50, 100, 74, 51, 95, 54, 97, 101, 116, 55,),
    (71, 128, 76, 75,),
    (77, 98, 122, 104,),
    (102,),
    (125, 129, 105, 108,),
    (78, 80, 79, 132,),
    (123,),
    (81, 99, 103, 83,),
    (126, 130, 109, 82, 136, 106,),
    (127, 131, 107,),
    (110, 133, 111, 134,),
    (137, 135,),
    (138, 139,),
    (),
    (),
)
RING = 24
ATT = 4


def run_if(cond, f):
    if cond is None:
        f()
    else:
        pl.when(cond())(f)


def both(*conds):
    conds = [c for c in conds if c is not None]
    if not conds:
        return None

    def value():
        out = conds[0]()
        for c in conds[1:]:
            out = jnp.logical_and(out, c())
        return out

    return value


class Net:
    def __init__(self, send_sem, recv_sem):
        self.send_sem, self.recv_sem = send_sem, recv_sem
        self.sent = self.used = 0
        dp, mp = lax.axis_index("dp"), lax.axis_index("mp")
        z, x, y, c = dp // 2, dp % 2, mp // 2, mp % 2
        self.z, self.x, self.y, self.c = z, x, y, c
        self.dp, self.mp = dp, mp
        self.peer = {
            "x": (2 * z + 1 - x, mp),
            "y": (dp, (1 - y) * 2 + c),
            "c": (dp, 2 * y + 1 - c),
            "u": (jnp.minimum(2 * z + 2 + x, 6 + x), mp),
            "d": (jnp.maximum(2 * z - 2 + x, x), mp),
        }
        self.ring = [None] * RING

    def alloc(self, n):
        first = self.used
        self.used += n
        return first

    def send(self, way, view, sem, cond=None):
        i = self.sent % RING
        self.sent += 1
        if self.ring[i] is not None:
            self.wait_sent(i)

        def copy():
            v = view()
            return pltpu.make_async_remote_copy(
                src_ref=v,
                dst_ref=v,
                send_sem=self.send_sem.at[i],
                recv_sem=self.recv_sem.at[sem()],
                device_id=self.peer[way],
                device_id_type=MESH,
            )

        run_if(cond, lambda: copy().start())
        self.ring[i] = (cond, copy)

    def wait_sent(self, i):
        cond, copy = self.ring[i]
        run_if(cond, lambda: copy().wait_send())
        self.ring[i] = None

    def recv(self, view, sem, cond=None):
        def wait():
            v = view()
            pltpu.make_async_copy(v, v, self.recv_sem.at[sem()]).wait()

        run_if(cond, wait)

    def finish(self):
        for i in range(RING):
            if self.ring[i] is not None:
                self.wait_sent(i)


def gather_events(net, G, W, split):
    z, x, y, c = net.z, net.x, net.y, net.c
    r1, r2, r3, rows = split
    some = 4 if r3 > r1 else 0
    f_sem, zs_sem, zp_sem, m_sem, l_sem, c_sem = (net.alloc(n) for n in (1, some, 4, some, 4, 4))
    not_top, not_low = (lambda: z < 3), (lambda: z > 0)
    every = slice(None)

    def V(yy, d, first, last, other=False):
        def view():
            core = (1 - c) if other else c
            cols = pl.ds(pl.multiple_of(core * W, 128), W)
            return G.at[:, yy, d() if callable(d) else d, pl.ds(first, last - first), cols]

        return view

    def two(p):
        return lambda: pl.ds(2 * p(), 2)

    def one(p):
        return lambda: 2 * p() + x

    def at(sem, p):
        return lambda: sem + p()

    own = lambda: z

    def send(way, yy, d, first, last, sem, cond=None):
        if last > first:
            net.send(way, V(yy, d, first, last), sem, cond)

    def planes(k):
        if k == 0:
            return [(own, None)]
        return [(lambda: z - k, lambda: z >= k), (lambda: z + k, lambda: z + k <= 3)]

    def middle(p, cond):
        send("x", y, one(p), r1, r2, at(m_sem, p), cond)
        send("y", y, one(p), r2, r3, at(m_sem, p), cond)

    def start():
        send("x", y, one(own), 0, r1, lambda: f_sem)
        send("y", y, one(own), r3, rows, lambda: f_sem)
        send("u", y, one(own), r1, r3, at(zs_sem, own), not_top)
        send("d", y, one(own), r1, r3, at(zs_sem, own), not_low)
        middle(own, None)

    def pair(way, p, cond):
        send(way, y, two(p), 0, r1, at(zp_sem, p), cond)
        send(way, every, one(p), r3, rows, at(zp_sem, p), cond)

    def first_hop():
        net.recv(V(y, one(own), 0, r1 + rows - r3), lambda: f_sem)
        pair("u", own, not_top)
        pair("d", own, not_low)

    def ways(k):
        return [(p, cond, w, far) for (p, cond), w, far in zip(planes(k), "ud", (not_top, not_low))]

    def single_hop(k):
        for p, cond, way, far in ways(k):
            net.recv(V(y, one(p), r1, r3), at(zs_sem, p), cond)
            if k < 3:
                send(way, y, one(p), r1, r3, at(zs_sem, p), both(cond, far))
            middle(p, cond)

    def pair_hop(k):
        for p, cond, way, far in ways(k):
            net.recv(V(y, two(p), 0, r1 + rows - r3), at(zp_sem, p), cond)
            if k < 3:
                pair(way, p, both(cond, far))

    def last_hop(k):
        for p, cond in planes(k):
            if r3 > r1:
                net.recv(V(y, one(p), r1, r3), at(m_sem, p), cond)
            send("y", y, two(p), 0, r2, at(l_sem, p), cond)
            send("x", every, one(p), r2, rows, at(l_sem, p), cond)

    def to_core(k):
        for p, cond in planes(k):
            net.recv(V(y, two(p), 0, rows), at(l_sem, p), cond)
            send("c", every, two(p), 0, rows, at(c_sem, p), cond)

    def from_core(k):
        for p, cond in planes(k):
            net.recv(V(every, two(p), 0, rows, other=True), at(c_sem, p), cond)

    kinds = (start, first_hop, single_hop, pair_hop, last_hop, to_core, from_core)
    return [f if i < 2 else functools.partial(f, k) for i, f in enumerate(kinds) for k in range(4)]


def at_step(t, groups):
    for j, group in enumerate(groups):
        if group:

            def go(group=group):
                for f in group:
                    f()

            pl.when(t == j)(go)


def nn(a, b):
    return lax.dot_general(a, b, (((1,), (0,)), ((), ())), preferred_element_type=F32)


def nt(a, b):
    return lax.dot_general(a, b, (((1,), (1,)), ((), ())), preferred_element_type=F32)


def tn(a, b):
    return lax.dot_general(a, b, (((0,), (0,)), ((), ())), preferred_element_type=F32)


def norm_parts(v):
    centre = jnp.mean(v, axis=-1, keepdims=True)
    shifted = v - centre
    spread = jnp.mean(shifted * shifted, axis=-1, keepdims=True)
    scaled = lax.rsqrt(spread + eps_norm)
    return shifted * scaled, scaled


def norm_back(v, gain, upstream):
    normal, scaled = norm_parts(v)
    weighted = upstream * gain
    return scaled * (
        weighted
        - jnp.mean(weighted, axis=-1, keepdims=True)
        - normal * jnp.mean(weighted * normal, axis=-1, keepdims=True)
    )


def keep(lanes, low, high):
    return jnp.where(lanes, low, high)


def layer_kernel(
    patches, lengths, tasks, master, gain_one, gain_two, qkv_in, out_in, u_in, d_in, cot_hbm,
    out_block, out_patch, out_task, out_stats,
    GP, GA, GM0, GM1, GM2, LOC, SEL, RES, N1, QKV, PT, CTX, RES2, N2, COT, ACT, GU, MACC, GACC, G2, G2B, DM, DC, LEADR,
    PAIR, PIN, BOUT, SEND, RECV, ONEHOT, SREC, STSUM, local_sem, send_sem, recv_sem, all_sem,
):
    net = Net(send_sem, recv_sem)
    z, x, y, c, dp, mp = net.z, net.x, net.y, net.c, net.dp, net.mp
    device = dp * 4 + mp
    GMS = (GM0, GM1, GM2)

    barrier = pltpu.get_barrier_semaphore()
    for way, cond in (("x", None), ("y", None), ("c", None), ("u", lambda: z < 3), ("d", lambda: z > 0)):
        run_if(
            cond,
            lambda way=way: pl.semaphore_signal(
                barrier, inc=1, device_id=net.peer[way], device_id_type=MESH
            ),
        )

    def own_cols(w):
        return pl.ds(pl.multiple_of(c * w, 128), w)

    cot_copy = pltpu.make_async_copy(cot_hbm.at[pl.ds(mp * IMGS, IMGS)], COT, local_sem.at[0])
    copies = []
    first = 0
    for i, (GM, w) in enumerate(zip(GMS, CHUNKS)):
        for j, weight_in in enumerate((u_in, d_in)):
            copies.append(
                pltpu.make_async_copy(
                    weight_in.at[:, pl.ds(first, w)],
                    GM.at[j, y, dp, :, own_cols(w)],
                    local_sem.at[1 + 2 * i + j],
                )
            )
        first += w
    for copy in copies:
        copy.start()
    patch_copy = pltpu.make_async_copy(patches, PIN, local_sem.at[7])
    patch_copy.start()
    cot_copy.start()

    qkv = [qkv_in[i].astype(F32) for i in range(3)]
    outs = out_in[...].astype(F32).T
    low = lax.broadcasted_iota(jnp.int32, (96, 128), 1) < HEAD_DIM

    def tail(v, high):
        v = jnp.concatenate([v[:, 128:192], v[:, 128:192]], axis=1)
        return v

    tiles = [qkv[0][:, 0:128], qkv[1][:, 0:128], qkv[2][:, 0:128]]
    tiles.append(jnp.where(low, tail(qkv[0], 0), tail(qkv[2], 1)))
    tiles.append(jnp.where(low, tail(qkv[1], 0), tail(outs, 1)))
    tiles.append(outs[:, 0:128])
    GA[0, pl.ds(y, 1), pl.ds(dp, 1), :, own_cols(D)] = (
        jnp.concatenate(tiles, axis=1).astype(BF16)[None, None]
    )

    LOC[:, 0:PART] = master[...]
    lane = lax.broadcasted_iota(jnp.int32, (TASKS, PADP - PART), 1)
    LOC[:, PART:PADP] = jnp.where(
        lane == 0, tasks[0, 0].astype(F32), jnp.where(lane == 1, tasks[0, 1].astype(F32), 0.0)
    )
    half = PADP // 2
    GP[0, pl.ds(y, 1), pl.ds(dp, 1), :, own_cols(half)] = (
        jnp.concatenate([LOC[:, 0:half], LOC[:, half:PADP]], axis=0).astype(BF16)[None, None]
    )
    for copy in copies:
        copy.wait()
    inner = jnp.logical_and(z > 0, z < 3)
    run_if(lambda: inner, lambda: pl.semaphore_wait(barrier, 5))
    run_if(lambda: jnp.logical_not(inner), lambda: pl.semaphore_wait(barrier, 4))

    split = (32, 48, 64, 96)
    gathers = [gather_events(net, GP, half, (16, 16, 16, 16)), gather_events(net, GA, D, split)]
    gathers += [gather_events(net, GM, w, split) for GM, w in zip(GMS, CHUNKS)]
    segments = [[gathers[i // 28][i % 28] for i in part] for part in ORDER]
    position = [0]

    def ahead(n=1):
        position[0] += n
        return segments[position[0] - n : position[0]]

    def advance():
        for f in ahead()[0]:
            f()

    g1 = gain_one[...].reshape(1, D)
    g2 = gain_two[...].reshape(1, D)
    limits = [lengths[b] + LEAD for b in range(IMGS)]
    live = [
        (lax.broadcasted_iota(jnp.int32, (ROWS, 1), 0) < limits[b]).astype(F32) for b in range(IMGS)
    ]

    advance()
    patch_copy.wait()
    for b in range(IMGS):
        RES[b, LEAD:ROWS, :] = PIN[:, b, :].astype(F32)
    MACC[...] = jnp.zeros_like(MACC)
    GACC[...] = jnp.zeros_like(GACC)
    advance()

    task_rows = lax.broadcasted_iota(jnp.int32, (TASKS, 1), 0)

    def pick(d, _):
        dd, mm = d // 4, d % 4
        raw = GP[0, mm // 2, dd, :, pl.ds(pl.multiple_of((mm % 2) * half, 128), half)].astype(F32)
        low, high = raw[0:8], raw[8:16]
        rep, j = d // 16, d % 16
        for b in range(IMGS):
            hot = (task_rows == tasks[0, b]).astype(F32)
            row = 2 * rep + b
            SEL[j, pl.ds(row, 1), 0:half] = jnp.sum(low * hot, axis=0, keepdims=True)
            SEL[j, pl.ds(row, 1), half:PADP] = jnp.sum(high * hot, axis=0, keepdims=True)
        base = PART - half
        for b in range(IMGS):
            which = high[0:1, base + b : base + b + 1]
            ONEHOT[d, b] = (
                lax.broadcasted_iota(jnp.int32, (TASKS, 128), 0).astype(F32) == which
            ).astype(F32)
        return 0

    lax.fori_loop(0, NDEV, pick, 0)
    wide = lax.broadcasted_iota(jnp.int32, (4, D), 1)
    for r in range(25):
        j, off = (D * r) // PART, (D * r) % PART
        first = min(D, PART - off)
        low = SEL[j, 0:4, :]
        seg = (pltpu.roll(low, PADP - off, 1) if off else low)[:, 0:D]
        if first < D:
            seg = jnp.where(wide < first, seg, pltpu.roll(SEL[j + 1, 0:4, :], first, 1)[:, 0:D])
        for rep in range(2):
            for b in range(IMGS):
                RES[b, 25 * rep + r : 25 * rep + r + 1, :] = seg[2 * rep + b : 2 * rep + b + 1]

    advance()
    for b in range(IMGS):
        N1[b] = (norm_parts(RES[b])[0] * g1).astype(BF16)

    def weight(ref, core, first, width, span):
        cols = pl.ds(pl.multiple_of(core * span + first, 128), width)
        return ref[:, :, cols].reshape(D, width)

    left = lax.broadcasted_iota(jnp.int32, (ROWS, 128), 1) < HEAD_DIM
    scale = 1.0 / math.sqrt(HEAD_DIM)
    wide = lax.broadcasted_iota(jnp.int32, (1, 640), 1)
    q_scale = jnp.where((wide < 128) | ((wide >= 384) & (wide < 448)), scale, 1.0)

    groups = ahead(2)

    def project(t, _):
        at_step(t, groups)
        for core in range(2):
            w = weight(GA.at[0, t], core, 0, 640, D)
            mixed = nn(N1[...].reshape(IMGS * ROWS, D), w) * q_scale
            QKV[2 * t + core] = mixed.astype(BF16).reshape(IMGS, ROWS, 640)
        return 0

    lax.fori_loop(0, 2, project, 0)

    key_rows = lax.broadcasted_iota(jnp.int32, (ROWS, ROWS), 0)
    zero = jnp.zeros((), BF16)
    groups_a = ahead(ATT)

    def attend(t):
        b, m = t // 4, t % 4
        tile = lambda i: QKV[m, b, :, 128 * i : 128 * i + 128]
        q01, k01, v01, q2v2, k2 = (tile(i) for i in range(5))
        mask = key_rows < (lengths[b] + LEAD)

        def soft(keys, queries):
            s = jnp.where(mask, nt(keys, queries), -1e30)
            e = jnp.exp(s - jnp.max(s, axis=0, keepdims=True))
            return (e * (1.0 / jnp.sum(e, axis=0, keepdims=True))).astype(BF16)

        p0 = soft(k01, keep(left, q01, zero))
        p1 = soft(k01, keep(left, zero, q01))
        p2 = soft(k2, keep(left, q2v2, zero))
        PT[t, 0], PT[t, 1], PT[t, 2] = p0, p1, p2
        CTX[b, :, pl.ds(pl.multiple_of(m * 256, 128), 128)] = keep(left, 0.0, tn(p2, q2v2)).astype(BF16)
        CTX[b, :, pl.ds(pl.multiple_of(m * 256 + 128, 128), 128)] = keep(
            left, tn(p0, v01), tn(p1, v01)
        ).astype(BF16)

    def attend_some(t, _):
        at_step(t, groups_a)
        for j in range(8 // ATT):
            attend(t * (8 // ATT) + j)
        return 0

    lax.fori_loop(0, ATT, attend_some, 0)

    sums = [jnp.zeros((1, 1), F32) for _ in range(3)]

    def total(v):
        return jnp.sum(jnp.sum(v, axis=0, keepdims=True), axis=1, keepdims=True)

    for b in range(IMGS):
        advance()
        attn = jnp.zeros((ROWS, D), F32)
        for m in range(4):
            attn += nt(CTX[b, :, 256 * m : 256 * m + 256], weight(GA.at[0, m // 2], m % 2, 512, 256, D))
        sums[1] += total(attn * attn * live[b])
        res2 = RES[b] + attn
        RES2[b] = res2
        N2[b] = (norm_parts(res2)[0] * g2).astype(BF16)
    cot_copy.wait()

    def feed(i, yy):
        GM, w = GMS[i], CHUNKS[i]
        rows2 = N2[...].reshape(IMGS * ROWS, D)
        cot = COT[...].reshape(IMGS * ROWS, D)
        for core in range(2):
            up = nn(rows2, weight(GM.at[0, yy], core, 0, w, w))
            back = nn(cot, weight(GM.at[1, yy], core, 0, w, w))
            cumul = 0.5 * (1.0 + lax.erf(up * 0.7071067811865476))
            density = jnp.exp(-0.5 * up * up) * 0.3989422804014327
            ACT[:, w * core : w * (core + 1)] = (up * cumul).astype(BF16)
            GU[:, w * core : w * (core + 1)] = (back * (cumul + up * density)).astype(BF16)
        MACC[...] += nt(ACT[:, 0 : 2 * w], weight(GM.at[1, yy], 0, 0, 2 * w, w)).reshape(IMGS, ROWS, D)
        GACC[...] += nt(GU[:, 0 : 2 * w], weight(GM.at[0, yy], 0, 0, 2 * w, w)).reshape(IMGS, ROWS, D)

    for i in range(len(CHUNKS)):
        groups_m = ahead(2)

        def step(t, _, i=i, groups_m=groups_m):
            at_step(t, groups_m)
            feed(i, t)
            return 0

        lax.fori_loop(0, 2, step, 0)
    advance()

    for b in range(IMGS):
        g = COT[b].astype(F32) + norm_back(RES2[b], g2, GACC[b])
        G2[b] = g
        G2B[b] = g.astype(BF16)

    def context_back(m, _):
        cols = pl.ds(pl.multiple_of((m % 2) * D + 512, 128), 256)
        w = GA[0, m // 2, :, :, cols].reshape(D, 256)
        DC[m] = nn(G2B[...].reshape(IMGS * ROWS, D), w).astype(BF16).reshape(IMGS, ROWS, 256)
        return 0

    lax.fori_loop(0, 4, context_back, 0, unroll=4)

    def attend_back(b):
        tiles, grad_probs, grad_scores = [], [], []
        for m in range(4):
            tiles.append(
                [QKV[m, b, :, 128 * i : 128 * i + 128] for i in range(5)]
                + [DC[m, b, :, 0:128], DC[m, b, :, 128:256]]
            )
            q01, k01, v01, q2v2, k2, c2, c01 = tiles[m]
            grad_probs.append(
                [nt(keep(left, v01, zero), c01), nt(keep(left, zero, v01), c01), nt(keep(left, zero, q2v2), c2)]
            )
        for m in range(4):
            out = []
            for h in range(3):
                pf, dp_ = PT[4 * b + m, h].astype(F32), grad_probs[m][h]
                inner = jnp.sum(pf * dp_, axis=0, keepdims=True)
                out.append((pf * (dp_ - inner)).astype(BF16))
            grad_scores.append(out)
        for m in range(4):
            q01, k01, v01, q2v2, k2, c2, c01 = tiles[m]
            s0, s1, s2 = grad_scores[m]
            p0, p1, p2 = (PT[4 * b + m, h] for h in range(3))
            DM[m, b, :, 0:128] = (keep(left, tn(s0, k01), tn(s1, k01)) * scale).astype(BF16)
            DM[m, b, :, 128:256] = keep(left, nn(s0, q01), nn(s1, q01)).astype(BF16)
            DM[m, b, :, 256:384] = keep(left, nn(p0, c01), nn(p1, c01)).astype(BF16)
            DM[m, b, :, 384:512] = keep(left, tn(s2, k2) * scale, nn(p2, c2)).astype(BF16)
            DM[m, b, :, 512:640] = keep(left, nn(s2, q2v2), 0.0).astype(BF16)

    def grad_rows(b, first, last):
        grad = jnp.zeros((last - first, D), F32)
        for m in range(4):
            grad += nt(DM[m, b, first:last], weight(GA.at[0, m // 2], m % 2, 0, 640, D))
        GACC[b, first:last] = G2[b, first:last] + norm_back(RES[b, first:last], g1, grad)

    def swap(k, src, dst, sems):
        other = lax.rem(device + k, NDEV)
        pltpu.make_async_remote_copy(
            src_ref=src(other),
            dst_ref=dst,
            send_sem=all_sem.at[sems],
            recv_sem=all_sem.at[sems + 1],
            device_id=(other // 4, lax.rem(other, 4)),
            device_id_type=MESH,
        ).start()

    wide = lax.broadcasted_iota(jnp.int32, (2, PADP), 1)

    def to_owners(b):
        for rep in range(2):
            LEADR[:, rep : rep + 1, :] = GACC[b, 25 * rep : 25 * rep + 25, :][:, None, :]
        for q in range(16):
            r, off = (PART * q) // D, (PART * q) % D
            msg, have = None, -off
            while have < PART:
                row = LEADR[r]
                moved = pltpu.roll(row, have % D, 1) if have % D else row
                moved = jnp.concatenate([moved, moved[:, 0 : PADP - D]], axis=1)
                msg = moved if msg is None else jnp.where(wide < have, msg, moved)
                have += D
                r += 1
            msg = jnp.where(wide < PART, msg, 0.0).astype(BF16)
            for rep in range(2):
                SEND[b, 16 * rep + q] = jnp.concatenate(
                    [msg[rep : rep + 1, 0:half], msg[rep : rep + 1, half:PADP]], axis=0
                )
        for k in range(1, NDEV):
            swap(k, lambda other: SEND.at[b, other], RECV.at[b, device], 2 * b)
        RECV[b, pl.ds(device, 1)] = SEND[b, pl.ds(device, 1)]

    def others(ref):
        return ref.at[pl.ds(0, NDEV - 1)]

    def wait_all(ref, sem):
        pltpu.make_async_copy(others(ref), others(ref), all_sem.at[sem]).wait()

    attend_back(0)
    grad_rows(0, 0, ROWS)
    to_owners(0)
    attend_back(1)
    some = 64
    grad_rows(1, 0, some)
    to_owners(1)

    grad_rows(1, some, ROWS)
    for b in range(IMGS):
        mlp = MACC[b]
        block = RES2[b] + mlp
        BOUT[b] = block.astype(BF16)
        sums[0] += total(block * block * live[b])
        sums[2] += total(mlp * mlp * live[b])
    block_copy = pltpu.make_async_copy(BOUT, out_block, local_sem.at[8])
    block_copy.start()

    def add_image(b, acc):
        wait_all(RECV.at[b], 2 * b + 1)

        def add(s, acc):
            rows = RECV[b, s].astype(F32)
            hot = jnp.concatenate([ONEHOT[s, b]] * (half // 128), axis=1)
            return acc[0] + hot * rows[0:1], acc[1] + hot * rows[1:2]

        return lax.fori_loop(0, NDEV, add, acc, unroll=8)

    acc = (jnp.zeros((TASKS, half), F32), jnp.zeros((TASKS, half), F32))
    acc = add_image(1, add_image(0, acc))
    square = total(acc[0] * acc[0]) + total(acc[1] * acc[1])
    lane = lax.broadcasted_iota(jnp.int32, (1, 128), 1)
    count = (limits[0] + limits[1]).astype(F32)
    stats = jnp.zeros((1, 128), F32)
    for i, v in enumerate((square, sums[0], sums[1], sums[2], count)):
        stats = jnp.where(lane == i, v, stats)
    STSUM[...] = stats
    SREC[pl.ds(device, 1)] = stats[None]
    for k in range(1, NDEV):
        swap(k, lambda other: STSUM, SREC.at[device], 4)

    out_task[...] = jnp.concatenate(acc, axis=1)[:, 0:PART]
    for b in range(IMGS):
        PAIR[:, b : b + 1, :] = GACC[b, LEAD:ROWS, :][:, None, :]
    PIN[...] = PAIR[...].astype(BF16)
    patch_out = pltpu.make_async_copy(PIN, out_patch, local_sem.at[9])
    patch_out.start()
    for b in range(IMGS):
        wait_all(RECV.at[b], 2 * b)
    net.finish()
    block_copy.wait()
    wait_all(SREC, 5)
    out_stats[...] = jnp.sum(SREC[...], axis=0)
    wait_all(SREC, 4)
    patch_out.wait()


def update_kernel(
    task_grad, stats, master, first_moment, second_moment, block_in, patch_in,
    out_grad, out_first, out_second, out_master, out_copy, out_norm, out_rms, block_out, patch_out,
    block_held, patch_held, sem,
):
    inward = [
        pltpu.make_async_copy(block_in.at[0], block_held.at[0], sem.at[0]),
        pltpu.make_async_copy(block_in.at[1], block_held.at[1], sem.at[1]),
        pltpu.make_async_copy(patch_in, patch_held, sem.at[2]),
    ]
    outward = [
        pltpu.make_async_copy(block_held.at[0], block_out.at[0], sem.at[3]),
        pltpu.make_async_copy(block_held.at[1], block_out.at[1], sem.at[4]),
        pltpu.make_async_copy(patch_held, patch_out, sem.at[5]),
    ]
    for copy in inward:
        copy.start()
    st = stats[0:1, :]
    norm = jnp.sqrt(st[0:1, 0:1])
    grad = task_grad[...] * (clip_level / jnp.maximum(norm, clip_level))
    first = beta_one * first_moment[...] + (1.0 - beta_one) * grad
    second = beta_two * second_moment[...] + (1.0 - beta_two) * grad * grad
    step_size = (
        first / (1.0 - beta_one**STEP) / (jnp.sqrt(second / (1.0 - beta_two**STEP)) + adam_eps)
    )
    old = master[...]
    new = old - learn_rate * (step_size + decay_rate * old)
    out_grad[...] = grad
    out_first[...] = first
    out_second[...] = second
    out_master[...] = new
    out_copy[...] = new.astype(BF16)
    out_norm[0] = norm[0, 0]
    rms = jnp.sqrt(st / (st[0:1, 4:5] * D))
    for i in range(3):
        out_rms[i] = rms[0, i + 1]
    for copy, after in zip(inward, outward):
        copy.wait()
        after.start()
    for copy in outward:
        copy.wait()


def fast_body(
    patches, lengths, tasks, prompt_master, first_moment, second_moment,
    gain_one, gain_two, w_qkv, w_out, w_up, w_down, cotangent,
):
    vmem = pl.BlockSpec(memory_space=pltpu.VMEM)
    smem = pl.BlockSpec(memory_space=pltpu.SMEM)
    anywhere = pl.BlockSpec(memory_space=pl.ANY)
    V = pltpu.VMEM
    block, patch, task, stats = pl.pallas_call(
        layer_kernel,
        out_shape=[
            jax.ShapeDtypeStruct((IMGS, ROWS, D), BF16),
            jax.ShapeDtypeStruct((PATCH, IMGS, D), BF16),
            jax.ShapeDtypeStruct((TASKS, PART), F32),
            jax.ShapeDtypeStruct((1, 128), F32),
        ],
        in_specs=[anywhere, smem, smem, vmem, vmem, vmem, vmem, vmem, anywhere, anywhere, anywhere],
        out_specs=[anywhere] * 2 + [vmem] * 2,
        scratch_shapes=[
            V((1, 2, 8, 16, PADP), BF16),
            V((1, 2, 8, 96, 2 * D), BF16),
            V((2, 2, 8, 96, 2 * CHUNKS[0]), BF16),
            V((2, 2, 8, 96, 2 * CHUNKS[1]), BF16),
            V((2, 2, 8, 96, 2 * CHUNKS[2]), BF16),
            V((TASKS, PADP), F32),
            V((16, 4, PADP), F32),
            V((IMGS, ROWS, D), F32),
            V((IMGS, ROWS, D), BF16),
            V((4, IMGS, ROWS, 640), BF16),
            V((8, 3, ROWS, ROWS), BF16),
            V((IMGS, ROWS, 1024), BF16),
            V((IMGS, ROWS, D), F32),
            V((IMGS, ROWS, D), BF16),
            V((IMGS, ROWS, D), BF16),
            V((IMGS * ROWS, 2 * CHUNKS[0]), BF16),
            V((IMGS * ROWS, 2 * CHUNKS[0]), BF16),
            V((IMGS, ROWS, D), F32),
            V((IMGS, ROWS, D), F32),
            V((IMGS, ROWS, D), F32),
            V((IMGS, ROWS, D), BF16),
            V((4, IMGS, ROWS, 640), BF16),
            V((4, IMGS, ROWS, 256), BF16),
            V((25, 2, D), F32),
            V((PATCH, IMGS, D), F32),
            V((PATCH, IMGS, D), BF16),
            V((IMGS, ROWS, D), BF16),
            V((IMGS, NDEV, 2, PADP // 2), BF16),
            V((IMGS, NDEV, 2, PADP // 2), BF16),
            V((NDEV, IMGS, TASKS, 128), F32),
            V((NDEV, 1, 128), F32),
            V((1, 128), F32),
            pltpu.SemaphoreType.DMA((10,)),
            pltpu.SemaphoreType.DMA((RING,)),
            pltpu.SemaphoreType.DMA((13 + 21 * (1 + len(CHUNKS)),)),
            pltpu.SemaphoreType.DMA((6,)),
        ],
        compiler_params=pltpu.CompilerParams(
            collective_id=0, has_side_effects=True, vmem_limit_bytes=58 << 20
        ),
    )(
        patches.transpose(1, 0, 2), lengths, tasks.T, prompt_master, gain_one, gain_two,
        w_qkv.transpose(1, 0, 2), w_out, w_up, w_down.T, cotangent,
    )
    state = jax.ShapeDtypeStruct((TASKS, PART), F32)
    grad, first, second, master, copy, norm, rms, block_out, patch_out = pl.pallas_call(
        update_kernel,
        out_shape=[state] * 4
        + [
            jax.ShapeDtypeStruct((TASKS, PART), BF16),
            jax.ShapeDtypeStruct((1,), F32),
            jax.ShapeDtypeStruct((3,), F32),
            jax.ShapeDtypeStruct((IMGS, ROWS, D), BF16),
            jax.ShapeDtypeStruct((PATCH, IMGS, D), BF16),
        ],
        in_specs=[vmem] * 5 + [anywhere] * 2,
        out_specs=[vmem] * 5 + [smem] * 2 + [anywhere] * 2,
        scratch_shapes=[V((IMGS, ROWS, D), BF16), V((PATCH, IMGS, D), BF16), pltpu.SemaphoreType.DMA((6,))],
    )(task, stats, prompt_master, first_moment, second_moment, block, patch)
    return (
        block_out, patch_out.transpose(1, 0, 2), grad, norm.reshape(()), first, second, master, copy, rms,
    )


def layer_norm(values, gain):
    centre = jnp.mean(values, axis=-1, keepdims=True)
    shifted = values - centre
    spread = jnp.mean(shifted * shifted, axis=-1, keepdims=True)
    return shifted * lax.rsqrt(spread + eps_norm) * gain


def whole_norm_back(values, gain, upstream):
    centre = jnp.mean(values, axis=-1, keepdims=True)
    shifted = values - centre
    spread = jnp.mean(shifted * shifted, axis=-1, keepdims=True)
    scaled = lax.rsqrt(spread + eps_norm)
    normal_part = shifted * scaled
    weighted = upstream * gain
    return scaled * (
        weighted
        - jnp.mean(weighted, axis=-1, keepdims=True)
        - normal_part * jnp.mean(weighted * normal_part, axis=-1, keepdims=True)
    )


def gelu_slope(upward):
    cumul = 0.5 * (1.0 + lax.erf(upward * 0.7071067811865476))
    density = jnp.exp(-0.5 * upward * upward) * 0.3989422804014327
    return cumul + upward * density


def attend_forward(group_normed, group_limit, w_mix, block_images):
    group_size, row_count, feature_count = group_normed.shape
    lane_width = w_mix.shape[2]
    head_count = lane_width // HEAD_DIM
    scale = 1.0 / math.sqrt(HEAD_DIM)
    mask_all = jnp.arange(row_count, dtype=jnp.int32)[None, :] < group_limit[:, None]

    def one_block(block_index):
        first_row = block_index * block_images
        block_in = lax.dynamic_slice_in_dim(group_normed, first_row, block_images, 0)
        key_mask = lax.dynamic_slice_in_dim(mask_all, first_row, block_images, 0)
        mixed_qkv = jnp.einsum(
            "brd,dce->brce", block_in, w_mix, preferred_element_type=jnp.float32
        ).astype(jnp.bfloat16)
        split_heads = mixed_qkv.reshape(block_images, row_count, 3, head_count, HEAD_DIM)
        scores = (
            jnp.einsum(
                "bqhe,bkhe->bhqk",
                split_heads[:, :, 0],
                split_heads[:, :, 1],
                preferred_element_type=jnp.float32,
            )
            * scale
        )
        scores = jnp.where(key_mask[:, None, None, :], scores, -1e30)
        row_top = jnp.max(scores, axis=-1, keepdims=True)
        exponent = jnp.exp(scores - row_top)
        row_total = jnp.sum(exponent, axis=-1, keepdims=True)
        attend_weights = (exponent / row_total).astype(jnp.bfloat16)
        context = jnp.einsum(
            "bhqk,bkhe->bqhe",
            attend_weights,
            split_heads[:, :, 2],
            preferred_element_type=jnp.float32,
        )
        context = context.astype(jnp.bfloat16).reshape(block_images, row_count, lane_width)
        return (mixed_qkv, context, (row_top + jnp.log(row_total))[..., 0])

    mixed_qkv, context, logsums = lax.map(
        one_block, jnp.arange(group_size // block_images, dtype=jnp.int32)
    )
    return (
        mixed_qkv.reshape(group_size, row_count, 3, lane_width),
        context.reshape(group_size, row_count, lane_width),
        logsums.reshape(group_size, head_count, row_count),
    )


def attend_back(mixed_qkv, logsums, group_limit, grad_context, block_images):
    group_size, row_count, three_parts, lane_width = mixed_qkv.shape
    head_count = lane_width // HEAD_DIM
    scale = 1.0 / math.sqrt(HEAD_DIM)
    mask_all = jnp.arange(row_count, dtype=jnp.int32)[None, :] < group_limit[:, None]

    def one_block(block_index):
        first_row = block_index * block_images
        split_heads = lax.dynamic_slice_in_dim(mixed_qkv, first_row, block_images, 0).reshape(
            block_images, row_count, 3, head_count, HEAD_DIM
        )
        queries = split_heads[:, :, 0]
        keys_all = split_heads[:, :, 1]
        values = split_heads[:, :, 2]
        key_mask = lax.dynamic_slice_in_dim(mask_all, first_row, block_images, 0)
        logsum = lax.dynamic_slice_in_dim(logsums, first_row, block_images, 0)
        grad_out = lax.dynamic_slice_in_dim(grad_context, first_row, block_images, 0).reshape(
            block_images, row_count, head_count, HEAD_DIM
        )
        scores = (
            jnp.einsum("bqhe,bkhe->bhqk", queries, keys_all, preferred_element_type=jnp.float32)
            * scale
        )
        scores = jnp.where(key_mask[:, None, None, :], scores, -1e30)
        attend_weights = jnp.exp(scores - logsum[..., None])
        grad_weights = jnp.einsum(
            "bqhe,bkhe->bhqk", grad_out, values, preferred_element_type=jnp.float32
        )
        row_inner = jnp.sum(attend_weights * grad_weights, axis=-1, keepdims=True)
        grad_scores = (attend_weights * (grad_weights - row_inner)).astype(jnp.bfloat16)
        grad_query = (
            jnp.einsum("bhqk,bkhe->bqhe", grad_scores, keys_all, preferred_element_type=jnp.float32)
            * scale
        )
        grad_key = (
            jnp.einsum("bhqk,bqhe->bkhe", grad_scores, queries, preferred_element_type=jnp.float32)
            * scale
        )
        grad_value = jnp.einsum(
            "bhqk,bqhe->bkhe",
            attend_weights.astype(jnp.bfloat16),
            grad_out,
            preferred_element_type=jnp.float32,
        )
        stacked = jnp.stack([grad_query, grad_key, grad_value], axis=2).astype(jnp.bfloat16)
        return stacked.reshape(block_images, row_count, 3, lane_width)

    grad_mixed = lax.map(one_block, jnp.arange(group_size // block_images, dtype=jnp.int32))
    return grad_mixed.reshape(group_size, row_count, 3, lane_width)


def expand_units(group_two, w_expand, block_images):
    group_size, row_count, feature_count = group_two.shape

    def one_block(block_index):
        block_in = lax.dynamic_slice_in_dim(group_two, block_index * block_images, block_images, 0)
        upward = jnp.einsum("brd,df->brf", block_in, w_expand, preferred_element_type=jnp.float32)
        return jax.nn.gelu(upward, approximate=False).astype(jnp.bfloat16)

    act_units = lax.map(one_block, jnp.arange(group_size // block_images, dtype=jnp.int32))
    return act_units.reshape(group_size, row_count, w_expand.shape[1])


def units_back(grad_group, group_two, w_expand, w_reduce, block_images):
    group_size, row_count, feature_count = group_two.shape

    def one_block(block_index):
        first_row = block_index * block_images
        grad_in = lax.dynamic_slice_in_dim(grad_group, first_row, block_images, 0)
        norm_in = lax.dynamic_slice_in_dim(group_two, first_row, block_images, 0)
        back_units = jnp.einsum(
            "brd,fd->brf", grad_in, w_reduce, preferred_element_type=jnp.float32
        )
        upward = jnp.einsum("brd,df->brf", norm_in, w_expand, preferred_element_type=jnp.float32)
        return (back_units * gelu_slope(upward)).astype(jnp.bfloat16)

    grad_units = lax.map(one_block, jnp.arange(group_size // block_images, dtype=jnp.int32))
    return grad_units.reshape(group_size, row_count, w_expand.shape[1])


def rows_term(source, weight, form):
    return jnp.einsum(form, source, weight, preferred_element_type=jnp.float32)


def body(
    patches,
    lengths,
    tasks,
    prompt_master,
    first_moment,
    second_moment,
    gain_one,
    gain_two,
    w_qkv,
    w_out,
    w_up,
    w_down,
    cotangent,
):
    held_count, patch_count, feature_count = patches.shape
    row_count = cotangent.shape[1]
    lead_count = row_count - patch_count
    task_count = prompt_master.shape[0]
    prompt_table = lax.all_gather(
        prompt_master.astype(jnp.bfloat16), ("dp", "mp"), axis=1, tiled=True
    )
    chosen = tasks == jnp.arange(task_count, dtype=jnp.int32)[None, :]
    lead_part = jnp.dot(
        chosen.astype(jnp.bfloat16), prompt_table, preferred_element_type=jnp.float32
    )
    residual = jnp.concatenate(
        [lead_part.reshape(held_count, lead_count, feature_count), patches.astype(jnp.float32)],
        axis=1,
    )
    row_limit = lengths + lead_count
    w_mix, w_expand, w_reduce, w_rows = (
        lax.all_gather(w_qkv, "dp", axis=0, tiled=True),
        lax.all_gather(w_up, "dp", axis=0, tiled=True),
        lax.all_gather(w_down, "dp", axis=1, tiled=True),
        lax.all_gather(w_out, "dp", axis=1, tiled=True),
    )
    normed = layer_norm(residual, gain_one).astype(jnp.bfloat16)
    mp_rank = lax.axis_index("mp")
    group_normed, group_bound = (
        lax.all_gather(normed, "mp", axis=0, tiled=True),
        lax.all_gather(row_limit.astype(jnp.bfloat16), "mp", axis=0, tiled=True),
    )
    group_limit = group_bound.astype(jnp.int32)
    mixed_qkv, context, logsums = attend_forward(group_normed, group_limit, w_mix, held_count)
    attn_out = lax.psum_scatter(
        rows_term(context, w_rows, "brc,cd->brd"), "mp", scatter_dimension=0, tiled=True
    )
    residual_two = residual + attn_out
    normed_two = layer_norm(residual_two, gain_two).astype(jnp.bfloat16)
    group_two = lax.all_gather(normed_two, "mp", axis=0, tiled=True)
    act_units = expand_units(group_two, w_expand, held_count)
    mlp_out = lax.psum_scatter(
        rows_term(act_units, w_reduce, "brf,fd->brd").astype(jnp.bfloat16),
        "mp",
        scatter_dimension=0,
        tiled=True,
    ).astype(jnp.float32)
    block_sum = residual_two + mlp_out
    live_rows = (jnp.arange(row_count, dtype=jnp.int32)[None, :] < row_limit[:, None]).astype(
        jnp.float32
    )[:, :, None]
    square_sums = jnp.stack(
        [
            jnp.sum(block_sum * block_sum * live_rows),
            jnp.sum(attn_out * attn_out * live_rows),
            jnp.sum(mlp_out * mlp_out * live_rows),
        ]
    )
    live_count = jnp.sum(row_limit).astype(jnp.float32)
    w_mix, w_expand, w_reduce, w_rows = (
        lax.all_gather(w_qkv, "dp", axis=0, tiled=True),
        lax.all_gather(w_up, "dp", axis=0, tiled=True),
        lax.all_gather(w_down, "dp", axis=1, tiled=True),
        lax.all_gather(w_out, "dp", axis=1, tiled=True),
    )
    grad_held = lax.dynamic_slice_in_dim(cotangent, mp_rank * held_count, held_count, 0)
    grad_units = units_back(cotangent, group_two, w_expand, w_reduce, held_count)
    grad_normed_two = lax.psum_scatter(
        rows_term(grad_units, w_expand, "brf,df->brd"), "mp", scatter_dimension=0, tiled=True
    )
    grad_two = grad_held.astype(jnp.float32) + whole_norm_back(residual_two, gain_two, grad_normed_two)
    grad_low = grad_two.astype(jnp.bfloat16)
    grad_context = jnp.einsum(
        "brd,cd->brc",
        lax.all_gather(grad_low, "mp", axis=0, tiled=True),
        w_rows,
        preferred_element_type=jnp.float32,
    ).astype(jnp.bfloat16)
    grad_mixed = attend_back(mixed_qkv, logsums, group_limit, grad_context, held_count)
    grad_normed = lax.psum_scatter(
        rows_term(grad_mixed, w_mix, "brce,dce->brd").astype(jnp.bfloat16),
        "mp",
        scatter_dimension=0,
        tiled=True,
    ).astype(jnp.float32)
    grad_residual = grad_two + whole_norm_back(residual, gain_one, grad_normed)
    patch_grad = grad_residual[:, lead_count:].astype(jnp.bfloat16)
    lead_grad = grad_residual[:, :lead_count].reshape(held_count, lead_count * feature_count)
    task_term = jnp.dot(
        chosen.astype(jnp.float32).T,
        lead_grad,
        precision=lax.Precision.HIGHEST,
        preferred_element_type=jnp.float32,
    )
    task_grad = lax.psum_scatter(task_term, ("dp", "mp"), scatter_dimension=1, tiled=True)
    square = jnp.sum(task_grad * task_grad)
    square, square_sums, live_count = lax.psum((square, square_sums, live_count), ("dp", "mp"))
    grad_norm = jnp.sqrt(square)
    prompt_grad = task_grad * (clip_level / jnp.maximum(grad_norm, clip_level))
    new_first = beta_one * first_moment + (1.0 - beta_one) * prompt_grad
    new_second = beta_two * second_moment + (1.0 - beta_two) * prompt_grad * prompt_grad
    step_size = (
        new_first
        / (1.0 - beta_one**STEP)
        / (jnp.sqrt(new_second / (1.0 - beta_two**STEP)) + adam_eps)
    )
    new_master = prompt_master - learn_rate * (step_size + decay_rate * prompt_master)
    rms_stats = jnp.sqrt(square_sums / (live_count * feature_count))
    return (
        block_sum.astype(jnp.bfloat16),
        patch_grad,
        prompt_grad,
        grad_norm,
        new_first,
        new_second,
        new_master,
        new_master.astype(jnp.bfloat16),
        rms_stats,
    )


def solution(mesh):
    small = mesh.shape["dp"] == 8 and mesh.shape["mp"] == 4
    return jax.shard_map(
        fast_body if small else body,
        mesh=mesh,
        in_specs=(
            P(("dp", "mp"), None, None),
            P(("dp", "mp")),
            P(("dp", "mp"), None),
            P(None, ("dp", "mp")),
            P(None, ("dp", "mp")),
            P(None, ("dp", "mp")),
            P(),
            P(),
            P("dp", None, "mp"),
            P("mp", "dp"),
            P("dp", "mp"),
            P("mp", "dp"),
            P("dp", None, None),
        ),
        out_specs=(
            P(("dp", "mp"), None, None),
            P(("dp", "mp"), None, None),
            P(None, ("dp", "mp")),
            P(),
            P(None, ("dp", "mp")),
            P(None, ("dp", "mp")),
            P(None, ("dp", "mp")),
            P(None, ("dp", "mp")),
            P(),
        ),
        check_vma=False,
    )
```

```python
import functools
import math

import jax
import jax.numpy as jnp
from jax import lax
from jax.experimental import pallas as pl
from jax.experimental.pallas import tpu as pltpu
from jax.sharding import PartitionSpec as P

HEAD_DIM = 64
STEP = 10
MESH = pl.DeviceIdType.MESH
F32 = jnp.float32
BF16 = jnp.bfloat16

eps_norm = 1e-06
clip_level = 1.0
beta_one = 0.9
beta_two = 0.999
learn_rate = 3.0
decay_rate = 0.05
adam_eps = 1e-08

D = 768
ROWS = 256
LEAD = 50
PATCH = 206
IMGS = 2
TASKS = 8
PART = 1200
PADP = 1280
NDEV = 32
DOWNS = (384, 384)
UPS = (384, 384)
SPLITS = ((16, 48, 64, 96), (32, 48, 80, 96), (16, 48, 64, 96), (32, 48, 80, 96), (16, 48, 64, 96))
ORDER = (
    0, 28, 56, 84, 1000, 4, 16, 32, 37, 60, 44, 13, 17, 72, 41, 112, 38, 45, 20, 14,
    18, 65, 48, 42, 46, 15, 19, 39, 69, 49, 140, 66, 21, 76, 121, 73, 116, 22, 43, 47,
    23, 93, 70, 128, 88, 27, 50, 1001, 149, 67, 100, 122, 51, 1002, 125, 74, 71, 75, 55, 144,
    1003, 97, 156, 1004, 94, 1005, 123, 150, 126, 129, 130, 1006, 1007, 153, 98, 101, 1008, 95, 151, 78,
    77, 1009, 127, 79, 131, 1010, 157, 132, 133, 134, 154, 102, 83, 1011, 1013, 99, 103, 1014, 135, 160,
    104, 1012, 158, 139, 1017, 155, 105, 161, 159, 1018, 106, 1019, 107, 162, 1020, 163, 111, 1015, 1016, 167,
    1021, 1022, 1023, 1024,
)


def run_if(cond, f):
    if cond is None:
        f()
    else:
        pl.when(cond())(f)


class Net:
    def __init__(self, send_sem, recv_sem):
        self.send_sem, self.recv_sem = send_sem, recv_sem
        self.sends = self.recvs = 0
        dp, mp = lax.axis_index("dp"), lax.axis_index("mp")
        z, x, y, c = dp // 2, dp % 2, mp // 2, mp % 2
        self.z, self.x, self.y, self.c = z, x, y, c
        self.dp, self.mp = dp, mp
        self.peer = {
            "x": (2 * z + 1 - x, mp),
            "y": (dp, (1 - y) * 2 + c),
            "c": (dp, 2 * y + 1 - c),
            "u": (jnp.minimum(2 * z + 2 + x, 6 + x), mp),
            "d": (jnp.maximum(2 * z - 2 + x, x), mp),
        }

    def send(self, way, view, sem, landed):
        pltpu.make_async_remote_copy(
            src_ref=view,
            dst_ref=view,
            send_sem=self.send_sem.at[sem],
            recv_sem=self.recv_sem.at[landed],
            device_id=self.peer[way],
            device_id_type=MESH,
        ).start()

    def recv(self, view, landed):
        pltpu.make_async_copy(view, view, self.recv_sem.at[landed]).wait()

    def wait_sent(self, view, sem):
        pltpu.make_async_copy(view, view, self.send_sem.at[sem]).wait()


def gather_events(net, G, W, split):
    z, x, y, c = net.z, net.x, net.y, net.c
    r1, r2, r3, rows = split
    some = 4 if r3 > r1 else 0
    f_sem = net.recvs
    zs_sem, zp_sem, m_sem = f_sem + 1, f_sem + 1 + some, f_sem + 5 + some
    l_sem, c_sem = f_sem + 5 + 2 * some, f_sem + 9 + 2 * some
    net.recvs = c_sem + 1
    start_sent, single_sent, pair_sent, middle_sent, last_sent, core_sent = range(net.sends, net.sends + 6)
    net.sends += 6
    every = slice(None)
    ends = r1 + rows - r3

    def V(yy, d, first, last, other=False):
        core = (1 - c) if other else c
        cols = pl.ds(pl.multiple_of(core * W, 128), W)
        return G.at[:, yy, d, pl.ds(first, last - first), cols]

    def two(p):
        return pl.ds(2 * p, 2)

    def one(p):
        return 2 * p + x

    def send(way, yy, d, first, last, sem, landed):
        if last > first:
            net.send(way, V(yy, d, first, last), sem, landed)

    def sides(k, f):
        if k == 0:
            f(z, None, None)
        else:
            pl.when(z >= k)(lambda: f(z - k, "u", z < 3))
            pl.when(z + k <= 3)(lambda: f(z + k, "d", z > 0))

    def middle(p):
        send("x", y, one(p), r1, r2, middle_sent, m_sem + p)
        send("y", y, one(p), r2, r3, middle_sent, m_sem + p)

    def start():
        send("x", y, one(z), 0, r1, start_sent, f_sem)
        send("y", y, one(z), r3, rows, start_sent, f_sem)
        if r3 > r1:
            pl.when(z < 3)(lambda: send("u", y, one(z), r1, r3, single_sent, zs_sem + z))
            pl.when(z > 0)(lambda: send("d", y, one(z), r1, r3, single_sent, zs_sem + z))
            middle(z)

    def pair(way, p):
        send(way, y, two(p), 0, r1, pair_sent, zp_sem + p)
        send(way, every, one(p), r3, rows, pair_sent, zp_sem + p)

    def first_hop():
        net.recv(V(y, one(z), 0, ends), f_sem)
        pl.when(z < 3)(lambda: pair("u", z))
        pl.when(z > 0)(lambda: pair("d", z))

    def single_hop(k):
        def hop(p, way, more):
            net.recv(V(y, one(p), r1, r3), zs_sem + p)
            if k < 3:
                pl.when(more)(lambda: send(way, y, one(p), r1, r3, single_sent, zs_sem + p))
            middle(p)

        sides(k, hop)

    def pair_hop(k):
        def hop(p, way, more):
            net.recv(V(y, two(p), 0, ends), zp_sem + p)
            if k < 3:
                pl.when(more)(lambda: pair(way, p))

        sides(k, hop)

    def last_hop(k):
        def hop(p, way, more):
            if r3 > r1:
                net.recv(V(y, one(p), r1, r3), m_sem + p)
            send("y", y, two(p), 0, r2, last_sent, l_sem + p)
            send("x", every, one(p), r2, rows, last_sent, l_sem + p)

        sides(k, hop)

    def to_core(k):
        def hop(p, way, more):
            net.recv(V(y, two(p), 0, rows), l_sem + p)
            send("c", every, two(p), 0, rows, core_sent, c_sem)

        sides(k, hop)

    def from_core(k):
        if k == 3:
            net.recv(V(every, every, 0, rows, other=True), c_sem)

    def finish():
        net.wait_sent(V(y, one(z), 0, ends), start_sent)
        net.wait_sent(V(y, every, 0, rows), last_sent)
        net.wait_sent(V(every, every, 0, rows), core_sent)
        if r3 > r1:
            net.wait_sent(V(y, pl.ds(0, 4), r1, r3), middle_sent)

        def along(count):
            if r3 > r1:
                net.wait_sent(V(y, pl.ds(0, count), r1, r3), single_sent)
            total = 2 * ends * count
            yy, blocks = min(
                (yy, n) for yy in (1, 2) for n in range(1, 9) if total % (yy * n * 16) == 0 and total // (yy * n) <= rows
            )
            net.wait_sent(V(y if yy == 1 else every, pl.ds(0, blocks), 0, total // (yy * blocks)), pair_sent)

        inner = jnp.logical_and(z > 0, z < 3)
        pl.when(inner)(lambda: along(5))
        pl.when(jnp.logical_not(inner))(lambda: along(1))

    kinds = (start, first_hop, single_hop, pair_hop, last_hop, to_core, from_core)
    return [f if i < 2 else functools.partial(f, k) for i, f in enumerate(kinds) for k in range(4)], finish


def nn(a, b):
    return lax.dot_general(a, b, (((1,), (0,)), ((), ())), preferred_element_type=F32)


def nt(a, b):
    return lax.dot_general(a, b, (((1,), (1,)), ((), ())), preferred_element_type=F32)


def tn(a, b):
    return lax.dot_general(a, b, (((0,), (0,)), ((), ())), preferred_element_type=F32)


def norm_parts(v):
    centre = jnp.mean(v, axis=-1, keepdims=True)
    shifted = v - centre
    spread = jnp.mean(shifted * shifted, axis=-1, keepdims=True)
    scaled = lax.rsqrt(spread + eps_norm)
    return shifted * scaled, scaled


def norm_back(v, gain, upstream):
    normal, scaled = norm_parts(v)
    weighted = upstream * gain
    return scaled * (
        weighted
        - jnp.mean(weighted, axis=-1, keepdims=True)
        - normal * jnp.mean(weighted * normal, axis=-1, keepdims=True)
    )


def keep(lanes, low, high):
    return jnp.where(lanes, low, high)


def layer_kernel(
    patches, lengths, tasks, master, gain_one, gain_two, qkv_in, out_in, u_in, d_in, cot_hbm,
    out_block, out_patch, out_task, out_stats,
    GP, GA, GDS, GUS, LOC, SEL, RES, N1, QKV, PT, CTX, RES2, N2, COT, BACK, ACT, GU, MACC, GACC, G2, G2B, DM, DC, LEADR,
    PAIR, PIN, BOUT, SEND, RECV, ONEHOT, SREC, STSUM, QIN, OIN, MIN, GIN, own_sem, local_sem, send_sem, recv_sem, all_sem,
):
    net = Net(send_sem, recv_sem)
    z, x, y, c, dp, mp = net.z, net.x, net.y, net.c, net.dp, net.mp
    device = dp * 4 + mp

    barrier = pltpu.get_barrier_semaphore()
    for way, cond in (("x", None), ("y", None), ("c", None), ("u", lambda: z < 3), ("d", lambda: z > 0)):
        run_if(
            cond,
            lambda way=way: pl.semaphore_signal(
                barrier, inc=1, device_id=net.peer[way], device_id_type=MESH
            ),
        )

    def own_cols(w):
        return pl.ds(pl.multiple_of(c * w, 128), w)

    cot_copy = pltpu.make_async_copy(cot_hbm.at[pl.ds(mp * IMGS, IMGS)], COT, local_sem.at[0])
    copies = []
    for refs, widths, weight_in in ((GDS, DOWNS, d_in), (GUS, UPS, u_in)):
        first = 0
        for ref, w in zip(refs, widths):
            copies.append(
                pltpu.make_async_copy(
                    weight_in.at[:, pl.ds(first, w)], ref.at[0, y, dp, :, own_cols(w)], own_sem.at[len(copies)]
                )
            )
            first += w
    for copy in copies:
        copy.start()
    patch_copy = pltpu.make_async_copy(patches, PIN, local_sem.at[1])
    small = [
        pltpu.make_async_copy(src, dst, own_sem.at[len(copies) + i])
        for i, (src, dst) in enumerate(
            ((qkv_in, QIN), (out_in, OIN), (master, MIN), (gain_one, GIN.at[0]), (gain_two, GIN.at[1]))
        )
    ]
    for copy in small:
        copy.start()
    patch_copy.start()
    cot_copy.start()
    for copy in small:
        copy.wait()

    qkv = [QIN[i].astype(F32) for i in range(3)]
    outs = OIN[...].astype(F32).T
    low = lax.broadcasted_iota(jnp.int32, (96, 128), 1) < HEAD_DIM

    def tail(v, high):
        v = jnp.concatenate([v[:, 128:192], v[:, 128:192]], axis=1)
        return v

    tiles = [qkv[0][:, 0:128], qkv[1][:, 0:128], qkv[2][:, 0:128]]
    tiles.append(jnp.where(low, tail(qkv[0], 0), tail(qkv[2], 1)))
    tiles.append(jnp.where(low, tail(qkv[1], 0), tail(outs, 1)))
    tiles.append(outs[:, 0:128])
    GA[0, pl.ds(y, 1), pl.ds(dp, 1), :, own_cols(D)] = (
        jnp.concatenate(tiles, axis=1).astype(BF16)[None, None]
    )

    LOC[:, 0:PART] = MIN[...]
    lane = lax.broadcasted_iota(jnp.int32, (TASKS, PADP - PART), 1)
    LOC[:, PART:PADP] = jnp.where(
        lane == 0, tasks[0, 0].astype(F32), jnp.where(lane == 1, tasks[0, 1].astype(F32), 0.0)
    )
    half = PADP // 2
    GP[0, pl.ds(y, 1), pl.ds(dp, 1), :, own_cols(half)] = (
        jnp.concatenate([LOC[:, 0:half], LOC[:, half:PADP]], axis=0).astype(BF16)[None, None]
    )
    for copy in copies:
        copy.wait()
    inner = jnp.logical_and(z > 0, z < 3)
    run_if(lambda: inner, lambda: pl.semaphore_wait(barrier, 5))
    run_if(lambda: jnp.logical_not(inner), lambda: pl.semaphore_wait(barrier, 4))

    gathers = [gather_events(net, GP, half, (16, 16, 16, 16))]
    for ref, w, split in zip((GA, *GDS, *GUS), (D, *DOWNS, *UPS), SPLITS):
        gathers.append(gather_events(net, ref, w, split))

    g1 = GIN[0].reshape(1, D)
    g2 = GIN[1].reshape(1, D)
    limits = [lengths[b] + LEAD for b in range(IMGS)]
    live = [
        (lax.broadcasted_iota(jnp.int32, (ROWS, 1), 0) < limits[b]).astype(F32) for b in range(IMGS)
    ]

    def place_rows():
        patch_copy.wait()
        cot_copy.wait()
        for b in range(IMGS):
            RES[b, LEAD:ROWS, :] = PIN[:, b, :].astype(F32)

    task_rows = lax.broadcasted_iota(jnp.int32, (TASKS, 1), 0)

    def pick(d, _):
        dd, mm = d // 4, d % 4
        raw = GP[0, mm // 2, dd, :, pl.ds(pl.multiple_of((mm % 2) * half, 128), half)].astype(F32)
        low, high = raw[0:8], raw[8:16]
        rep, j = d // 16, d % 16
        for b in range(IMGS):
            hot = (task_rows == tasks[0, b]).astype(F32)
            row = 2 * rep + b
            SEL[j, pl.ds(row, 1), 0:half] = jnp.sum(low * hot, axis=0, keepdims=True)
            SEL[j, pl.ds(row, 1), half:PADP] = jnp.sum(high * hot, axis=0, keepdims=True)
        base = PART - half
        for b in range(IMGS):
            which = high[0:1, base + b : base + b + 1]
            ONEHOT[d, b] = (
                lax.broadcasted_iota(jnp.int32, (TASKS, 128), 0).astype(F32) == which
            ).astype(F32)
        return 0

    def place_prompts():
        lax.fori_loop(0, NDEV, pick, 0)
        wide = lax.broadcasted_iota(jnp.int32, (4, D), 1)
        for r in range(25):
            j, off = (D * r) // PART, (D * r) % PART
            first = min(D, PART - off)
            low = SEL[j, 0:4, :]
            seg = (pltpu.roll(low, PADP - off, 1) if off else low)[:, 0:D]
            if first < D:
                seg = jnp.where(wide < first, seg, pltpu.roll(SEL[j + 1, 0:4, :], first, 1)[:, 0:D])
            for rep in range(2):
                for b in range(IMGS):
                    RES[b, 25 * rep + r : 25 * rep + r + 1, :] = seg[2 * rep + b : 2 * rep + b + 1]

    def norm_one():
        for b in range(IMGS):
            N1[b] = (norm_parts(RES[b])[0] * g1).astype(BF16)

    def weight(ref, core, first, width, span):
        cols = pl.ds(pl.multiple_of(core * span + first, 128), width)
        return ref[:, :, cols].reshape(D, width)

    left = lax.broadcasted_iota(jnp.int32, (ROWS, 128), 1) < HEAD_DIM
    scale = 1.0 / math.sqrt(HEAD_DIM)
    wide = lax.broadcasted_iota(jnp.int32, (1, 640), 1)
    q_scale = jnp.where((wide < 128) | ((wide >= 384) & (wide < 448)), scale, 1.0)

    def project(m):
        w = weight(GA.at[0, m // 2], m % 2, 0, 640, D)
        mixed = nn(N1[...].reshape(IMGS * ROWS, D), w) * q_scale
        QKV[m] = mixed.astype(BF16).reshape(IMGS, ROWS, 640)

    key_rows = lax.broadcasted_iota(jnp.int32, (ROWS, ROWS), 0)
    zero = jnp.zeros((), BF16)

    def attend(t):
        b, m = t // 4, t % 4
        tile = lambda i: QKV[m, b, :, 128 * i : 128 * i + 128]
        q01, k01, v01, q2v2, k2 = (tile(i) for i in range(5))
        mask = key_rows < (lengths[b] + LEAD)

        def soft(keys, queries):
            s = jnp.where(mask, nt(keys, queries), -1e30)
            e = jnp.exp(s - jnp.max(s, axis=0, keepdims=True))
            return (e * (1.0 / jnp.sum(e, axis=0, keepdims=True))).astype(BF16)

        p0 = soft(k01, keep(left, q01, zero))
        p1 = soft(k01, keep(left, zero, q01))
        p2 = soft(k2, keep(left, q2v2, zero))
        PT[t, 0], PT[t, 1], PT[t, 2] = p0, p1, p2
        CTX[b, :, m * 256 : m * 256 + 128] = keep(left, 0.0, tn(p2, q2v2)).astype(BF16)
        CTX[b, :, m * 256 + 128 : m * 256 + 256] = keep(
            left, tn(p0, v01), tn(p1, v01)
        ).astype(BF16)

    def attend_two(t):
        attend(2 * t)
        attend(2 * t + 1)

    sums = [jnp.zeros((1, 1), F32) for _ in range(3)]

    def total(v):
        return jnp.sum(jnp.sum(v, axis=0, keepdims=True), axis=1, keepdims=True)

    def project_out(b):
        attn = jnp.zeros((ROWS, D), F32)
        for m in range(4):
            attn += nt(CTX[b, :, 256 * m : 256 * m + 256], weight(GA.at[0, m // 2], m % 2, 512, 256, D))
        sums[1] += total(attn * attn * live[b])
        res2 = RES[b] + attn
        RES2[b] = res2
        N2[b] = (norm_parts(res2)[0] * g2).astype(BF16)

    def back_units(i, yy):
        w, first = DOWNS[i], sum(DOWNS[:i])
        cot = COT[...].reshape(IMGS * ROWS, D)
        for core in range(2):
            back = nn(cot, weight(GDS[i].at[0, yy], core, 0, w, w))
            BACK[yy, :, core * D + first : core * D + first + w] = back.astype(BF16)

    def up_units(i, yy):
        w, first = UPS[i], sum(UPS[:i])
        rows2 = N2[...].reshape(IMGS * ROWS, D)
        for core in range(2):
            up = nn(rows2, weight(GUS[i].at[0, yy], core, 0, w, w))
            back = BACK[yy, :, core * D + first : core * D + first + w].astype(F32)
            cumul = 0.5 * (1.0 + lax.erf(up * 0.7071067811865476))
            density = jnp.exp(-0.5 * up * up) * 0.3989422804014327
            ACT[:, w * core : w * (core + 1)] = (up * cumul).astype(BF16)
            GU[:, w * core : w * (core + 1)] = (back * (cumul + up * density)).astype(BF16)

    def add_units(i, yy):
        w, first = UPS[i], sum(UPS[:i])
        d = max(d for d in range(len(DOWNS)) if sum(DOWNS[:d]) <= first)
        inside = first - sum(DOWNS[:d])
        if w == DOWNS[d]:
            mlp = nt(ACT[:, 0 : 2 * w], weight(GDS[d].at[0, yy], 0, 0, 2 * w, w))
        else:
            mlp = sum(
                nt(ACT[:, w * core : w * (core + 1)], weight(GDS[d].at[0, yy], core, inside, w, DOWNS[d]))
                for core in range(2)
            )
        grad = nt(GU[:, 0 : 2 * w], weight(GUS[i].at[0, yy], 0, 0, 2 * w, w))
        mlp, grad = mlp.reshape(IMGS, ROWS, D), grad.reshape(IMGS, ROWS, D)
        if i == 0 and yy == 0:
            MACC[...] = mlp
            GACC[...] = grad
        else:
            MACC[...] += mlp
            GACC[...] += grad

    steps = [place_rows, place_prompts, norm_one]
    steps += [functools.partial(project, m) for m in range(4)]
    steps += [functools.partial(attend_two, t) for t in range(4)]
    steps += [functools.partial(project_out, b) for b in range(IMGS)]
    steps += [functools.partial(back_units, i, yy) for i in range(len(DOWNS)) for yy in range(2)]
    for i in range(len(UPS)):
        for yy in range(2):
            steps += [functools.partial(up_units, i, yy), functools.partial(add_units, i, yy)]
    for item in ORDER:
        if item < 1000:
            gathers[item // 28][0][item % 28]()
        else:
            steps[item - 1000]()

    for b in range(IMGS):
        g = COT[b].astype(F32) + norm_back(RES2[b], g2, GACC[b])
        G2[b] = g
        G2B[b] = g.astype(BF16)

    def context_back(m, _):
        cols = pl.ds(pl.multiple_of((m % 2) * D + 512, 128), 256)
        w = GA[0, m // 2, :, :, cols].reshape(D, 256)
        DC[m] = nn(G2B[...].reshape(IMGS * ROWS, D), w).astype(BF16).reshape(IMGS, ROWS, 256)
        return 0

    lax.fori_loop(0, 4, context_back, 0, unroll=4)

    def attend_back(b):
        tiles, grad_probs, grad_scores = [], [], []
        for m in range(4):
            tiles.append(
                [QKV[m, b, :, 128 * i : 128 * i + 128] for i in range(5)]
                + [DC[m, b, :, 0:128], DC[m, b, :, 128:256]]
            )
            q01, k01, v01, q2v2, k2, c2, c01 = tiles[m]
            grad_probs.append(
                [nt(keep(left, v01, zero), c01), nt(keep(left, zero, v01), c01), nt(keep(left, zero, q2v2), c2)]
            )
        for m in range(4):
            out = []
            for h in range(3):
                pf, dp_ = PT[4 * b + m, h].astype(F32), grad_probs[m][h]
                inner = jnp.sum(pf * dp_, axis=0, keepdims=True)
                out.append((pf * (dp_ - inner)).astype(BF16))
            grad_scores.append(out)
        for m in range(4):
            q01, k01, v01, q2v2, k2, c2, c01 = tiles[m]
            s0, s1, s2 = grad_scores[m]
            p0, p1, p2 = (PT[4 * b + m, h] for h in range(3))
            DM[m, b, :, 0:128] = (keep(left, tn(s0, k01), tn(s1, k01)) * scale).astype(BF16)
            DM[m, b, :, 128:256] = keep(left, nn(s0, q01), nn(s1, q01)).astype(BF16)
            DM[m, b, :, 256:384] = keep(left, nn(p0, c01), nn(p1, c01)).astype(BF16)
            DM[m, b, :, 384:512] = keep(left, tn(s2, k2) * scale, nn(p2, c2)).astype(BF16)
            DM[m, b, :, 512:640] = keep(left, nn(s2, q2v2), 0.0).astype(BF16)

    def grad_rows(b, first, last):
        grad = jnp.zeros((last - first, D), F32)
        for m in range(4):
            grad += nt(DM[m, b, first:last], weight(GA.at[0, m // 2], m % 2, 0, 640, D))
        GACC[b, first:last] = G2[b, first:last] + norm_back(RES[b, first:last], g1, grad)

    def swap(k, src, dst, sems):
        other = lax.rem(device + k, NDEV)
        pltpu.make_async_remote_copy(
            src_ref=src(other),
            dst_ref=dst,
            send_sem=all_sem.at[sems],
            recv_sem=all_sem.at[sems + 1],
            device_id=(other // 4, lax.rem(other, 4)),
            device_id_type=MESH,
        ).start()

    wide = lax.broadcasted_iota(jnp.int32, (2, PADP), 1)

    def to_owners(b):
        for rep in range(2):
            LEADR[:, rep : rep + 1, :] = GACC[b, 25 * rep : 25 * rep + 25, :][:, None, :]
        for q in range(16):
            r, off = (PART * q) // D, (PART * q) % D
            msg, have = None, -off
            while have < PART:
                row = LEADR[r]
                moved = pltpu.roll(row, have % D, 1) if have % D else row
                moved = jnp.concatenate([moved, moved[:, 0 : PADP - D]], axis=1)
                msg = moved if msg is None else jnp.where(wide < have, msg, moved)
                have += D
                r += 1
            msg = jnp.where(wide < PART, msg, 0.0).astype(BF16)
            for rep in range(2):
                SEND[b, 16 * rep + q] = jnp.concatenate(
                    [msg[rep : rep + 1, 0:half], msg[rep : rep + 1, half:PADP]], axis=0
                )
        for k in range(1, NDEV):
            swap(k, lambda other: SEND.at[b, other], RECV.at[b, device], 2 * b)
        RECV[b, pl.ds(device, 1)] = SEND[b, pl.ds(device, 1)]

    def others(ref):
        return ref.at[pl.ds(0, NDEV - 1)]

    def wait_all(ref, sem):
        pltpu.make_async_copy(others(ref), others(ref), all_sem.at[sem]).wait()

    attend_back(0)
    grad_rows(0, 0, ROWS)
    to_owners(0)
    attend_back(1)
    some = 64
    grad_rows(1, 0, some)
    to_owners(1)

    grad_rows(1, some, ROWS)
    for b in range(IMGS):
        mlp = MACC[b]
        block = RES2[b] + mlp
        BOUT[b] = block.astype(BF16)
        sums[0] += total(block * block * live[b])
        sums[2] += total(mlp * mlp * live[b])
    block_copy = pltpu.make_async_copy(BOUT, out_block, local_sem.at[2])
    block_copy.start()

    def add_image(b, acc):
        wait_all(RECV.at[b], 2 * b + 1)

        def add(s, acc):
            rows = RECV[b, s].astype(F32)
            hot = jnp.concatenate([ONEHOT[s, b]] * (half // 128), axis=1)
            return acc[0] + hot * rows[0:1], acc[1] + hot * rows[1:2]

        return lax.fori_loop(0, NDEV, add, acc, unroll=8)

    acc = (jnp.zeros((TASKS, half), F32), jnp.zeros((TASKS, half), F32))
    acc = add_image(1, add_image(0, acc))
    square = total(acc[0] * acc[0]) + total(acc[1] * acc[1])
    lane = lax.broadcasted_iota(jnp.int32, (1, 128), 1)
    count = (limits[0] + limits[1]).astype(F32)
    stats = jnp.zeros((1, 128), F32)
    for i, v in enumerate((square, sums[0], sums[1], sums[2], count)):
        stats = jnp.where(lane == i, v, stats)
    STSUM[...] = stats
    SREC[pl.ds(device, 1)] = stats[None]
    for k in range(1, NDEV):
        swap(k, lambda other: STSUM, SREC.at[device], 4)

    out_task[...] = jnp.concatenate(acc, axis=1)[:, 0:PART]
    for b in range(IMGS):
        PAIR[:, b : b + 1, :] = GACC[b, LEAD:ROWS, :][:, None, :]
    PIN[...] = PAIR[...].astype(BF16)
    patch_out = pltpu.make_async_copy(PIN, out_patch, local_sem.at[3])
    patch_out.start()
    for b in range(IMGS):
        wait_all(RECV.at[b], 2 * b)
    for gather in gathers:
        gather[1]()
    block_copy.wait()
    wait_all(SREC, 5)
    out_stats[...] = jnp.sum(SREC[...], axis=0)
    wait_all(SREC, 4)
    patch_out.wait()


def update_kernel(
    task_grad, stats, master, first_moment, second_moment, block_in, patch_in,
    out_grad, out_first, out_second, out_master, out_copy, out_norm, out_rms, block_out, patch_out, sem,
):
    copies = [
        pltpu.make_async_copy(block_in, block_out, sem.at[0]),
        pltpu.make_async_copy(patch_in, patch_out, sem.at[1]),
    ]
    for copy in copies:
        copy.start()
    st = stats[0:1, :]
    norm = jnp.sqrt(st[0:1, 0:1])
    grad = task_grad[...] * (clip_level / jnp.maximum(norm, clip_level))
    first = beta_one * first_moment[...] + (1.0 - beta_one) * grad
    second = beta_two * second_moment[...] + (1.0 - beta_two) * grad * grad
    step_size = (
        first / (1.0 - beta_one**STEP) / (jnp.sqrt(second / (1.0 - beta_two**STEP)) + adam_eps)
    )
    old = master[...]
    new = old - learn_rate * (step_size + decay_rate * old)
    out_grad[...] = grad
    out_first[...] = first
    out_second[...] = second
    out_master[...] = new
    out_copy[...] = new.astype(BF16)
    out_norm[0] = norm[0, 0]
    rms = jnp.sqrt(st / (st[0:1, 4:5] * D))
    for i in range(3):
        out_rms[i] = rms[0, i + 1]
    for copy in copies:
        copy.wait()


def fast_body(
    patches, lengths, tasks, prompt_master, first_moment, second_moment,
    gain_one, gain_two, w_qkv, w_out, w_up, w_down, cotangent,
):
    vmem = pl.BlockSpec(memory_space=pltpu.VMEM)
    smem = pl.BlockSpec(memory_space=pltpu.SMEM)
    anywhere = pl.BlockSpec(memory_space=pl.ANY)
    V = pltpu.VMEM
    block, patch, task, stats = pl.pallas_call(
        layer_kernel,
        out_shape=[
            jax.ShapeDtypeStruct((IMGS, ROWS, D), BF16),
            jax.ShapeDtypeStruct((PATCH, IMGS, D), BF16),
            jax.ShapeDtypeStruct((TASKS, PART), F32),
            jax.ShapeDtypeStruct((1, 128), F32),
        ],
        in_specs=[anywhere, smem, smem] + [anywhere] * 8,
        out_specs=[anywhere] * 2 + [vmem] * 2,
        scratch_shapes=[
            V((1, 2, 8, 16, PADP), BF16),
            V((1, 2, 8, 96, 2 * D), BF16),
            [V((1, 2, 8, 96, 2 * w), BF16) for w in DOWNS],
            [V((1, 2, 8, 96, 2 * w), BF16) for w in UPS],
            V((TASKS, PADP), F32),
            V((16, 4, PADP), F32),
            V((IMGS, ROWS, D), F32),
            V((IMGS, ROWS, D), BF16),
            V((4, IMGS, ROWS, 640), BF16),
            V((8, 3, ROWS, ROWS), BF16),
            V((IMGS, ROWS, 1024), BF16),
            V((IMGS, ROWS, D), F32),
            V((IMGS, ROWS, D), BF16),
            V((IMGS, ROWS, D), BF16),
            V((2, IMGS * ROWS, 2 * D), BF16),
            V((IMGS * ROWS, 2 * max(UPS)), BF16),
            V((IMGS * ROWS, 2 * max(UPS)), BF16),
            V((IMGS, ROWS, D), F32),
            V((IMGS, ROWS, D), F32),
            V((IMGS, ROWS, D), F32),
            V((IMGS, ROWS, D), BF16),
            V((4, IMGS, ROWS, 640), BF16),
            V((4, IMGS, ROWS, 256), BF16),
            V((25, 2, D), F32),
            V((PATCH, IMGS, D), F32),
            V((PATCH, IMGS, D), BF16),
            V((IMGS, ROWS, D), BF16),
            V((IMGS, NDEV, 2, PADP // 2), BF16),
            V((IMGS, NDEV, 2, PADP // 2), BF16),
            V((NDEV, IMGS, TASKS, 128), F32),
            V((NDEV, 1, 128), F32),
            V((1, 128), F32),
            V((3, 96, 192), BF16),
            V((192, 96), BF16),
            V((TASKS, PART), F32),
            V((2, D), F32),
            pltpu.SemaphoreType.DMA((5 + len(DOWNS) + len(UPS),)),
            pltpu.SemaphoreType.DMA((4,)),
            pltpu.SemaphoreType.DMA((6 * (2 + len(DOWNS) + len(UPS)),)),
            pltpu.SemaphoreType.DMA((10 + 18 * (1 + len(DOWNS) + len(UPS)),)),
            pltpu.SemaphoreType.DMA((6,)),
        ],
        compiler_params=pltpu.CompilerParams(
            collective_id=0, has_side_effects=True, vmem_limit_bytes=58 << 20
        ),
    )(
        patches.transpose(1, 0, 2), lengths, tasks.T, prompt_master, gain_one, gain_two,
        w_qkv.transpose(1, 0, 2), w_out, w_up, w_down.T, cotangent,
    )
    state = jax.ShapeDtypeStruct((TASKS, PART), F32)
    grad, first, second, master, copy, norm, rms, block_out, patch_out = pl.pallas_call(
        update_kernel,
        out_shape=[state] * 4
        + [
            jax.ShapeDtypeStruct((TASKS, PART), BF16),
            jax.ShapeDtypeStruct((1,), F32),
            jax.ShapeDtypeStruct((3,), F32),
            jax.ShapeDtypeStruct((IMGS, ROWS, D), BF16),
            jax.ShapeDtypeStruct((PATCH, IMGS, D), BF16),
        ],
        in_specs=[vmem] * 7,
        out_specs=[vmem] * 5 + [smem] * 2 + [anywhere] * 2,
        scratch_shapes=[pltpu.SemaphoreType.DMA((2,))],
    )(task, stats, prompt_master, first_moment, second_moment, block, patch)
    return (
        block_out, patch_out.transpose(1, 0, 2), grad, norm.reshape(()), first, second, master, copy, rms,
    )


def layer_norm(values, gain):
    centre = jnp.mean(values, axis=-1, keepdims=True)
    shifted = values - centre
    spread = jnp.mean(shifted * shifted, axis=-1, keepdims=True)
    return shifted * lax.rsqrt(spread + eps_norm) * gain


def whole_norm_back(values, gain, upstream):
    centre = jnp.mean(values, axis=-1, keepdims=True)
    shifted = values - centre
    spread = jnp.mean(shifted * shifted, axis=-1, keepdims=True)
    scaled = lax.rsqrt(spread + eps_norm)
    normal_part = shifted * scaled
    weighted = upstream * gain
    return scaled * (
        weighted
        - jnp.mean(weighted, axis=-1, keepdims=True)
        - normal_part * jnp.mean(weighted * normal_part, axis=-1, keepdims=True)
    )


def gelu_slope(upward):
    cumul = 0.5 * (1.0 + lax.erf(upward * 0.7071067811865476))
    density = jnp.exp(-0.5 * upward * upward) * 0.3989422804014327
    return cumul + upward * density


def attend_forward(group_normed, group_limit, w_mix, block_images):
    group_size, row_count, feature_count = group_normed.shape
    lane_width = w_mix.shape[2]
    head_count = lane_width // HEAD_DIM
    scale = 1.0 / math.sqrt(HEAD_DIM)
    mask_all = jnp.arange(row_count, dtype=jnp.int32)[None, :] < group_limit[:, None]

    def one_block(block_index):
        first_row = block_index * block_images
        block_in = lax.dynamic_slice_in_dim(group_normed, first_row, block_images, 0)
        key_mask = lax.dynamic_slice_in_dim(mask_all, first_row, block_images, 0)
        mixed_qkv = jnp.einsum(
            "brd,dce->brce", block_in, w_mix, preferred_element_type=jnp.float32
        ).astype(jnp.bfloat16)
        split_heads = mixed_qkv.reshape(block_images, row_count, 3, head_count, HEAD_DIM)
        scores = (
            jnp.einsum(
                "bqhe,bkhe->bhqk",
                split_heads[:, :, 0],
                split_heads[:, :, 1],
                preferred_element_type=jnp.float32,
            )
            * scale
        )
        scores = jnp.where(key_mask[:, None, None, :], scores, -1e30)
        row_top = jnp.max(scores, axis=-1, keepdims=True)
        exponent = jnp.exp(scores - row_top)
        row_total = jnp.sum(exponent, axis=-1, keepdims=True)
        attend_weights = (exponent / row_total).astype(jnp.bfloat16)
        context = jnp.einsum(
            "bhqk,bkhe->bqhe",
            attend_weights,
            split_heads[:, :, 2],
            preferred_element_type=jnp.float32,
        )
        context = context.astype(jnp.bfloat16).reshape(block_images, row_count, lane_width)
        return (mixed_qkv, context, (row_top + jnp.log(row_total))[..., 0])

    mixed_qkv, context, logsums = lax.map(
        one_block, jnp.arange(group_size // block_images, dtype=jnp.int32)
    )
    return (
        mixed_qkv.reshape(group_size, row_count, 3, lane_width),
        context.reshape(group_size, row_count, lane_width),
        logsums.reshape(group_size, head_count, row_count),
    )


def attend_back(mixed_qkv, logsums, group_limit, grad_context, block_images):
    group_size, row_count, three_parts, lane_width = mixed_qkv.shape
    head_count = lane_width // HEAD_DIM
    scale = 1.0 / math.sqrt(HEAD_DIM)
    mask_all = jnp.arange(row_count, dtype=jnp.int32)[None, :] < group_limit[:, None]

    def one_block(block_index):
        first_row = block_index * block_images
        split_heads = lax.dynamic_slice_in_dim(mixed_qkv, first_row, block_images, 0).reshape(
            block_images, row_count, 3, head_count, HEAD_DIM
        )
        queries = split_heads[:, :, 0]
        keys_all = split_heads[:, :, 1]
        values = split_heads[:, :, 2]
        key_mask = lax.dynamic_slice_in_dim(mask_all, first_row, block_images, 0)
        logsum = lax.dynamic_slice_in_dim(logsums, first_row, block_images, 0)
        grad_out = lax.dynamic_slice_in_dim(grad_context, first_row, block_images, 0).reshape(
            block_images, row_count, head_count, HEAD_DIM
        )
        scores = (
            jnp.einsum("bqhe,bkhe->bhqk", queries, keys_all, preferred_element_type=jnp.float32)
            * scale
        )
        scores = jnp.where(key_mask[:, None, None, :], scores, -1e30)
        attend_weights = jnp.exp(scores - logsum[..., None])
        grad_weights = jnp.einsum(
            "bqhe,bkhe->bhqk", grad_out, values, preferred_element_type=jnp.float32
        )
        row_inner = jnp.sum(attend_weights * grad_weights, axis=-1, keepdims=True)
        grad_scores = (attend_weights * (grad_weights - row_inner)).astype(jnp.bfloat16)
        grad_query = (
            jnp.einsum("bhqk,bkhe->bqhe", grad_scores, keys_all, preferred_element_type=jnp.float32)
            * scale
        )
        grad_key = (
            jnp.einsum("bhqk,bqhe->bkhe", grad_scores, queries, preferred_element_type=jnp.float32)
            * scale
        )
        grad_value = jnp.einsum(
            "bhqk,bqhe->bkhe",
            attend_weights.astype(jnp.bfloat16),
            grad_out,
            preferred_element_type=jnp.float32,
        )
        stacked = jnp.stack([grad_query, grad_key, grad_value], axis=2).astype(jnp.bfloat16)
        return stacked.reshape(block_images, row_count, 3, lane_width)

    grad_mixed = lax.map(one_block, jnp.arange(group_size // block_images, dtype=jnp.int32))
    return grad_mixed.reshape(group_size, row_count, 3, lane_width)


def expand_units(group_two, w_expand, block_images):
    group_size, row_count, feature_count = group_two.shape

    def one_block(block_index):
        block_in = lax.dynamic_slice_in_dim(group_two, block_index * block_images, block_images, 0)
        upward = jnp.einsum("brd,df->brf", block_in, w_expand, preferred_element_type=jnp.float32)
        return jax.nn.gelu(upward, approximate=False).astype(jnp.bfloat16)

    act_units = lax.map(one_block, jnp.arange(group_size // block_images, dtype=jnp.int32))
    return act_units.reshape(group_size, row_count, w_expand.shape[1])


def units_back(grad_group, group_two, w_expand, w_reduce, block_images):
    group_size, row_count, feature_count = group_two.shape

    def one_block(block_index):
        first_row = block_index * block_images
        grad_in = lax.dynamic_slice_in_dim(grad_group, first_row, block_images, 0)
        norm_in = lax.dynamic_slice_in_dim(group_two, first_row, block_images, 0)
        back_units = jnp.einsum(
            "brd,fd->brf", grad_in, w_reduce, preferred_element_type=jnp.float32
        )
        upward = jnp.einsum("brd,df->brf", norm_in, w_expand, preferred_element_type=jnp.float32)
        return (back_units * gelu_slope(upward)).astype(jnp.bfloat16)

    grad_units = lax.map(one_block, jnp.arange(group_size // block_images, dtype=jnp.int32))
    return grad_units.reshape(group_size, row_count, w_expand.shape[1])


def rows_term(source, weight, form):
    return jnp.einsum(form, source, weight, preferred_element_type=jnp.float32)


def body(
    patches,
    lengths,
    tasks,
    prompt_master,
    first_moment,
    second_moment,
    gain_one,
    gain_two,
    w_qkv,
    w_out,
    w_up,
    w_down,
    cotangent,
):
    held_count, patch_count, feature_count = patches.shape
    row_count = cotangent.shape[1]
    lead_count = row_count - patch_count
    task_count = prompt_master.shape[0]
    prompt_table = lax.all_gather(
        prompt_master.astype(jnp.bfloat16), ("dp", "mp"), axis=1, tiled=True
    )
    chosen = tasks == jnp.arange(task_count, dtype=jnp.int32)[None, :]
    lead_part = jnp.dot(
        chosen.astype(jnp.bfloat16), prompt_table, preferred_element_type=jnp.float32
    )
    residual = jnp.concatenate(
        [lead_part.reshape(held_count, lead_count, feature_count), patches.astype(jnp.float32)],
        axis=1,
    )
    row_limit = lengths + lead_count
    w_mix, w_expand, w_reduce, w_rows = (
        lax.all_gather(w_qkv, "dp", axis=0, tiled=True),
        lax.all_gather(w_up, "dp", axis=0, tiled=True),
        lax.all_gather(w_down, "dp", axis=1, tiled=True),
        lax.all_gather(w_out, "dp", axis=1, tiled=True),
    )
    normed = layer_norm(residual, gain_one).astype(jnp.bfloat16)
    mp_rank = lax.axis_index("mp")
    group_normed, group_bound = (
        lax.all_gather(normed, "mp", axis=0, tiled=True),
        lax.all_gather(row_limit.astype(jnp.bfloat16), "mp", axis=0, tiled=True),
    )
    group_limit = group_bound.astype(jnp.int32)
    mixed_qkv, context, logsums = attend_forward(group_normed, group_limit, w_mix, held_count)
    attn_out = lax.psum_scatter(
        rows_term(context, w_rows, "brc,cd->brd"), "mp", scatter_dimension=0, tiled=True
    )
    residual_two = residual + attn_out
    normed_two = layer_norm(residual_two, gain_two).astype(jnp.bfloat16)
    group_two = lax.all_gather(normed_two, "mp", axis=0, tiled=True)
    act_units = expand_units(group_two, w_expand, held_count)
    mlp_out = lax.psum_scatter(
        rows_term(act_units, w_reduce, "brf,fd->brd").astype(jnp.bfloat16),
        "mp",
        scatter_dimension=0,
        tiled=True,
    ).astype(jnp.float32)
    block_sum = residual_two + mlp_out
    live_rows = (jnp.arange(row_count, dtype=jnp.int32)[None, :] < row_limit[:, None]).astype(
        jnp.float32
    )[:, :, None]
    square_sums = jnp.stack(
        [
            jnp.sum(block_sum * block_sum * live_rows),
            jnp.sum(attn_out * attn_out * live_rows),
            jnp.sum(mlp_out * mlp_out * live_rows),
        ]
    )
    live_count = jnp.sum(row_limit).astype(jnp.float32)
    w_mix, w_expand, w_reduce, w_rows = (
        lax.all_gather(w_qkv, "dp", axis=0, tiled=True),
        lax.all_gather(w_up, "dp", axis=0, tiled=True),
        lax.all_gather(w_down, "dp", axis=1, tiled=True),
        lax.all_gather(w_out, "dp", axis=1, tiled=True),
    )
    grad_held = lax.dynamic_slice_in_dim(cotangent, mp_rank * held_count, held_count, 0)
    grad_units = units_back(cotangent, group_two, w_expand, w_reduce, held_count)
    grad_normed_two = lax.psum_scatter(
        rows_term(grad_units, w_expand, "brf,df->brd"), "mp", scatter_dimension=0, tiled=True
    )
    grad_two = grad_held.astype(jnp.float32) + whole_norm_back(residual_two, gain_two, grad_normed_two)
    grad_low = grad_two.astype(jnp.bfloat16)
    grad_context = jnp.einsum(
        "brd,cd->brc",
        lax.all_gather(grad_low, "mp", axis=0, tiled=True),
        w_rows,
        preferred_element_type=jnp.float32,
    ).astype(jnp.bfloat16)
    grad_mixed = attend_back(mixed_qkv, logsums, group_limit, grad_context, held_count)
    grad_normed = lax.psum_scatter(
        rows_term(grad_mixed, w_mix, "brce,dce->brd").astype(jnp.bfloat16),
        "mp",
        scatter_dimension=0,
        tiled=True,
    ).astype(jnp.float32)
    grad_residual = grad_two + whole_norm_back(residual, gain_one, grad_normed)
    patch_grad = grad_residual[:, lead_count:].astype(jnp.bfloat16)
    lead_grad = grad_residual[:, :lead_count].reshape(held_count, lead_count * feature_count)
    task_term = jnp.dot(
        chosen.astype(jnp.float32).T,
        lead_grad,
        precision=lax.Precision.HIGHEST,
        preferred_element_type=jnp.float32,
    )
    task_grad = lax.psum_scatter(task_term, ("dp", "mp"), scatter_dimension=1, tiled=True)
    square = jnp.sum(task_grad * task_grad)
    square, square_sums, live_count = lax.psum((square, square_sums, live_count), ("dp", "mp"))
    grad_norm = jnp.sqrt(square)
    prompt_grad = task_grad * (clip_level / jnp.maximum(grad_norm, clip_level))
    new_first = beta_one * first_moment + (1.0 - beta_one) * prompt_grad
    new_second = beta_two * second_moment + (1.0 - beta_two) * prompt_grad * prompt_grad
    step_size = (
        new_first
        / (1.0 - beta_one**STEP)
        / (jnp.sqrt(new_second / (1.0 - beta_two**STEP)) + adam_eps)
    )
    new_master = prompt_master - learn_rate * (step_size + decay_rate * prompt_master)
    rms_stats = jnp.sqrt(square_sums / (live_count * feature_count))
    return (
        block_sum.astype(jnp.bfloat16),
        patch_grad,
        prompt_grad,
        grad_norm,
        new_first,
        new_second,
        new_master,
        new_master.astype(jnp.bfloat16),
        rms_stats,
    )


def solution(mesh):
    small = mesh.shape["dp"] == 8 and mesh.shape["mp"] == 4
    return jax.shard_map(
        fast_body if small else body,
        mesh=mesh,
        in_specs=(
            P(("dp", "mp"), None, None),
            P(("dp", "mp")),
            P(("dp", "mp"), None),
            P(None, ("dp", "mp")),
            P(None, ("dp", "mp")),
            P(None, ("dp", "mp")),
            P(),
            P(),
            P("dp", None, "mp"),
            P("mp", "dp"),
            P("dp", "mp"),
            P("mp", "dp"),
            P("dp", None, None),
        ),
        out_specs=(
            P(("dp", "mp"), None, None),
            P(("dp", "mp"), None, None),
            P(None, ("dp", "mp")),
            P(),
            P(None, ("dp", "mp")),
            P(None, ("dp", "mp")),
            P(None, ("dp", "mp")),
            P(None, ("dp", "mp")),
            P(),
        ),
        check_vma=False,
    )
```

```python
import functools
import math

import jax
import jax.numpy as jnp
from jax import lax
from jax.experimental import pallas as pl
from jax.experimental.pallas import tpu as pltpu
from jax.sharding import PartitionSpec as P

HEAD_DIM = 64
STEP = 10
MESH = pl.DeviceIdType.MESH
F32 = jnp.float32
BF16 = jnp.bfloat16

eps_norm = 1e-06
clip_level = 1.0
beta_one = 0.9
beta_two = 0.999
learn_rate = 3.0
decay_rate = 0.05
adam_eps = 1e-08

D = 768
ROWS = 256
LEAD = 50
PATCH = 206
IMGS = 2
TASKS = 8
PART = 1200
PADP = 1280
NDEV = 32
DOWNS = (384, 384)
UPS = (384, 384)
SPLITS = ((16, 48, 80, 96), (32, 32, 64, 96), (16, 48, 64, 96), (32, 48, 48, 96), (32, 48, 80, 96))
ORDER = (
    0, 28, 112, 84, 56, 4, 16, 32, 37, 1000, 44, 13, 121, 41, 45, 38, 14, 17, 18, 60,
    20, 72, 42, 48, 122, 49, 65, 39, 15, 19, 93, 116, 21, 46, 69, 22, 23, 43, 140, 47,
    66, 88, 128, 76, 27, 1001, 94, 100, 125, 73, 50, 123, 1002, 70, 51, 74, 129, 149, 132, 55,
    1003, 67, 97, 1004, 1005, 144, 156, 104, 1006, 126, 71, 77, 75, 1007, 78, 98, 130, 1008, 102, 150,
    153, 1009, 79, 95, 133, 160, 127, 131, 101, 1010, 134, 83, 1011, 151, 1013, 99, 103, 154, 157, 135,
    1012, 158, 1014, 1017, 105, 139, 106, 1018, 107, 155, 159, 1019, 161, 1020, 111, 162, 1015, 163, 1016, 1021,
    167, 1022, 1023, 1024,
)


def run_if(cond, f):
    if cond is None:
        f()
    else:
        pl.when(cond())(f)


class Net:
    def __init__(self, send_sem, recv_sem):
        self.send_sem, self.recv_sem = send_sem, recv_sem
        self.sends = self.recvs = 0
        dp, mp = lax.axis_index("dp"), lax.axis_index("mp")
        z, x, y, c = dp // 2, dp % 2, mp // 2, mp % 2
        self.z, self.x, self.y, self.c = z, x, y, c
        self.dp, self.mp = dp, mp
        self.peer = {
            "x": (2 * z + 1 - x, mp),
            "y": (dp, (1 - y) * 2 + c),
            "c": (dp, 2 * y + 1 - c),
            "u": (jnp.minimum(2 * z + 2 + x, 6 + x), mp),
            "d": (jnp.maximum(2 * z - 2 + x, x), mp),
        }

    def send(self, way, view, sem, landed):
        pltpu.make_async_remote_copy(
            src_ref=view,
            dst_ref=view,
            send_sem=self.send_sem.at[sem],
            recv_sem=self.recv_sem.at[landed],
            device_id=self.peer[way],
            device_id_type=MESH,
        ).start()

    def recv(self, view, landed):
        pltpu.make_async_copy(view, view, self.recv_sem.at[landed]).wait()

    def wait_sent(self, view, sem):
        pltpu.make_async_copy(view, view, self.send_sem.at[sem]).wait()


def gather_events(net, G, W, split):
    z, x, y, c = net.z, net.x, net.y, net.c
    r1, r2, r3, rows = split
    some = 4 if r3 > r1 else 0
    f_sem = net.recvs
    zs_sem, zp_sem, m_sem = f_sem + 1, f_sem + 1 + some, f_sem + 5 + some
    l_sem, c_sem = f_sem + 5 + 2 * some, f_sem + 9 + 2 * some
    net.recvs = c_sem + 1
    start_sent, single_sent, pair_sent, middle_sent, last_sent, core_sent = range(net.sends, net.sends + 6)
    net.sends += 6
    every = slice(None)
    ends = r1 + rows - r3

    def V(yy, d, first, last, other=False):
        core = (1 - c) if other else c
        cols = pl.ds(pl.multiple_of(core * W, 128), W)
        return G.at[:, yy, d, pl.ds(first, last - first), cols]

    def two(p):
        return pl.ds(2 * p, 2)

    def one(p):
        return 2 * p + x

    def send(way, yy, d, first, last, sem, landed):
        if last > first:
            net.send(way, V(yy, d, first, last), sem, landed)

    def sides(k, f):
        if k == 0:
            f(z, None, None)
        else:
            pl.when(z >= k)(lambda: f(z - k, "u", z < 3))
            pl.when(z + k <= 3)(lambda: f(z + k, "d", z > 0))

    def middle(p):
        send("x", y, one(p), r1, r2, middle_sent, m_sem + p)
        send("y", y, one(p), r2, r3, middle_sent, m_sem + p)

    def start():
        send("x", y, one(z), 0, r1, start_sent, f_sem)
        send("y", y, one(z), r3, rows, start_sent, f_sem)
        if r3 > r1:
            pl.when(z < 3)(lambda: send("u", y, one(z), r1, r3, single_sent, zs_sem + z))
            pl.when(z > 0)(lambda: send("d", y, one(z), r1, r3, single_sent, zs_sem + z))
            middle(z)

    def pair(way, p):
        send(way, y, two(p), 0, r1, pair_sent, zp_sem + p)
        send(way, every, one(p), r3, rows, pair_sent, zp_sem + p)

    def first_hop():
        net.recv(V(y, one(z), 0, ends), f_sem)
        pl.when(z < 3)(lambda: pair("u", z))
        pl.when(z > 0)(lambda: pair("d", z))

    def single_hop(k):
        def hop(p, way, more):
            net.recv(V(y, one(p), r1, r3), zs_sem + p)
            if k < 3:
                pl.when(more)(lambda: send(way, y, one(p), r1, r3, single_sent, zs_sem + p))
            middle(p)

        sides(k, hop)

    def pair_hop(k):
        def hop(p, way, more):
            net.recv(V(y, two(p), 0, ends), zp_sem + p)
            if k < 3:
                pl.when(more)(lambda: pair(way, p))

        sides(k, hop)

    def last_hop(k):
        def hop(p, way, more):
            if r3 > r1:
                net.recv(V(y, one(p), r1, r3), m_sem + p)
            send("y", y, two(p), 0, r2, last_sent, l_sem + p)
            send("x", every, one(p), r2, rows, last_sent, l_sem + p)

        sides(k, hop)

    def to_core(k):
        def hop(p, way, more):
            net.recv(V(y, two(p), 0, rows), l_sem + p)
            send("c", every, two(p), 0, rows, core_sent, c_sem)

        sides(k, hop)

    def from_core(k):
        if k == 3:
            net.recv(V(every, every, 0, rows, other=True), c_sem)

    def finish():
        net.wait_sent(V(y, one(z), 0, ends), start_sent)
        net.wait_sent(V(y, every, 0, rows), last_sent)
        net.wait_sent(V(every, every, 0, rows), core_sent)
        if r3 > r1:
            net.wait_sent(V(y, pl.ds(0, 4), r1, r3), middle_sent)

        def along(count):
            if r3 > r1:
                net.wait_sent(V(y, pl.ds(0, count), r1, r3), single_sent)
            total = 2 * ends * count
            yy, blocks = min(
                (yy, n) for yy in (1, 2) for n in range(1, 9) if total % (yy * n * 16) == 0 and total // (yy * n) <= rows
            )
            net.wait_sent(V(y if yy == 1 else every, pl.ds(0, blocks), 0, total // (yy * blocks)), pair_sent)

        inner = jnp.logical_and(z > 0, z < 3)
        pl.when(inner)(lambda: along(5))
        pl.when(jnp.logical_not(inner))(lambda: along(1))

    kinds = (start, first_hop, single_hop, pair_hop, last_hop, to_core, from_core)
    return [f if i < 2 else functools.partial(f, k) for i, f in enumerate(kinds) for k in range(4)], finish


def nn(a, b):
    return lax.dot_general(a, b, (((1,), (0,)), ((), ())), preferred_element_type=F32)


def nt(a, b):
    return lax.dot_general(a, b, (((1,), (1,)), ((), ())), preferred_element_type=F32)


def tn(a, b):
    return lax.dot_general(a, b, (((0,), (0,)), ((), ())), preferred_element_type=F32)


def norm_parts(v):
    centre = jnp.mean(v, axis=-1, keepdims=True)
    shifted = v - centre
    spread = jnp.mean(shifted * shifted, axis=-1, keepdims=True)
    scaled = lax.rsqrt(spread + eps_norm)
    return shifted * scaled, scaled


def norm_back(normal, scaled, gain, upstream):
    weighted = upstream * gain
    return scaled * (
        weighted
        - jnp.mean(weighted, axis=-1, keepdims=True)
        - normal * jnp.mean(weighted * normal, axis=-1, keepdims=True)
    )


def keep(lanes, low, high):
    return jnp.where(lanes, low, high)


def layer_kernel(
    patches, lengths, tasks, master, gain_one, gain_two, qkv_in, out_in, u_in, d_in, cot_hbm,
    out_block, out_patch, out_task, out_stats,
    GP, GA, GDS, GUS, LOC, SEL, RES, N1, QKV, PT, CTX, RES2, N2, NRM1, NRM2, SC1, SC2, COT, BACK, ACT, GU, MACC, GACC, G2, G2B, DM, DC, LEADR,
    PAIR, PIN, SEND, RECV, ONEHOT, SREC, STSUM, QIN, OIN, MIN, GIN, own_sem, local_sem, send_sem, recv_sem, all_sem,
):
    net = Net(send_sem, recv_sem)
    z, x, y, c, dp, mp = net.z, net.x, net.y, net.c, net.dp, net.mp
    device = dp * 4 + mp

    barrier = pltpu.get_barrier_semaphore()
    for way, cond in (("x", None), ("y", None), ("c", None), ("u", lambda: z < 3), ("d", lambda: z > 0)):
        run_if(
            cond,
            lambda way=way: pl.semaphore_signal(
                barrier, inc=1, device_id=net.peer[way], device_id_type=MESH
            ),
        )

    def own_cols(w):
        return pl.ds(pl.multiple_of(c * w, 128), w)

    cot_copy = pltpu.make_async_copy(cot_hbm.at[pl.ds(mp * IMGS, IMGS)], COT, local_sem.at[0])
    copies = []
    for refs, widths, weight_in in ((GDS, DOWNS, d_in), (GUS, UPS, u_in)):
        first = 0
        for ref, w in zip(refs, widths):
            copies.append(
                pltpu.make_async_copy(
                    weight_in.at[:, pl.ds(first, w)], ref.at[0, y, dp, :, own_cols(w)], own_sem.at[len(copies)]
                )
            )
            first += w
    for copy in copies:
        copy.start()
    patch_copy = pltpu.make_async_copy(patches, PIN, local_sem.at[1])
    small = [
        pltpu.make_async_copy(src, dst, own_sem.at[len(copies) + i])
        for i, (src, dst) in enumerate(
            ((qkv_in, QIN), (out_in, OIN), (master, MIN), (gain_one, GIN.at[0]), (gain_two, GIN.at[1]))
        )
    ]
    for copy in small:
        copy.start()
    patch_copy.start()
    cot_copy.start()
    for copy in small:
        copy.wait()

    qkv = [QIN[i].astype(F32) for i in range(3)]
    outs = OIN[...].astype(F32).T
    low = lax.broadcasted_iota(jnp.int32, (96, 128), 1) < HEAD_DIM

    def tail(v, high):
        v = jnp.concatenate([v[:, 128:192], v[:, 128:192]], axis=1)
        return v

    tiles = [qkv[0][:, 0:128], qkv[1][:, 0:128], qkv[2][:, 0:128]]
    tiles.append(jnp.where(low, tail(qkv[0], 0), tail(qkv[2], 1)))
    tiles.append(jnp.where(low, tail(qkv[1], 0), tail(outs, 1)))
    tiles.append(outs[:, 0:128])
    GA[0, pl.ds(y, 1), pl.ds(dp, 1), :, own_cols(D)] = (
        jnp.concatenate(tiles, axis=1).astype(BF16)[None, None]
    )

    LOC[:, 0:PART] = MIN[...]
    lane = lax.broadcasted_iota(jnp.int32, (TASKS, PADP - PART), 1)
    LOC[:, PART:PADP] = jnp.where(
        lane == 0, tasks[0, 0].astype(F32), jnp.where(lane == 1, tasks[0, 1].astype(F32), 0.0)
    )
    half = PADP // 2
    GP[0, pl.ds(y, 1), pl.ds(dp, 1), :, own_cols(half)] = (
        jnp.concatenate([LOC[:, 0:half], LOC[:, half:PADP]], axis=0).astype(BF16)[None, None]
    )
    for copy in copies:
        copy.wait()
    inner = jnp.logical_and(z > 0, z < 3)
    run_if(lambda: inner, lambda: pl.semaphore_wait(barrier, 5))
    run_if(lambda: jnp.logical_not(inner), lambda: pl.semaphore_wait(barrier, 4))

    gathers = [gather_events(net, GP, half, (16, 16, 16, 16))]
    for ref, w, split in zip((GA, *GDS, *GUS), (D, *DOWNS, *UPS), SPLITS):
        gathers.append(gather_events(net, ref, w, split))

    g1 = GIN[0].reshape(1, D)
    g2 = GIN[1].reshape(1, D)
    limits = [lengths[b] + LEAD for b in range(IMGS)]
    live = [
        (lax.broadcasted_iota(jnp.int32, (ROWS, 1), 0) < limits[b]).astype(F32) for b in range(IMGS)
    ]

    def place_rows():
        patch_copy.wait()
        cot_copy.wait()
        for b in range(IMGS):
            RES[b, LEAD:ROWS, :] = PIN[:, b, :].astype(F32)

    task_rows = lax.broadcasted_iota(jnp.int32, (TASKS, 1), 0)

    def pick(d, _):
        dd, mm = d // 4, d % 4
        raw = GP[0, mm // 2, dd, :, pl.ds(pl.multiple_of((mm % 2) * half, 128), half)].astype(F32)
        low, high = raw[0:8], raw[8:16]
        rep, j = d // 16, d % 16
        for b in range(IMGS):
            hot = (task_rows == tasks[0, b]).astype(F32)
            row = 2 * rep + b
            SEL[j, pl.ds(row, 1), 0:half] = jnp.sum(low * hot, axis=0, keepdims=True)
            SEL[j, pl.ds(row, 1), half:PADP] = jnp.sum(high * hot, axis=0, keepdims=True)
        base = PART - half
        for b in range(IMGS):
            which = high[0:1, base + b : base + b + 1]
            ONEHOT[d, b] = (
                lax.broadcasted_iota(jnp.int32, (TASKS, 128), 0).astype(F32) == which
            ).astype(F32)
        return 0

    def place_prompts():
        lax.fori_loop(0, NDEV, pick, 0)
        wide = lax.broadcasted_iota(jnp.int32, (4, D), 1)
        for r in range(25):
            j, off = (D * r) // PART, (D * r) % PART
            first = min(D, PART - off)
            low = SEL[j, 0:4, :]
            seg = (pltpu.roll(low, PADP - off, 1) if off else low)[:, 0:D]
            if first < D:
                seg = jnp.where(wide < first, seg, pltpu.roll(SEL[j + 1, 0:4, :], first, 1)[:, 0:D])
            for rep in range(2):
                for b in range(IMGS):
                    RES[b, 25 * rep + r : 25 * rep + r + 1, :] = seg[2 * rep + b : 2 * rep + b + 1]

    def norm_one():
        for b in range(IMGS):
            normal, SC1[b] = norm_parts(RES[b])
            NRM1[b] = normal
            N1[b] = (normal * g1).astype(BF16)

    def weight(ref, core, first, width, span):
        cols = pl.ds(pl.multiple_of(core * span + first, 128), width)
        return ref[:, :, cols].reshape(D, width)

    left = lax.broadcasted_iota(jnp.int32, (ROWS, 128), 1) < HEAD_DIM
    scale = 1.0 / math.sqrt(HEAD_DIM)
    wide = lax.broadcasted_iota(jnp.int32, (1, 640), 1)
    q_scale = jnp.where((wide < 128) | ((wide >= 384) & (wide < 448)), scale, 1.0)

    def project(m):
        w = weight(GA.at[0, m // 2], m % 2, 0, 640, D)
        mixed = nn(N1[...].reshape(IMGS * ROWS, D), w) * q_scale
        QKV[m] = mixed.astype(BF16).reshape(IMGS, ROWS, 640)

    key_rows = lax.broadcasted_iota(jnp.int32, (ROWS, ROWS), 0)
    zero = jnp.zeros((), BF16)

    def attend(t):
        b, m = t // 4, t % 4
        tile = lambda i: QKV[m, b, :, 128 * i : 128 * i + 128]
        q01, k01, v01, q2v2, k2 = (tile(i) for i in range(5))
        mask = key_rows < (lengths[b] + LEAD)

        def soft(keys, queries):
            s = jnp.where(mask, nt(keys, queries), -1e30)
            e = jnp.exp(s - jnp.max(s, axis=0, keepdims=True))
            return (e * (1.0 / jnp.sum(e, axis=0, keepdims=True))).astype(BF16)

        p0 = soft(k01, keep(left, q01, zero))
        p1 = soft(k01, keep(left, zero, q01))
        p2 = soft(k2, keep(left, q2v2, zero))
        PT[t, 0], PT[t, 1], PT[t, 2] = p0, p1, p2
        CTX[b, :, m * 256 : m * 256 + 128] = keep(left, 0.0, tn(p2, q2v2)).astype(BF16)
        CTX[b, :, m * 256 + 128 : m * 256 + 256] = keep(
            left, tn(p0, v01), tn(p1, v01)
        ).astype(BF16)

    def attend_two(t):
        attend(2 * t)
        attend(2 * t + 1)

    sums = [jnp.zeros((1, 1), F32) for _ in range(3)]

    def total(v):
        return jnp.sum(jnp.sum(v, axis=0, keepdims=True), axis=1, keepdims=True)

    def project_out(b):
        attn = jnp.zeros((ROWS, D), F32)
        for m in range(4):
            attn += nt(CTX[b, :, 256 * m : 256 * m + 256], weight(GA.at[0, m // 2], m % 2, 512, 256, D))
        sums[1] += total(attn * attn * live[b])
        res2 = RES[b] + attn
        RES2[b] = res2
        normal, SC2[b] = norm_parts(res2)
        NRM2[b] = normal
        N2[b] = (normal * g2).astype(BF16)

    def back_units(i, yy):
        w, first = DOWNS[i], sum(DOWNS[:i])
        cot = COT[...].reshape(IMGS * ROWS, D)
        for core in range(2):
            back = nn(cot, weight(GDS[i].at[0, yy], core, 0, w, w))
            BACK[yy, :, core * D + first : core * D + first + w] = back.astype(BF16)

    def up_units(i, core):
        w, first = UPS[i], sum(UPS[:i])
        rows2 = N2[...].reshape(IMGS * ROWS, D)
        here = pl.ds(pl.multiple_of(core * w, 128), w)
        for yy in range(2):
            up = nn(rows2, weight(GUS[i].at[0, yy], core, 0, w, w))
            back = BACK[yy, :, pl.ds(pl.multiple_of(core * D + first, 128), w)].astype(F32)
            cumul = 0.5 * (1.0 + lax.erf(up * 0.7071067811865476))
            density = jnp.exp(-0.5 * up * up) * 0.3989422804014327
            ACT[yy, :, here] = (up * cumul).astype(BF16)
            GU[yy, :, here] = (back * (cumul + up * density)).astype(BF16)

    def add_units(i, yy):
        w, first = UPS[i], sum(UPS[:i])
        d = max(d for d in range(len(DOWNS)) if sum(DOWNS[:d]) <= first)
        inside = first - sum(DOWNS[:d])
        if w == DOWNS[d]:
            mlp = nt(ACT[yy, :, 0 : 2 * w], weight(GDS[d].at[0, yy], 0, 0, 2 * w, w))
        else:
            mlp = sum(
                nt(ACT[yy, :, w * core : w * (core + 1)], weight(GDS[d].at[0, yy], core, inside, w, DOWNS[d]))
                for core in range(2)
            )
        grad = nt(GU[yy, :, 0 : 2 * w], weight(GUS[i].at[0, yy], 0, 0, 2 * w, w))
        mlp, grad = mlp.reshape(IMGS, ROWS, D), grad.reshape(IMGS, ROWS, D)
        if i == 0 and yy == 0:
            MACC[...] = mlp
            GACC[...] = grad
        else:
            MACC[...] += mlp
            GACC[...] += grad

    steps = [place_rows, place_prompts, norm_one]
    steps += [functools.partial(project, m) for m in range(4)]
    steps += [functools.partial(attend_two, t) for t in range(4)]
    steps += [functools.partial(project_out, b) for b in range(IMGS)]
    steps += [functools.partial(back_units, i, yy) for i in range(len(DOWNS)) for yy in range(2)]
    for i in range(len(UPS)):
        steps += [functools.partial(up_units, i, c), functools.partial(up_units, i, 1 - c)]
        steps += [functools.partial(add_units, i, yy) for yy in range(2)]
    for item in ORDER:
        if item < 1000:
            gathers[item // 28][0][item % 28]()
        else:
            steps[item - 1000]()

    for b in range(IMGS):
        g = COT[b].astype(F32) + norm_back(NRM2[b], SC2[b], g2, GACC[b])
        G2[b] = g
        G2B[b] = g.astype(BF16)

    def context_back(m, _):
        cols = pl.ds(pl.multiple_of((m % 2) * D + 512, 128), 256)
        w = GA[0, m // 2, :, :, cols].reshape(D, 256)
        DC[m] = nn(G2B[...].reshape(IMGS * ROWS, D), w).astype(BF16).reshape(IMGS, ROWS, 256)
        return 0

    lax.fori_loop(0, 4, context_back, 0, unroll=4)

    def attend_back(b):
        tiles, grad_probs, grad_scores = [], [], []
        for m in range(4):
            tiles.append(
                [QKV[m, b, :, 128 * i : 128 * i + 128] for i in range(5)]
                + [DC[m, b, :, 0:128], DC[m, b, :, 128:256]]
            )
            q01, k01, v01, q2v2, k2, c2, c01 = tiles[m]
            grad_probs.append(
                [nt(keep(left, v01, zero), c01), nt(keep(left, zero, v01), c01), nt(keep(left, zero, q2v2), c2)]
            )
        for m in range(4):
            out = []
            for h in range(3):
                pf, dp_ = PT[4 * b + m, h].astype(F32), grad_probs[m][h]
                inner = jnp.sum(pf * dp_, axis=0, keepdims=True)
                out.append((pf * (dp_ - inner)).astype(BF16))
            grad_scores.append(out)
        for m in range(4):
            q01, k01, v01, q2v2, k2, c2, c01 = tiles[m]
            s0, s1, s2 = grad_scores[m]
            p0, p1, p2 = (PT[4 * b + m, h] for h in range(3))
            DM[m, b, :, 0:128] = (keep(left, tn(s0, k01), tn(s1, k01)) * scale).astype(BF16)
            DM[m, b, :, 128:256] = keep(left, nn(s0, q01), nn(s1, q01)).astype(BF16)
            DM[m, b, :, 256:384] = keep(left, nn(p0, c01), nn(p1, c01)).astype(BF16)
            DM[m, b, :, 384:512] = keep(left, tn(s2, k2) * scale, nn(p2, c2)).astype(BF16)
            DM[m, b, :, 512:640] = keep(left, nn(s2, q2v2), 0.0).astype(BF16)

    def grad_rows(rows, first, last):
        count = last - first
        grad = jnp.zeros((len(rows) * count, D), F32)
        for m in range(4):
            mixed = jnp.concatenate([DM[m, b, first:last] for b in rows], axis=0)
            grad += nt(mixed, weight(GA.at[0, m // 2], m % 2, 0, 640, D))
        for i, b in enumerate(rows):
            part = grad[count * i : count * (i + 1)]
            GACC[b, first:last] = G2[b, first:last] + norm_back(NRM1[b, first:last], SC1[b, first:last], g1, part)

    def swap(k, src, dst, sems):
        to_dp, to_mp = (dp + k // 4) & 7, (mp + k) & 3
        other = to_dp * 4 + to_mp
        pltpu.make_async_remote_copy(
            src_ref=src(other),
            dst_ref=dst,
            send_sem=all_sem.at[sems],
            recv_sem=all_sem.at[sems + 1],
            device_id=(to_dp, to_mp),
            device_id_type=MESH,
        ).start()

    wide = lax.broadcasted_iota(jnp.int32, (4, PADP), 1)

    def to_owners():
        for rep in range(2):
            for b in range(IMGS):
                LEADR[:, 2 * rep + b : 2 * rep + b + 1, :] = GACC[b, 25 * rep : 25 * rep + 25, :][:, None, :]
        for q in range(16):
            r, off = (PART * q) // D, (PART * q) % D
            msg, have = None, -off
            while have < PART:
                row = LEADR[r]
                moved = pltpu.roll(row, have % D, 1) if have % D else row
                moved = jnp.concatenate([moved, moved[:, 0 : PADP - D]], axis=1)
                msg = moved if msg is None else jnp.where(wide < have, msg, moved)
                have += D
                r += 1
            msg = jnp.where(wide < PART, msg, 0.0).astype(BF16)
            for rep in range(2):
                SEND[16 * rep + q] = jnp.concatenate(
                    [msg[2 * rep + b : 2 * rep + b + 1, half * h : half * h + half] for b in range(IMGS) for h in range(2)],
                    axis=0,
                )
        for k in range(1, NDEV):
            swap(k, lambda other: SEND.at[other], RECV.at[device], 0)
        RECV[pl.ds(device, 1)] = SEND[pl.ds(device, 1)]

    def others(ref):
        return ref.at[pl.ds(0, NDEV - 1)]

    def wait_all(ref, sem):
        pltpu.make_async_copy(others(ref), others(ref), all_sem.at[sem]).wait()

    some = 64
    for b in range(IMGS):
        attend_back(b)
    grad_rows((0, 1), 0, some)
    to_owners()

    grad_rows((0, 1), some, ROWS)
    for b in range(IMGS):
        mlp = MACC[b]
        block = RES2[b] + mlp
        out_block[b] = block.astype(BF16)
        sums[0] += total(block * block * live[b])
        sums[2] += total(mlp * mlp * live[b])

    wait_all(RECV, 1)

    def add(s, acc):
        rows = RECV[s].astype(F32)
        low, high = acc
        for b in range(IMGS):
            hot = jnp.concatenate([ONEHOT[s, b]] * (half // 128), axis=1)
            low, high = low + hot * rows[2 * b : 2 * b + 1], high + hot * rows[2 * b + 1 : 2 * b + 2]
        return low, high

    acc = (jnp.zeros((TASKS, half), F32), jnp.zeros((TASKS, half), F32))
    acc = lax.fori_loop(0, NDEV, add, acc, unroll=8)
    square = total(acc[0] * acc[0]) + total(acc[1] * acc[1])
    lane = lax.broadcasted_iota(jnp.int32, (1, 128), 1)
    count = (limits[0] + limits[1]).astype(F32)
    stats = jnp.zeros((1, 128), F32)
    for i, v in enumerate((square, sums[0], sums[1], sums[2], count)):
        stats = jnp.where(lane == i, v, stats)
    STSUM[...] = stats
    SREC[pl.ds(device, 1)] = stats[None]
    for k in range(1, NDEV):
        swap(k, lambda other: STSUM, SREC.at[device], 2)

    out_task[...] = jnp.concatenate(acc, axis=1)[:, 0:PART]
    for b in range(IMGS):
        PAIR[:, b : b + 1, :] = GACC[b, LEAD:ROWS, :][:, None, :]
    out_patch[...] = PAIR[...].astype(BF16)
    wait_all(RECV, 0)
    for gather in gathers:
        gather[1]()
    wait_all(SREC, 3)
    out_stats[...] = jnp.sum(SREC[...], axis=0)
    wait_all(SREC, 2)


def update_kernel(
    task_grad, stats, master, first_moment, second_moment, block_in, patch_in,
    out_grad, out_first, out_second, out_master, out_copy, out_norm, out_rms, block_out, patch_out, sem,
):
    copies = [
        pltpu.make_async_copy(block_in, block_out, sem.at[0]),
        pltpu.make_async_copy(patch_in, patch_out, sem.at[1]),
    ]
    for copy in copies:
        copy.start()
    st = stats[0:1, :]
    norm = jnp.sqrt(st[0:1, 0:1])
    grad = task_grad[...] * (clip_level / jnp.maximum(norm, clip_level))
    first = beta_one * first_moment[...] + (1.0 - beta_one) * grad
    second = beta_two * second_moment[...] + (1.0 - beta_two) * grad * grad
    step_size = (
        first / (1.0 - beta_one**STEP) / (jnp.sqrt(second / (1.0 - beta_two**STEP)) + adam_eps)
    )
    old = master[...]
    new = old - learn_rate * (step_size + decay_rate * old)
    out_grad[...] = grad
    out_first[...] = first
    out_second[...] = second
    out_master[...] = new
    out_copy[...] = new.astype(BF16)
    out_norm[0] = norm[0, 0]
    rms = jnp.sqrt(st / (st[0:1, 4:5] * D))
    for i in range(3):
        out_rms[i] = rms[0, i + 1]
    for copy in copies:
        copy.wait()


def fast_body(
    patches, lengths, tasks, prompt_master, first_moment, second_moment,
    gain_one, gain_two, w_qkv, w_out, w_up, w_down, cotangent,
):
    vmem = pl.BlockSpec(memory_space=pltpu.VMEM)
    smem = pl.BlockSpec(memory_space=pltpu.SMEM)
    anywhere = pl.BlockSpec(memory_space=pl.ANY)
    V = pltpu.VMEM
    block, patch, task, stats = pl.pallas_call(
        layer_kernel,
        out_shape=[
            V((IMGS, ROWS, D), BF16),
            V((PATCH, IMGS, D), BF16),
            V((TASKS, PART), F32),
            V((1, 128), F32),
        ],
        in_specs=[anywhere, smem, smem] + [anywhere] * 8,
        out_specs=[vmem] * 4,
        scratch_shapes=[
            V((1, 2, 8, 16, PADP), BF16),
            V((1, 2, 8, 96, 2 * D), BF16),
            [V((1, 2, 8, 96, 2 * w), BF16) for w in DOWNS],
            [V((1, 2, 8, 96, 2 * w), BF16) for w in UPS],
            V((TASKS, PADP), F32),
            V((16, 4, PADP), F32),
            V((IMGS, ROWS, D), F32),
            V((IMGS, ROWS, D), BF16),
            V((4, IMGS, ROWS, 640), BF16),
            V((8, 3, ROWS, ROWS), BF16),
            V((IMGS, ROWS, 1024), BF16),
            V((IMGS, ROWS, D), F32),
            V((IMGS, ROWS, D), BF16),
            V((IMGS, ROWS, D), F32),
            V((IMGS, ROWS, D), F32),
            V((IMGS, ROWS, 1), F32),
            V((IMGS, ROWS, 1), F32),
            V((IMGS, ROWS, D), BF16),
            V((2, IMGS * ROWS, 2 * D), BF16),
            V((2, IMGS * ROWS, 2 * max(UPS)), BF16),
            V((2, IMGS * ROWS, 2 * max(UPS)), BF16),
            V((IMGS, ROWS, D), F32),
            V((IMGS, ROWS, D), F32),
            V((IMGS, ROWS, D), F32),
            V((IMGS, ROWS, D), BF16),
            V((4, IMGS, ROWS, 640), BF16),
            V((4, IMGS, ROWS, 256), BF16),
            V((25, 4, D), F32),
            V((PATCH, IMGS, D), F32),
            V((PATCH, IMGS, D), BF16),
            V((NDEV, 2 * IMGS, PADP // 2), BF16),
            V((NDEV, 2 * IMGS, PADP // 2), BF16),
            V((NDEV, IMGS, TASKS, 128), F32),
            V((NDEV, 1, 128), F32),
            V((1, 128), F32),
            V((3, 96, 192), BF16),
            V((192, 96), BF16),
            V((TASKS, PART), F32),
            V((2, D), F32),
            pltpu.SemaphoreType.DMA((5 + len(DOWNS) + len(UPS),)),
            pltpu.SemaphoreType.DMA((2,)),
            pltpu.SemaphoreType.DMA((6 * (2 + len(DOWNS) + len(UPS)),)),
            pltpu.SemaphoreType.DMA((10 + 18 * (1 + len(DOWNS) + len(UPS)),)),
            pltpu.SemaphoreType.DMA((4,)),
        ],
        compiler_params=pltpu.CompilerParams(
            collective_id=0, has_side_effects=True, vmem_limit_bytes=58 << 20
        ),
    )(
        patches.transpose(1, 0, 2), lengths, tasks.T, prompt_master, gain_one, gain_two,
        w_qkv.transpose(1, 0, 2), w_out, w_up, w_down.T, cotangent,
    )
    state = jax.ShapeDtypeStruct((TASKS, PART), F32)

    def keep_near(v):
        return pltpu.with_memory_space_constraint(v, pltpu.VMEM)

    grad, first, second, master, copy, norm, rms, block_out, patch_out = pl.pallas_call(
        update_kernel,
        out_shape=[state] * 4
        + [
            jax.ShapeDtypeStruct((TASKS, PART), BF16),
            jax.ShapeDtypeStruct((1,), F32),
            jax.ShapeDtypeStruct((3,), F32),
            jax.ShapeDtypeStruct((IMGS, ROWS, D), BF16),
            jax.ShapeDtypeStruct((PATCH, IMGS, D), BF16),
        ],
        in_specs=[vmem] * 7,
        out_specs=[vmem] * 5 + [smem] * 2 + [anywhere] * 2,
        scratch_shapes=[pltpu.SemaphoreType.DMA((2,))],
    )(
        keep_near(task), keep_near(stats), prompt_master, first_moment, second_moment, keep_near(block), keep_near(patch),
    )
    return (
        block_out, patch_out.transpose(1, 0, 2), grad, norm.reshape(()), first, second, master, copy, rms,
    )


def layer_norm(values, gain):
    centre = jnp.mean(values, axis=-1, keepdims=True)
    shifted = values - centre
    spread = jnp.mean(shifted * shifted, axis=-1, keepdims=True)
    return shifted * lax.rsqrt(spread + eps_norm) * gain


def whole_norm_back(values, gain, upstream):
    centre = jnp.mean(values, axis=-1, keepdims=True)
    shifted = values - centre
    spread = jnp.mean(shifted * shifted, axis=-1, keepdims=True)
    scaled = lax.rsqrt(spread + eps_norm)
    normal_part = shifted * scaled
    weighted = upstream * gain
    return scaled * (
        weighted
        - jnp.mean(weighted, axis=-1, keepdims=True)
        - normal_part * jnp.mean(weighted * normal_part, axis=-1, keepdims=True)
    )


def gelu_slope(upward):
    cumul = 0.5 * (1.0 + lax.erf(upward * 0.7071067811865476))
    density = jnp.exp(-0.5 * upward * upward) * 0.3989422804014327
    return cumul + upward * density


def attend_forward(group_normed, group_limit, w_mix, block_images):
    group_size, row_count, feature_count = group_normed.shape
    lane_width = w_mix.shape[2]
    head_count = lane_width // HEAD_DIM
    scale = 1.0 / math.sqrt(HEAD_DIM)
    mask_all = jnp.arange(row_count, dtype=jnp.int32)[None, :] < group_limit[:, None]

    def one_block(block_index):
        first_row = block_index * block_images
        block_in = lax.dynamic_slice_in_dim(group_normed, first_row, block_images, 0)
        key_mask = lax.dynamic_slice_in_dim(mask_all, first_row, block_images, 0)
        mixed_qkv = jnp.einsum(
            "brd,dce->brce", block_in, w_mix, preferred_element_type=jnp.float32
        ).astype(jnp.bfloat16)
        split_heads = mixed_qkv.reshape(block_images, row_count, 3, head_count, HEAD_DIM)
        scores = (
            jnp.einsum(
                "bqhe,bkhe->bhqk",
                split_heads[:, :, 0],
                split_heads[:, :, 1],
                preferred_element_type=jnp.float32,
            )
            * scale
        )
        scores = jnp.where(key_mask[:, None, None, :], scores, -1e30)
        row_top = jnp.max(scores, axis=-1, keepdims=True)
        exponent = jnp.exp(scores - row_top)
        row_total = jnp.sum(exponent, axis=-1, keepdims=True)
        attend_weights = (exponent / row_total).astype(jnp.bfloat16)
        context = jnp.einsum(
            "bhqk,bkhe->bqhe",
            attend_weights,
            split_heads[:, :, 2],
            preferred_element_type=jnp.float32,
        )
        context = context.astype(jnp.bfloat16).reshape(block_images, row_count, lane_width)
        return (mixed_qkv, context, (row_top + jnp.log(row_total))[..., 0])

    mixed_qkv, context, logsums = lax.map(
        one_block, jnp.arange(group_size // block_images, dtype=jnp.int32)
    )
    return (
        mixed_qkv.reshape(group_size, row_count, 3, lane_width),
        context.reshape(group_size, row_count, lane_width),
        logsums.reshape(group_size, head_count, row_count),
    )


def attend_back(mixed_qkv, logsums, group_limit, grad_context, block_images):
    group_size, row_count, three_parts, lane_width = mixed_qkv.shape
    head_count = lane_width // HEAD_DIM
    scale = 1.0 / math.sqrt(HEAD_DIM)
    mask_all = jnp.arange(row_count, dtype=jnp.int32)[None, :] < group_limit[:, None]

    def one_block(block_index):
        first_row = block_index * block_images
        split_heads = lax.dynamic_slice_in_dim(mixed_qkv, first_row, block_images, 0).reshape(
            block_images, row_count, 3, head_count, HEAD_DIM
        )
        queries = split_heads[:, :, 0]
        keys_all = split_heads[:, :, 1]
        values = split_heads[:, :, 2]
        key_mask = lax.dynamic_slice_in_dim(mask_all, first_row, block_images, 0)
        logsum = lax.dynamic_slice_in_dim(logsums, first_row, block_images, 0)
        grad_out = lax.dynamic_slice_in_dim(grad_context, first_row, block_images, 0).reshape(
            block_images, row_count, head_count, HEAD_DIM
        )
        scores = (
            jnp.einsum("bqhe,bkhe->bhqk", queries, keys_all, preferred_element_type=jnp.float32)
            * scale
        )
        scores = jnp.where(key_mask[:, None, None, :], scores, -1e30)
        attend_weights = jnp.exp(scores - logsum[..., None])
        grad_weights = jnp.einsum(
            "bqhe,bkhe->bhqk", grad_out, values, preferred_element_type=jnp.float32
        )
        row_inner = jnp.sum(attend_weights * grad_weights, axis=-1, keepdims=True)
        grad_scores = (attend_weights * (grad_weights - row_inner)).astype(jnp.bfloat16)
        grad_query = (
            jnp.einsum("bhqk,bkhe->bqhe", grad_scores, keys_all, preferred_element_type=jnp.float32)
            * scale
        )
        grad_key = (
            jnp.einsum("bhqk,bqhe->bkhe", grad_scores, queries, preferred_element_type=jnp.float32)
            * scale
        )
        grad_value = jnp.einsum(
            "bhqk,bqhe->bkhe",
            attend_weights.astype(jnp.bfloat16),
            grad_out,
            preferred_element_type=jnp.float32,
        )
        stacked = jnp.stack([grad_query, grad_key, grad_value], axis=2).astype(jnp.bfloat16)
        return stacked.reshape(block_images, row_count, 3, lane_width)

    grad_mixed = lax.map(one_block, jnp.arange(group_size // block_images, dtype=jnp.int32))
    return grad_mixed.reshape(group_size, row_count, 3, lane_width)


def expand_units(group_two, w_expand, block_images):
    group_size, row_count, feature_count = group_two.shape

    def one_block(block_index):
        block_in = lax.dynamic_slice_in_dim(group_two, block_index * block_images, block_images, 0)
        upward = jnp.einsum("brd,df->brf", block_in, w_expand, preferred_element_type=jnp.float32)
        return jax.nn.gelu(upward, approximate=False).astype(jnp.bfloat16)

    act_units = lax.map(one_block, jnp.arange(group_size // block_images, dtype=jnp.int32))
    return act_units.reshape(group_size, row_count, w_expand.shape[1])


def units_back(grad_group, group_two, w_expand, w_reduce, block_images):
    group_size, row_count, feature_count = group_two.shape

    def one_block(block_index):
        first_row = block_index * block_images
        grad_in = lax.dynamic_slice_in_dim(grad_group, first_row, block_images, 0)
        norm_in = lax.dynamic_slice_in_dim(group_two, first_row, block_images, 0)
        back_units = jnp.einsum(
            "brd,fd->brf", grad_in, w_reduce, preferred_element_type=jnp.float32
        )
        upward = jnp.einsum("brd,df->brf", norm_in, w_expand, preferred_element_type=jnp.float32)
        return (back_units * gelu_slope(upward)).astype(jnp.bfloat16)

    grad_units = lax.map(one_block, jnp.arange(group_size // block_images, dtype=jnp.int32))
    return grad_units.reshape(group_size, row_count, w_expand.shape[1])


def rows_term(source, weight, form):
    return jnp.einsum(form, source, weight, preferred_element_type=jnp.float32)


def body(
    patches,
    lengths,
    tasks,
    prompt_master,
    first_moment,
    second_moment,
    gain_one,
    gain_two,
    w_qkv,
    w_out,
    w_up,
    w_down,
    cotangent,
):
    held_count, patch_count, feature_count = patches.shape
    row_count = cotangent.shape[1]
    lead_count = row_count - patch_count
    task_count = prompt_master.shape[0]
    prompt_table = lax.all_gather(
        prompt_master.astype(jnp.bfloat16), ("dp", "mp"), axis=1, tiled=True
    )
    chosen = tasks == jnp.arange(task_count, dtype=jnp.int32)[None, :]
    lead_part = jnp.dot(
        chosen.astype(jnp.bfloat16), prompt_table, preferred_element_type=jnp.float32
    )
    residual = jnp.concatenate(
        [lead_part.reshape(held_count, lead_count, feature_count), patches.astype(jnp.float32)],
        axis=1,
    )
    row_limit = lengths + lead_count
    w_mix, w_expand, w_reduce, w_rows = (
        lax.all_gather(w_qkv, "dp", axis=0, tiled=True),
        lax.all_gather(w_up, "dp", axis=0, tiled=True),
        lax.all_gather(w_down, "dp", axis=1, tiled=True),
        lax.all_gather(w_out, "dp", axis=1, tiled=True),
    )
    normed = layer_norm(residual, gain_one).astype(jnp.bfloat16)
    mp_rank = lax.axis_index("mp")
    group_normed, group_bound = (
        lax.all_gather(normed, "mp", axis=0, tiled=True),
        lax.all_gather(row_limit.astype(jnp.bfloat16), "mp", axis=0, tiled=True),
    )
    group_limit = group_bound.astype(jnp.int32)
    mixed_qkv, context, logsums = attend_forward(group_normed, group_limit, w_mix, held_count)
    attn_out = lax.psum_scatter(
        rows_term(context, w_rows, "brc,cd->brd"), "mp", scatter_dimension=0, tiled=True
    )
    residual_two = residual + attn_out
    normed_two = layer_norm(residual_two, gain_two).astype(jnp.bfloat16)
    group_two = lax.all_gather(normed_two, "mp", axis=0, tiled=True)
    act_units = expand_units(group_two, w_expand, held_count)
    mlp_out = lax.psum_scatter(
        rows_term(act_units, w_reduce, "brf,fd->brd").astype(jnp.bfloat16),
        "mp",
        scatter_dimension=0,
        tiled=True,
    ).astype(jnp.float32)
    block_sum = residual_two + mlp_out
    live_rows = (jnp.arange(row_count, dtype=jnp.int32)[None, :] < row_limit[:, None]).astype(
        jnp.float32
    )[:, :, None]
    square_sums = jnp.stack(
        [
            jnp.sum(block_sum * block_sum * live_rows),
            jnp.sum(attn_out * attn_out * live_rows),
            jnp.sum(mlp_out * mlp_out * live_rows),
        ]
    )
    live_count = jnp.sum(row_limit).astype(jnp.float32)
    w_mix, w_expand, w_reduce, w_rows = (
        lax.all_gather(w_qkv, "dp", axis=0, tiled=True),
        lax.all_gather(w_up, "dp", axis=0, tiled=True),
        lax.all_gather(w_down, "dp", axis=1, tiled=True),
        lax.all_gather(w_out, "dp", axis=1, tiled=True),
    )
    grad_held = lax.dynamic_slice_in_dim(cotangent, mp_rank * held_count, held_count, 0)
    grad_units = units_back(cotangent, group_two, w_expand, w_reduce, held_count)
    grad_normed_two = lax.psum_scatter(
        rows_term(grad_units, w_expand, "brf,df->brd"), "mp", scatter_dimension=0, tiled=True
    )
    grad_two = grad_held.astype(jnp.float32) + whole_norm_back(residual_two, gain_two, grad_normed_two)
    grad_low = grad_two.astype(jnp.bfloat16)
    grad_context = jnp.einsum(
        "brd,cd->brc",
        lax.all_gather(grad_low, "mp", axis=0, tiled=True),
        w_rows,
        preferred_element_type=jnp.float32,
    ).astype(jnp.bfloat16)
    grad_mixed = attend_back(mixed_qkv, logsums, group_limit, grad_context, held_count)
    grad_normed = lax.psum_scatter(
        rows_term(grad_mixed, w_mix, "brce,dce->brd").astype(jnp.bfloat16),
        "mp",
        scatter_dimension=0,
        tiled=True,
    ).astype(jnp.float32)
    grad_residual = grad_two + whole_norm_back(residual, gain_one, grad_normed)
    patch_grad = grad_residual[:, lead_count:].astype(jnp.bfloat16)
    lead_grad = grad_residual[:, :lead_count].reshape(held_count, lead_count * feature_count)
    task_term = jnp.dot(
        chosen.astype(jnp.float32).T,
        lead_grad,
        precision=lax.Precision.HIGHEST,
        preferred_element_type=jnp.float32,
    )
    task_grad = lax.psum_scatter(task_term, ("dp", "mp"), scatter_dimension=1, tiled=True)
    square = jnp.sum(task_grad * task_grad)
    square, square_sums, live_count = lax.psum((square, square_sums, live_count), ("dp", "mp"))
    grad_norm = jnp.sqrt(square)
    prompt_grad = task_grad * (clip_level / jnp.maximum(grad_norm, clip_level))
    new_first = beta_one * first_moment + (1.0 - beta_one) * prompt_grad
    new_second = beta_two * second_moment + (1.0 - beta_two) * prompt_grad * prompt_grad
    step_size = (
        new_first
        / (1.0 - beta_one**STEP)
        / (jnp.sqrt(new_second / (1.0 - beta_two**STEP)) + adam_eps)
    )
    new_master = prompt_master - learn_rate * (step_size + decay_rate * prompt_master)
    rms_stats = jnp.sqrt(square_sums / (live_count * feature_count))
    return (
        block_sum.astype(jnp.bfloat16),
        patch_grad,
        prompt_grad,
        grad_norm,
        new_first,
        new_second,
        new_master,
        new_master.astype(jnp.bfloat16),
        rms_stats,
    )


def solution(mesh):
    small = mesh.shape["dp"] == 8 and mesh.shape["mp"] == 4
    return jax.shard_map(
        fast_body if small else body,
        mesh=mesh,
        in_specs=(
            P(("dp", "mp"), None, None),
            P(("dp", "mp")),
            P(("dp", "mp"), None),
            P(None, ("dp", "mp")),
            P(None, ("dp", "mp")),
            P(None, ("dp", "mp")),
            P(),
            P(),
            P("dp", None, "mp"),
            P("mp", "dp"),
            P("dp", "mp"),
            P("mp", "dp"),
            P("dp", None, None),
        ),
        out_specs=(
            P(("dp", "mp"), None, None),
            P(("dp", "mp"), None, None),
            P(None, ("dp", "mp")),
            P(),
            P(None, ("dp", "mp")),
            P(None, ("dp", "mp")),
            P(None, ("dp", "mp")),
            P(None, ("dp", "mp")),
            P(),
        ),
        check_vma=False,
    )
```

```python
import functools
import math

import jax
import jax.numpy as jnp
from jax import lax
from jax.experimental import pallas as pl
from jax.experimental.pallas import tpu as pltpu
from jax.sharding import PartitionSpec as P

HEAD_DIM = 64
STEP = 10
MESH = pl.DeviceIdType.MESH
F32 = jnp.float32
BF16 = jnp.bfloat16

eps_norm = 1e-06
clip_level = 1.0
beta_one = 0.9
beta_two = 0.999
learn_rate = 3.0
decay_rate = 0.05
adam_eps = 1e-08

D = 768
ROWS = 256
LEAD = 50
PATCH = 206
IMGS = 2
TASKS = 8
PART = 1200
PADP = 1280
NDEV = 32
DOWNS = (512, 256)
UPS = (512, 256)
SPLITS = ((16, 48, 80, 96), (32, 48, 64, 96), (16, 48, 48, 96), (32, 48, 64, 96), (16, 32, 64, 96))
ORDER = (
    28, 56, 0, 1000, 112, 32, 84, 44, 4, 16, 37, 140, 13, 41, 17, 38, 14, 18, 48, 60,
    45, 42, 144, 121, 65, 21, 22, 39, 15, 19, 46, 156, 20, 23, 43, 47, 69, 72, 116, 149,
    49, 27, 1001, 93, 66, 50, 1002, 51, 128, 70, 160, 73, 125, 122, 76, 88, 150, 74, 55, 1003,
    1004, 1005, 67, 129, 1006, 94, 1007, 126, 71, 153, 132, 77, 123, 75, 1008, 78, 130, 1009, 97, 157,
    1010, 79, 127, 131, 1011, 1012, 95, 133, 154, 100, 151, 158, 83, 98, 102, 101, 1013, 134, 1014, 135,
    161, 1017, 99, 155, 104, 103, 159, 139, 1018, 162, 106, 1019, 105, 107, 1020, 111, 163, 1015, 1016, 1021,
    167, 1022, 1023, 1024,
)


def run_if(cond, f):
    if cond is None:
        f()
    else:
        pl.when(cond())(f)


class Net:
    def __init__(self, send_sem, recv_sem):
        self.send_sem, self.recv_sem = send_sem, recv_sem
        self.sends = self.recvs = 0
        dp, mp = lax.axis_index("dp"), lax.axis_index("mp")
        z, x, y, c = dp // 2, dp % 2, mp // 2, mp % 2
        self.z, self.x, self.y, self.c = z, x, y, c
        self.dp, self.mp = dp, mp
        self.peer = {
            "x": (2 * z + 1 - x, mp),
            "y": (dp, (1 - y) * 2 + c),
            "c": (dp, 2 * y + 1 - c),
            "u": (jnp.minimum(2 * z + 2 + x, 6 + x), mp),
            "d": (jnp.maximum(2 * z - 2 + x, x), mp),
        }

    def send(self, way, view, sem, landed):
        pltpu.make_async_remote_copy(
            src_ref=view,
            dst_ref=view,
            send_sem=self.send_sem.at[sem],
            recv_sem=self.recv_sem.at[landed],
            device_id=self.peer[way],
            device_id_type=MESH,
        ).start()

    def recv(self, view, landed):
        pltpu.make_async_copy(view, view, self.recv_sem.at[landed]).wait()

    def wait_sent(self, view, sem):
        pltpu.make_async_copy(view, view, self.send_sem.at[sem]).wait()


def gather_events(net, G, W, split):
    z, x, y, c = net.z, net.x, net.y, net.c
    r1, r2, r3, rows = split
    some = 4 if r3 > r1 else 0
    f_sem = net.recvs
    zs_sem, zp_sem, m_sem = f_sem + 1, f_sem + 1 + some, f_sem + 5 + some
    l_sem, c_sem = f_sem + 5 + 2 * some, f_sem + 9 + 2 * some
    net.recvs = c_sem + 1
    start_sent, single_sent, pair_sent, middle_sent, last_sent, core_sent = range(net.sends, net.sends + 6)
    net.sends += 6
    every = slice(None)
    ends = r1 + rows - r3

    def V(yy, d, first, last, other=False):
        core = (1 - c) if other else c
        cols = pl.ds(pl.multiple_of(core * W, 128), W)
        return G.at[:, yy, d, pl.ds(first, last - first), cols]

    def two(p):
        return pl.ds(2 * p, 2)

    def one(p):
        return 2 * p + x

    def send(way, yy, d, first, last, sem, landed):
        if last > first:
            net.send(way, V(yy, d, first, last), sem, landed)

    def sides(k, f):
        if k == 0:
            f(z, None, None)
        else:
            pl.when(z >= k)(lambda: f(z - k, "u", z < 3))
            pl.when(z + k <= 3)(lambda: f(z + k, "d", z > 0))

    def middle(p):
        send("x", y, one(p), r1, r2, middle_sent, m_sem + p)
        send("y", y, one(p), r2, r3, middle_sent, m_sem + p)

    def start():
        send("x", y, one(z), 0, r1, start_sent, f_sem)
        send("y", y, one(z), r3, rows, start_sent, f_sem)
        if r3 > r1:
            pl.when(z < 3)(lambda: send("u", y, one(z), r1, r3, single_sent, zs_sem + z))
            pl.when(z > 0)(lambda: send("d", y, one(z), r1, r3, single_sent, zs_sem + z))
            middle(z)

    def pair(way, p):
        send(way, y, two(p), 0, r1, pair_sent, zp_sem + p)
        send(way, every, one(p), r3, rows, pair_sent, zp_sem + p)

    def first_hop():
        net.recv(V(y, one(z), 0, ends), f_sem)
        pl.when(z < 3)(lambda: pair("u", z))
        pl.when(z > 0)(lambda: pair("d", z))

    def single_hop(k):
        def hop(p, way, more):
            net.recv(V(y, one(p), r1, r3), zs_sem + p)
            if k < 3:
                pl.when(more)(lambda: send(way, y, one(p), r1, r3, single_sent, zs_sem + p))
            middle(p)

        sides(k, hop)

    def pair_hop(k):
        def hop(p, way, more):
            net.recv(V(y, two(p), 0, ends), zp_sem + p)
            if k < 3:
                pl.when(more)(lambda: pair(way, p))

        sides(k, hop)

    def last_hop(k):
        def hop(p, way, more):
            if r3 > r1:
                net.recv(V(y, one(p), r1, r3), m_sem + p)
            send("y", y, two(p), 0, r2, last_sent, l_sem + p)
            send("x", every, one(p), r2, rows, last_sent, l_sem + p)

        sides(k, hop)

    def to_core(k):
        def hop(p, way, more):
            net.recv(V(y, two(p), 0, rows), l_sem + p)
            send("c", every, two(p), 0, rows, core_sent, c_sem)

        sides(k, hop)

    def from_core(k):
        if k == 3:
            net.recv(V(every, every, 0, rows, other=True), c_sem)

    def finish():
        net.wait_sent(V(y, one(z), 0, ends), start_sent)
        net.wait_sent(V(y, every, 0, rows), last_sent)
        net.wait_sent(V(every, every, 0, rows), core_sent)
        if r3 > r1:
            net.wait_sent(V(y, pl.ds(0, 4), r1, r3), middle_sent)

        def along(count):
            if r3 > r1:
                net.wait_sent(V(y, pl.ds(0, count), r1, r3), single_sent)
            total = 2 * ends * count
            yy, blocks = min(
                (yy, n) for yy in (1, 2) for n in range(1, 9) if total % (yy * n * 16) == 0 and total // (yy * n) <= rows
            )
            net.wait_sent(V(y if yy == 1 else every, pl.ds(0, blocks), 0, total // (yy * blocks)), pair_sent)

        inner = jnp.logical_and(z > 0, z < 3)
        pl.when(inner)(lambda: along(5))
        pl.when(jnp.logical_not(inner))(lambda: along(1))

    kinds = (start, first_hop, single_hop, pair_hop, last_hop, to_core, from_core)
    return [f if i < 2 else functools.partial(f, k) for i, f in enumerate(kinds) for k in range(4)], finish


def nn(a, b):
    return lax.dot_general(a, b, (((1,), (0,)), ((), ())), preferred_element_type=F32)


def nt(a, b):
    return lax.dot_general(a, b, (((1,), (1,)), ((), ())), preferred_element_type=F32)


def tn(a, b):
    return lax.dot_general(a, b, (((0,), (0,)), ((), ())), preferred_element_type=F32)


def norm_parts(v):
    centre = jnp.mean(v, axis=-1, keepdims=True)
    shifted = v - centre
    spread = jnp.mean(shifted * shifted, axis=-1, keepdims=True)
    scaled = lax.rsqrt(spread + eps_norm)
    return shifted * scaled, scaled


def norm_back(normal, scaled, gain, upstream):
    weighted = upstream * gain
    return scaled * (
        weighted
        - jnp.mean(weighted, axis=-1, keepdims=True)
        - normal * jnp.mean(weighted * normal, axis=-1, keepdims=True)
    )


def keep(lanes, low, high):
    return jnp.where(lanes, low, high)


def layer_kernel(
    patches, lengths_in, tasks_in, master, first_moment, second_moment, gain_one, gain_two, qkv_in, out_in, u_in, d_in,
    cot_hbm, out_block, out_patch, out_task, out_stats, MIN, FIRST, SECOND,
    GP, GA, GDS, GUS, LOC, SEL, RES, N1, QKV, PT, CTX, RES2, N2, NRM1, NRM2, SC1, SC2, COT, BACK, ACT, GU, MACC, GACC, G2, G2B, DM, DC, LEADR,
    PAIR, PIN, SEND, RECV, ONEHOT, SREC, STSUM, QIN, OIN, GIN, lengths, tasks, own_sem, local_sem, send_sem, recv_sem, all_sem,
):
    net = Net(send_sem, recv_sem)
    z, x, y, c, dp, mp = net.z, net.x, net.y, net.c, net.dp, net.mp
    device = dp * 4 + mp

    barrier = pltpu.get_barrier_semaphore()
    for way, cond in (("x", None), ("y", None), ("c", None), ("u", lambda: z < 3), ("d", lambda: z > 0)):
        run_if(
            cond,
            lambda way=way: pl.semaphore_signal(
                barrier, inc=1, device_id=net.peer[way], device_id_type=MESH
            ),
        )

    def own_cols(w):
        return pl.ds(pl.multiple_of(c * w, 128), w)

    cot_copy = pltpu.make_async_copy(cot_hbm.at[pl.ds(mp * IMGS, IMGS)], COT, local_sem.at[0])
    copies = []
    for refs, widths, weight_in in ((GDS, DOWNS, d_in), (GUS, UPS, u_in)):
        first = 0
        for ref, w in zip(refs, widths):
            copies.append(
                pltpu.make_async_copy(
                    weight_in.at[:, pl.ds(first, w)], ref.at[0, y, dp, :, own_cols(w)], own_sem.at[len(copies)]
                )
            )
            first += w
    for copy in copies:
        copy.start()
    patch_copy = pltpu.make_async_copy(patches, PIN, local_sem.at[1])
    small = [
        pltpu.make_async_copy(src, dst, own_sem.at[len(copies) + i])
        for i, (src, dst) in enumerate(
            ((qkv_in, QIN), (out_in, OIN), (master, MIN), (gain_one, GIN.at[0]), (gain_two, GIN.at[1]),
             (lengths_in, lengths), (tasks_in, tasks))
        )
    ]
    for copy in small:
        copy.start()
    patch_copy.start()
    cot_copy.start()
    moments = [
        pltpu.make_async_copy(first_moment, FIRST, local_sem.at[2]),
        pltpu.make_async_copy(second_moment, SECOND, local_sem.at[3]),
    ]
    for copy in moments:
        copy.start()
    for copy in small:
        copy.wait()

    qkv = [QIN[i].astype(F32) for i in range(3)]
    outs = OIN[...].astype(F32).T
    low = lax.broadcasted_iota(jnp.int32, (96, 128), 1) < HEAD_DIM

    def tail(v, high):
        v = jnp.concatenate([v[:, 128:192], v[:, 128:192]], axis=1)
        return v

    tiles = [qkv[0][:, 0:128], qkv[1][:, 0:128], qkv[2][:, 0:128]]
    tiles.append(jnp.where(low, tail(qkv[0], 0), tail(qkv[2], 1)))
    tiles.append(jnp.where(low, tail(qkv[1], 0), tail(outs, 1)))
    tiles.append(outs[:, 0:128])
    GA[0, pl.ds(y, 1), pl.ds(dp, 1), :, own_cols(D)] = (
        jnp.concatenate(tiles, axis=1).astype(BF16)[None, None]
    )

    LOC[:, 0:PART] = MIN[...]
    lane = lax.broadcasted_iota(jnp.int32, (TASKS, PADP - PART), 1)
    LOC[:, PART:PADP] = jnp.where(
        lane == 0, tasks[0, 0].astype(F32), jnp.where(lane == 1, tasks[0, 1].astype(F32), 0.0)
    )
    half = PADP // 2
    GP[0, pl.ds(y, 1), pl.ds(dp, 1), :, own_cols(half)] = (
        jnp.concatenate([LOC[:, 0:half], LOC[:, half:PADP]], axis=0).astype(BF16)[None, None]
    )
    for copy in copies:
        copy.wait()
    inner = jnp.logical_and(z > 0, z < 3)
    run_if(lambda: inner, lambda: pl.semaphore_wait(barrier, 5))
    run_if(lambda: jnp.logical_not(inner), lambda: pl.semaphore_wait(barrier, 4))

    gathers = [gather_events(net, GP, half, (16, 16, 16, 16))]
    for ref, w, split in zip((GA, *GDS, *GUS), (D, *DOWNS, *UPS), SPLITS):
        gathers.append(gather_events(net, ref, w, split))

    g1 = GIN[0].reshape(1, D)
    g2 = GIN[1].reshape(1, D)
    limits = [lengths[b] + LEAD for b in range(IMGS)]
    live = [
        (lax.broadcasted_iota(jnp.int32, (ROWS, 1), 0) < limits[b]).astype(F32) for b in range(IMGS)
    ]

    def place_rows():
        patch_copy.wait()
        cot_copy.wait()
        for copy in moments:
            copy.wait()
        for b in range(IMGS):
            RES[b, LEAD:ROWS, :] = PIN[:, b, :].astype(F32)

    task_rows = lax.broadcasted_iota(jnp.int32, (TASKS, 1), 0)

    columns = lax.broadcasted_iota(jnp.int32, (TASKS, 128), 1)

    def pick(d, _):
        dd, mm = d // 4, d % 4
        raw = GP[0, mm // 2, dd, :, pl.ds(pl.multiple_of((mm % 2) * half, 128), half)].astype(F32)
        low, high = raw[0:8], raw[8:16]
        rep, j = d // 16, d % 16
        for b in range(IMGS):
            hot = (task_rows == tasks[0, b]).astype(F32)
            row = 2 * rep + b
            SEL[j, pl.ds(row, 1), 0:half] = jnp.sum(low * hot, axis=0, keepdims=True)
            SEL[j, pl.ds(row, 1), half:PADP] = jnp.sum(high * hot, axis=0, keepdims=True)
        base = PART - half
        for b in range(IMGS):
            which = high[0:1, base + b : base + b + 1]
            hot = (lax.broadcasted_iota(jnp.int32, (TASKS, 128), 0).astype(F32) == which).astype(F32)
            for h in range(2):
                ONEHOT[h] += jnp.where(columns == 2 * IMGS * d + 2 * b + h, hot, 0.0)
        return 0

    def place_prompts():
        ONEHOT[...] = jnp.zeros_like(ONEHOT)
        lax.fori_loop(0, NDEV, pick, 0)
        wide = lax.broadcasted_iota(jnp.int32, (4, D), 1)
        for r in range(25):
            j, off = (D * r) // PART, (D * r) % PART
            first = min(D, PART - off)
            low = SEL[j, 0:4, :]
            seg = (pltpu.roll(low, PADP - off, 1) if off else low)[:, 0:D]
            if first < D:
                seg = jnp.where(wide < first, seg, pltpu.roll(SEL[j + 1, 0:4, :], first, 1)[:, 0:D])
            for rep in range(2):
                for b in range(IMGS):
                    RES[b, 25 * rep + r : 25 * rep + r + 1, :] = seg[2 * rep + b : 2 * rep + b + 1]

    def norm_one():
        for b in range(IMGS):
            normal, SC1[b] = norm_parts(RES[b])
            NRM1[b] = normal
            N1[b] = (normal * g1).astype(BF16)

    def weight(ref, core, first, width, span):
        cols = pl.ds(pl.multiple_of(core * span + first, 128), width)
        return ref[:, :, cols].reshape(D, width)

    left = lax.broadcasted_iota(jnp.int32, (ROWS, 128), 1) < HEAD_DIM
    scale = 1.0 / math.sqrt(HEAD_DIM)
    wide = lax.broadcasted_iota(jnp.int32, (1, 640), 1)
    q_scale = jnp.where((wide < 128) | ((wide >= 384) & (wide < 448)), scale, 1.0)

    def project(m):
        w = weight(GA.at[0, m // 2], m % 2, 0, 640, D)
        mixed = nn(N1[...].reshape(IMGS * ROWS, D), w) * q_scale
        QKV[m] = mixed.astype(BF16).reshape(IMGS, ROWS, 640)

    key_rows = lax.broadcasted_iota(jnp.int32, (ROWS, ROWS), 0)
    zero = jnp.zeros((), BF16)

    def attend(t):
        b, m = t // 4, t % 4
        tile = lambda i: QKV[m, b, :, 128 * i : 128 * i + 128]
        q01, k01, v01, q2v2, k2 = (tile(i) for i in range(5))
        mask = key_rows < (lengths[b] + LEAD)

        def soft(keys, queries):
            s = jnp.where(mask, nt(keys, queries), -1e30)
            e = jnp.exp(s - jnp.max(s, axis=0, keepdims=True))
            return (e * (1.0 / jnp.sum(e, axis=0, keepdims=True))).astype(BF16)

        p0 = soft(k01, keep(left, q01, zero))
        p1 = soft(k01, keep(left, zero, q01))
        p2 = soft(k2, keep(left, q2v2, zero))
        PT[t, 0], PT[t, 1], PT[t, 2] = p0, p1, p2
        CTX[b, :, m * 256 : m * 256 + 128] = keep(left, 0.0, tn(p2, q2v2)).astype(BF16)
        CTX[b, :, m * 256 + 128 : m * 256 + 256] = keep(
            left, tn(p0, v01), tn(p1, v01)
        ).astype(BF16)

    def attend_two(t):
        attend(2 * t)
        attend(2 * t + 1)

    sums = [jnp.zeros((1, 1), F32) for _ in range(3)]

    def total(v):
        return jnp.sum(jnp.sum(v, axis=0, keepdims=True), axis=1, keepdims=True)

    def project_out(b):
        attn = jnp.zeros((ROWS, D), F32)
        for m in range(4):
            attn += nt(CTX[b, :, 256 * m : 256 * m + 256], weight(GA.at[0, m // 2], m % 2, 512, 256, D))
        sums[1] += total(attn * attn * live[b])
        res2 = RES[b] + attn
        RES2[b] = res2
        normal, SC2[b] = norm_parts(res2)
        NRM2[b] = normal
        N2[b] = (normal * g2).astype(BF16)

    def back_units(i, yy):
        w, first = DOWNS[i], sum(DOWNS[:i])
        cot = COT[...].reshape(IMGS * ROWS, D)
        for core in range(2):
            back = nn(cot, weight(GDS[i].at[0, yy], core, 0, w, w))
            BACK[yy, :, core * D + first : core * D + first + w] = back.astype(BF16)

    def up_units(i, core):
        w, first = UPS[i], sum(UPS[:i])
        rows2 = N2[...].reshape(IMGS * ROWS, D)
        here = pl.ds(pl.multiple_of(core * w, 128), w)
        for yy in range(2):
            up = nn(rows2, weight(GUS[i].at[0, yy], core, 0, w, w))
            back = BACK[yy, :, pl.ds(pl.multiple_of(core * D + first, 128), w)].astype(F32)
            cumul = 0.5 * (1.0 + lax.erf(up * 0.7071067811865476))
            density = jnp.exp(-0.5 * up * up) * 0.3989422804014327
            ACT[yy, :, here] = (up * cumul).astype(BF16)
            GU[yy, :, here] = (back * (cumul + up * density)).astype(BF16)

    def add_units(i, yy):
        w, first = UPS[i], sum(UPS[:i])
        d = max(d for d in range(len(DOWNS)) if sum(DOWNS[:d]) <= first)
        inside = first - sum(DOWNS[:d])
        if w == DOWNS[d]:
            mlp = nt(ACT[yy, :, 0 : 2 * w], weight(GDS[d].at[0, yy], 0, 0, 2 * w, w))
        else:
            mlp = sum(
                nt(ACT[yy, :, w * core : w * (core + 1)], weight(GDS[d].at[0, yy], core, inside, w, DOWNS[d]))
                for core in range(2)
            )
        grad = nt(GU[yy, :, 0 : 2 * w], weight(GUS[i].at[0, yy], 0, 0, 2 * w, w))
        mlp, grad = mlp.reshape(IMGS, ROWS, D), grad.reshape(IMGS, ROWS, D)
        if i == 0 and yy == 0:
            MACC[...] = mlp
            GACC[...] = grad
        else:
            MACC[...] += mlp
            GACC[...] += grad

    steps = [place_rows, place_prompts, norm_one]
    steps += [functools.partial(project, m) for m in range(4)]
    steps += [functools.partial(attend_two, t) for t in range(4)]
    steps += [functools.partial(project_out, b) for b in range(IMGS)]
    steps += [functools.partial(back_units, i, yy) for i in range(len(DOWNS)) for yy in range(2)]
    for i in range(len(UPS)):
        steps += [functools.partial(up_units, i, c), functools.partial(up_units, i, 1 - c)]
        steps += [functools.partial(add_units, i, yy) for yy in range(2)]
    for item in ORDER:
        if item < 1000:
            gathers[item // 28][0][item % 28]()
        else:
            steps[item - 1000]()

    for b in range(IMGS):
        g = COT[b].astype(F32) + norm_back(NRM2[b], SC2[b], g2, GACC[b])
        G2[b] = g
        G2B[b] = g.astype(BF16)

    def context_back(m, _):
        cols = pl.ds(pl.multiple_of((m % 2) * D + 512, 128), 256)
        w = GA[0, m // 2, :, :, cols].reshape(D, 256)
        DC[m] = nn(G2B[...].reshape(IMGS * ROWS, D), w).astype(BF16).reshape(IMGS, ROWS, 256)
        return 0

    lax.fori_loop(0, 4, context_back, 0, unroll=4)

    def attend_back(b):
        tiles, grad_probs, grad_scores = [], [], []
        for m in range(4):
            tiles.append(
                [QKV[m, b, :, 128 * i : 128 * i + 128] for i in range(5)]
                + [DC[m, b, :, 0:128], DC[m, b, :, 128:256]]
            )
            q01, k01, v01, q2v2, k2, c2, c01 = tiles[m]
            grad_probs.append(
                [nt(keep(left, v01, zero), c01), nt(keep(left, zero, v01), c01), nt(keep(left, zero, q2v2), c2)]
            )
        for m in range(4):
            out = []
            for h in range(3):
                pf, dp_ = PT[4 * b + m, h].astype(F32), grad_probs[m][h]
                inner = jnp.sum(pf * dp_, axis=0, keepdims=True)
                out.append((pf * (dp_ - inner)).astype(BF16))
            grad_scores.append(out)
        for m in range(4):
            q01, k01, v01, q2v2, k2, c2, c01 = tiles[m]
            s0, s1, s2 = grad_scores[m]
            p0, p1, p2 = (PT[4 * b + m, h] for h in range(3))
            DM[m, b, :, 0:128] = (keep(left, tn(s0, k01), tn(s1, k01)) * scale).astype(BF16)
            DM[m, b, :, 128:256] = keep(left, nn(s0, q01), nn(s1, q01)).astype(BF16)
            DM[m, b, :, 256:384] = keep(left, nn(p0, c01), nn(p1, c01)).astype(BF16)
            DM[m, b, :, 384:512] = keep(left, tn(s2, k2) * scale, nn(p2, c2)).astype(BF16)
            DM[m, b, :, 512:640] = keep(left, nn(s2, q2v2), 0.0).astype(BF16)

    def grad_rows(rows, first, last):
        count = last - first
        grad = jnp.zeros((len(rows) * count, D), F32)
        for m in range(4):
            mixed = jnp.concatenate([DM[m, b, first:last] for b in rows], axis=0)
            grad += nt(mixed, weight(GA.at[0, m // 2], m % 2, 0, 640, D))
        for i, b in enumerate(rows):
            part = grad[count * i : count * (i + 1)]
            GACC[b, first:last] = G2[b, first:last] + norm_back(NRM1[b, first:last], SC1[b, first:last], g1, part)

    def to_others(src, dst, sems):
        for step in (4, 5, 3, 6, 2, 7, 1, 0):
            to_dp = (dp + step) & 7
            for turn in range(4):
                if step or turn:
                    to_mp = (mp + turn) & 3
                    pltpu.make_async_remote_copy(
                        src_ref=src(to_dp * 4 + to_mp),
                        dst_ref=dst,
                        send_sem=all_sem.at[sems],
                        recv_sem=all_sem.at[sems + 1],
                        device_id=(to_dp, to_mp),
                        device_id_type=MESH,
                    ).start()

    wide = lax.broadcasted_iota(jnp.int32, (4, PADP), 1)

    def to_owners():
        for rep in range(2):
            for b in range(IMGS):
                LEADR[:, 2 * rep + b : 2 * rep + b + 1, :] = GACC[b, 25 * rep : 25 * rep + 25, :][:, None, :]
        for q in range(16):
            r, off = (PART * q) // D, (PART * q) % D
            msg, have = None, -off
            while have < PART:
                row = LEADR[r]
                moved = pltpu.roll(row, have % D, 1) if have % D else row
                moved = jnp.concatenate([moved, moved[:, 0 : PADP - D]], axis=1)
                msg = moved if msg is None else jnp.where(wide < have, msg, moved)
                have += D
                r += 1
            msg = jnp.where(wide < PART, msg, 0.0).astype(BF16)
            for rep in range(2):
                SEND[16 * rep + q] = jnp.concatenate(
                    [msg[2 * rep + b : 2 * rep + b + 1, half * h : half * h + half] for b in range(IMGS) for h in range(2)],
                    axis=0,
                )
        to_others(lambda other: SEND.at[other], RECV.at[device], 0)
        RECV[pl.ds(device, 1)] = SEND[pl.ds(device, 1)]

    def others(ref):
        return ref.at[pl.ds(0, NDEV - 1)]

    def wait_all(ref, sem):
        pltpu.make_async_copy(others(ref), others(ref), all_sem.at[sem]).wait()

    some = 64
    for b in range(IMGS):
        attend_back(b)
    grad_rows((0, 1), 0, some)
    to_owners()

    grad_rows((0, 1), some, ROWS)
    for b in range(IMGS):
        mlp = MACC[b]
        block = RES2[b] + mlp
        out_block[b] = block.astype(BF16)
        sums[0] += total(block * block * live[b])
        sums[2] += total(mlp * mlp * live[b])

    wait_all(RECV, 1)

    came = RECV[...].reshape(2 * IMGS * NDEV, half)
    acc = [nn(ONEHOT[h].astype(BF16), came) for h in range(2)]
    square = total(acc[0] * acc[0]) + total(acc[1] * acc[1])
    lane = lax.broadcasted_iota(jnp.int32, (1, 128), 1)
    count = (limits[0] + limits[1]).astype(F32)
    stats = jnp.zeros((1, 128), F32)
    for i, v in enumerate((square, sums[0], sums[1], sums[2], count)):
        stats = jnp.where(lane == i, v, stats)
    STSUM[...] = stats
    SREC[pl.ds(device, 1)] = stats[None]
    to_others(lambda other: STSUM, SREC.at[device], 2)

    out_task[...] = jnp.concatenate(acc, axis=1)[:, 0:PART]
    for b in range(IMGS):
        PAIR[:, b : b + 1, :] = GACC[b, LEAD:ROWS, :][:, None, :]
    out_patch[...] = PAIR[...].astype(BF16)
    wait_all(RECV, 0)
    for gather in gathers:
        gather[1]()
    wait_all(SREC, 3)
    out_stats[...] = jnp.sum(SREC[...], axis=0)
    wait_all(SREC, 2)


def update_kernel(
    task_grad, stats, master, first_moment, second_moment, block_in, patch_in,
    out_grad, out_first, out_second, out_master, out_copy, out_norm, out_rms, block_out, patch_out, sem,
):
    copies = [
        pltpu.make_async_copy(block_in, block_out, sem.at[0]),
        pltpu.make_async_copy(patch_in, patch_out, sem.at[1]),
    ]
    for copy in copies:
        copy.start()
    st = stats[0:1, :]
    norm = jnp.sqrt(st[0:1, 0:1])
    grad = task_grad[...] * (clip_level / jnp.maximum(norm, clip_level))
    first = beta_one * first_moment[...] + (1.0 - beta_one) * grad
    second = beta_two * second_moment[...] + (1.0 - beta_two) * grad * grad
    step_size = (
        first / (1.0 - beta_one**STEP) / (jnp.sqrt(second / (1.0 - beta_two**STEP)) + adam_eps)
    )
    old = master[...]
    new = old - learn_rate * (step_size + decay_rate * old)
    out_grad[...] = grad
    out_first[...] = first
    out_second[...] = second
    out_master[...] = new
    out_copy[...] = new.astype(BF16)
    out_norm[0] = norm[0, 0]
    rms = jnp.sqrt(st / (st[0:1, 4:5] * D))
    for i in range(3):
        out_rms[i] = rms[0, i + 1]
    for copy in copies:
        copy.wait()


def fast_body(
    patches, lengths, tasks, prompt_master, first_moment, second_moment,
    gain_one, gain_two, w_qkv, w_out, w_up, w_down, cotangent,
):
    vmem = pl.BlockSpec(memory_space=pltpu.VMEM)
    smem = pl.BlockSpec(memory_space=pltpu.SMEM)
    anywhere = pl.BlockSpec(memory_space=pl.ANY)
    V = pltpu.VMEM
    block, patch, *states = pl.pallas_call(
        layer_kernel,
        out_shape=[
            V((IMGS, ROWS, D), BF16),
            V((PATCH, IMGS, D), BF16),
            V((TASKS, PART), F32),
            V((1, 128), F32),
        ]
        + [V((TASKS, PART), F32)] * 3,
        in_specs=[anywhere] * 13,
        out_specs=[vmem] * 7,
        scratch_shapes=[
            V((1, 2, 8, 16, PADP), BF16),
            V((1, 2, 8, 96, 2 * D), BF16),
            [V((1, 2, 8, 96, 2 * w), BF16) for w in DOWNS],
            [V((1, 2, 8, 96, 2 * w), BF16) for w in UPS],
            V((TASKS, PADP), F32),
            V((16, 4, PADP), F32),
            V((IMGS, ROWS, D), F32),
            V((IMGS, ROWS, D), BF16),
            V((4, IMGS, ROWS, 640), BF16),
            V((8, 3, ROWS, ROWS), BF16),
            V((IMGS, ROWS, 1024), BF16),
            V((IMGS, ROWS, D), F32),
            V((IMGS, ROWS, D), BF16),
            V((IMGS, ROWS, D), F32),
            V((IMGS, ROWS, D), F32),
            V((IMGS, ROWS, 1), F32),
            V((IMGS, ROWS, 1), F32),
            V((IMGS, ROWS, D), BF16),
            V((2, IMGS * ROWS, 2 * D), BF16),
            V((2, IMGS * ROWS, 2 * max(UPS)), BF16),
            V((2, IMGS * ROWS, 2 * max(UPS)), BF16),
            V((IMGS, ROWS, D), F32),
            V((IMGS, ROWS, D), F32),
            V((IMGS, ROWS, D), F32),
            V((IMGS, ROWS, D), BF16),
            V((4, IMGS, ROWS, 640), BF16),
            V((4, IMGS, ROWS, 256), BF16),
            V((25, 4, D), F32),
            V((PATCH, IMGS, D), F32),
            V((PATCH, IMGS, D), BF16),
            V((NDEV, 2 * IMGS, PADP // 2), BF16),
            V((NDEV, 2 * IMGS, PADP // 2), BF16),
            V((2, TASKS, 128), F32),
            V((NDEV, 1, 128), F32),
            V((1, 128), F32),
            V((3, 96, 192), BF16),
            V((192, 96), BF16),
            V((2, D), F32),
            pltpu.SMEM((IMGS,), jnp.int32),
            pltpu.SMEM((1, IMGS), jnp.int32),
            pltpu.SemaphoreType.DMA((7 + len(DOWNS) + len(UPS),)),
            pltpu.SemaphoreType.DMA((4,)),
            pltpu.SemaphoreType.DMA((6 * (2 + len(DOWNS) + len(UPS)),)),
            pltpu.SemaphoreType.DMA((10 + 18 * (1 + len(DOWNS) + len(UPS)),)),
            pltpu.SemaphoreType.DMA((4,)),
        ],
        compiler_params=pltpu.CompilerParams(
            collective_id=0, has_side_effects=True, vmem_limit_bytes=58 << 20
        ),
    )(
        patches.transpose(1, 0, 2), lengths, tasks.T, prompt_master, first_moment, second_moment, gain_one, gain_two,
        w_qkv.transpose(1, 0, 2), w_out, w_up, w_down.T, cotangent,
    )
    state = jax.ShapeDtypeStruct((TASKS, PART), F32)

    def keep_near(v):
        return pltpu.with_memory_space_constraint(v, pltpu.VMEM)

    grad, first, second, master, copy, norm, rms, block_out, patch_out = pl.pallas_call(
        update_kernel,
        out_shape=[state] * 4
        + [
            jax.ShapeDtypeStruct((TASKS, PART), BF16),
            jax.ShapeDtypeStruct((1,), F32),
            jax.ShapeDtypeStruct((3,), F32),
            jax.ShapeDtypeStruct((IMGS, ROWS, D), BF16),
            jax.ShapeDtypeStruct((PATCH, IMGS, D), BF16),
        ],
        in_specs=[vmem] * 7,
        out_specs=[vmem] * 5 + [smem] * 2 + [anywhere] * 2,
        scratch_shapes=[pltpu.SemaphoreType.DMA((2,))],
    )(*(keep_near(v) for v in (*states, block, patch)))
    return (
        block_out, patch_out.transpose(1, 0, 2), grad, norm.reshape(()), first, second, master, copy, rms,
    )


def layer_norm(values, gain):
    centre = jnp.mean(values, axis=-1, keepdims=True)
    shifted = values - centre
    spread = jnp.mean(shifted * shifted, axis=-1, keepdims=True)
    return shifted * lax.rsqrt(spread + eps_norm) * gain


def whole_norm_back(values, gain, upstream):
    centre = jnp.mean(values, axis=-1, keepdims=True)
    shifted = values - centre
    spread = jnp.mean(shifted * shifted, axis=-1, keepdims=True)
    scaled = lax.rsqrt(spread + eps_norm)
    normal_part = shifted * scaled
    weighted = upstream * gain
    return scaled * (
        weighted
        - jnp.mean(weighted, axis=-1, keepdims=True)
        - normal_part * jnp.mean(weighted * normal_part, axis=-1, keepdims=True)
    )


def gelu_slope(upward):
    cumul = 0.5 * (1.0 + lax.erf(upward * 0.7071067811865476))
    density = jnp.exp(-0.5 * upward * upward) * 0.3989422804014327
    return cumul + upward * density


def attend_forward(group_normed, group_limit, w_mix, block_images):
    group_size, row_count, feature_count = group_normed.shape
    lane_width = w_mix.shape[2]
    head_count = lane_width // HEAD_DIM
    scale = 1.0 / math.sqrt(HEAD_DIM)
    mask_all = jnp.arange(row_count, dtype=jnp.int32)[None, :] < group_limit[:, None]

    def one_block(block_index):
        first_row = block_index * block_images
        block_in = lax.dynamic_slice_in_dim(group_normed, first_row, block_images, 0)
        key_mask = lax.dynamic_slice_in_dim(mask_all, first_row, block_images, 0)
        mixed_qkv = jnp.einsum(
            "brd,dce->brce", block_in, w_mix, preferred_element_type=jnp.float32
        ).astype(jnp.bfloat16)
        split_heads = mixed_qkv.reshape(block_images, row_count, 3, head_count, HEAD_DIM)
        scores = (
            jnp.einsum(
                "bqhe,bkhe->bhqk",
                split_heads[:, :, 0],
                split_heads[:, :, 1],
                preferred_element_type=jnp.float32,
            )
            * scale
        )
        scores = jnp.where(key_mask[:, None, None, :], scores, -1e30)
        row_top = jnp.max(scores, axis=-1, keepdims=True)
        exponent = jnp.exp(scores - row_top)
        row_total = jnp.sum(exponent, axis=-1, keepdims=True)
        attend_weights = (exponent / row_total).astype(jnp.bfloat16)
        context = jnp.einsum(
            "bhqk,bkhe->bqhe",
            attend_weights,
            split_heads[:, :, 2],
            preferred_element_type=jnp.float32,
        )
        context = context.astype(jnp.bfloat16).reshape(block_images, row_count, lane_width)
        return (mixed_qkv, context, (row_top + jnp.log(row_total))[..., 0])

    mixed_qkv, context, logsums = lax.map(
        one_block, jnp.arange(group_size // block_images, dtype=jnp.int32)
    )
    return (
        mixed_qkv.reshape(group_size, row_count, 3, lane_width),
        context.reshape(group_size, row_count, lane_width),
        logsums.reshape(group_size, head_count, row_count),
    )


def attend_back(mixed_qkv, logsums, group_limit, grad_context, block_images):
    group_size, row_count, three_parts, lane_width = mixed_qkv.shape
    head_count = lane_width // HEAD_DIM
    scale = 1.0 / math.sqrt(HEAD_DIM)
    mask_all = jnp.arange(row_count, dtype=jnp.int32)[None, :] < group_limit[:, None]

    def one_block(block_index):
        first_row = block_index * block_images
        split_heads = lax.dynamic_slice_in_dim(mixed_qkv, first_row, block_images, 0).reshape(
            block_images, row_count, 3, head_count, HEAD_DIM
        )
        queries = split_heads[:, :, 0]
        keys_all = split_heads[:, :, 1]
        values = split_heads[:, :, 2]
        key_mask = lax.dynamic_slice_in_dim(mask_all, first_row, block_images, 0)
        logsum = lax.dynamic_slice_in_dim(logsums, first_row, block_images, 0)
        grad_out = lax.dynamic_slice_in_dim(grad_context, first_row, block_images, 0).reshape(
            block_images, row_count, head_count, HEAD_DIM
        )
        scores = (
            jnp.einsum("bqhe,bkhe->bhqk", queries, keys_all, preferred_element_type=jnp.float32)
            * scale
        )
        scores = jnp.where(key_mask[:, None, None, :], scores, -1e30)
        attend_weights = jnp.exp(scores - logsum[..., None])
        grad_weights = jnp.einsum(
            "bqhe,bkhe->bhqk", grad_out, values, preferred_element_type=jnp.float32
        )
        row_inner = jnp.sum(attend_weights * grad_weights, axis=-1, keepdims=True)
        grad_scores = (attend_weights * (grad_weights - row_inner)).astype(jnp.bfloat16)
        grad_query = (
            jnp.einsum("bhqk,bkhe->bqhe", grad_scores, keys_all, preferred_element_type=jnp.float32)
            * scale
        )
        grad_key = (
            jnp.einsum("bhqk,bqhe->bkhe", grad_scores, queries, preferred_element_type=jnp.float32)
            * scale
        )
        grad_value = jnp.einsum(
            "bhqk,bqhe->bkhe",
            attend_weights.astype(jnp.bfloat16),
            grad_out,
            preferred_element_type=jnp.float32,
        )
        stacked = jnp.stack([grad_query, grad_key, grad_value], axis=2).astype(jnp.bfloat16)
        return stacked.reshape(block_images, row_count, 3, lane_width)

    grad_mixed = lax.map(one_block, jnp.arange(group_size // block_images, dtype=jnp.int32))
    return grad_mixed.reshape(group_size, row_count, 3, lane_width)


def expand_units(group_two, w_expand, block_images):
    group_size, row_count, feature_count = group_two.shape

    def one_block(block_index):
        block_in = lax.dynamic_slice_in_dim(group_two, block_index * block_images, block_images, 0)
        upward = jnp.einsum("brd,df->brf", block_in, w_expand, preferred_element_type=jnp.float32)
        return jax.nn.gelu(upward, approximate=False).astype(jnp.bfloat16)

    act_units = lax.map(one_block, jnp.arange(group_size // block_images, dtype=jnp.int32))
    return act_units.reshape(group_size, row_count, w_expand.shape[1])


def units_back(grad_group, group_two, w_expand, w_reduce, block_images):
    group_size, row_count, feature_count = group_two.shape

    def one_block(block_index):
        first_row = block_index * block_images
        grad_in = lax.dynamic_slice_in_dim(grad_group, first_row, block_images, 0)
        norm_in = lax.dynamic_slice_in_dim(group_two, first_row, block_images, 0)
        back_units = jnp.einsum(
            "brd,fd->brf", grad_in, w_reduce, preferred_element_type=jnp.float32
        )
        upward = jnp.einsum("brd,df->brf", norm_in, w_expand, preferred_element_type=jnp.float32)
        return (back_units * gelu_slope(upward)).astype(jnp.bfloat16)

    grad_units = lax.map(one_block, jnp.arange(group_size // block_images, dtype=jnp.int32))
    return grad_units.reshape(group_size, row_count, w_expand.shape[1])


def rows_term(source, weight, form):
    return jnp.einsum(form, source, weight, preferred_element_type=jnp.float32)


def body(
    patches,
    lengths,
    tasks,
    prompt_master,
    first_moment,
    second_moment,
    gain_one,
    gain_two,
    w_qkv,
    w_out,
    w_up,
    w_down,
    cotangent,
):
    held_count, patch_count, feature_count = patches.shape
    row_count = cotangent.shape[1]
    lead_count = row_count - patch_count
    task_count = prompt_master.shape[0]
    prompt_table = lax.all_gather(
        prompt_master.astype(jnp.bfloat16), ("dp", "mp"), axis=1, tiled=True
    )
    chosen = tasks == jnp.arange(task_count, dtype=jnp.int32)[None, :]
    lead_part = jnp.dot(
        chosen.astype(jnp.bfloat16), prompt_table, preferred_element_type=jnp.float32
    )
    residual = jnp.concatenate(
        [lead_part.reshape(held_count, lead_count, feature_count), patches.astype(jnp.float32)],
        axis=1,
    )
    row_limit = lengths + lead_count
    w_mix, w_expand, w_reduce, w_rows = (
        lax.all_gather(w_qkv, "dp", axis=0, tiled=True),
        lax.all_gather(w_up, "dp", axis=0, tiled=True),
        lax.all_gather(w_down, "dp", axis=1, tiled=True),
        lax.all_gather(w_out, "dp", axis=1, tiled=True),
    )
    normed = layer_norm(residual, gain_one).astype(jnp.bfloat16)
    mp_rank = lax.axis_index("mp")
    group_normed, group_bound = (
        lax.all_gather(normed, "mp", axis=0, tiled=True),
        lax.all_gather(row_limit.astype(jnp.bfloat16), "mp", axis=0, tiled=True),
    )
    group_limit = group_bound.astype(jnp.int32)
    mixed_qkv, context, logsums = attend_forward(group_normed, group_limit, w_mix, held_count)
    attn_out = lax.psum_scatter(
        rows_term(context, w_rows, "brc,cd->brd"), "mp", scatter_dimension=0, tiled=True
    )
    residual_two = residual + attn_out
    normed_two = layer_norm(residual_two, gain_two).astype(jnp.bfloat16)
    group_two = lax.all_gather(normed_two, "mp", axis=0, tiled=True)
    act_units = expand_units(group_two, w_expand, held_count)
    mlp_out = lax.psum_scatter(
        rows_term(act_units, w_reduce, "brf,fd->brd").astype(jnp.bfloat16),
        "mp",
        scatter_dimension=0,
        tiled=True,
    ).astype(jnp.float32)
    block_sum = residual_two + mlp_out
    live_rows = (jnp.arange(row_count, dtype=jnp.int32)[None, :] < row_limit[:, None]).astype(
        jnp.float32
    )[:, :, None]
    square_sums = jnp.stack(
        [
            jnp.sum(block_sum * block_sum * live_rows),
            jnp.sum(attn_out * attn_out * live_rows),
            jnp.sum(mlp_out * mlp_out * live_rows),
        ]
    )
    live_count = jnp.sum(row_limit).astype(jnp.float32)
    w_mix, w_expand, w_reduce, w_rows = (
        lax.all_gather(w_qkv, "dp", axis=0, tiled=True),
        lax.all_gather(w_up, "dp", axis=0, tiled=True),
        lax.all_gather(w_down, "dp", axis=1, tiled=True),
        lax.all_gather(w_out, "dp", axis=1, tiled=True),
    )
    grad_held = lax.dynamic_slice_in_dim(cotangent, mp_rank * held_count, held_count, 0)
    grad_units = units_back(cotangent, group_two, w_expand, w_reduce, held_count)
    grad_normed_two = lax.psum_scatter(
        rows_term(grad_units, w_expand, "brf,df->brd"), "mp", scatter_dimension=0, tiled=True
    )
    grad_two = grad_held.astype(jnp.float32) + whole_norm_back(residual_two, gain_two, grad_normed_two)
    grad_low = grad_two.astype(jnp.bfloat16)
    grad_context = jnp.einsum(
        "brd,cd->brc",
        lax.all_gather(grad_low, "mp", axis=0, tiled=True),
        w_rows,
        preferred_element_type=jnp.float32,
    ).astype(jnp.bfloat16)
    grad_mixed = attend_back(mixed_qkv, logsums, group_limit, grad_context, held_count)
    grad_normed = lax.psum_scatter(
        rows_term(grad_mixed, w_mix, "brce,dce->brd").astype(jnp.bfloat16),
        "mp",
        scatter_dimension=0,
        tiled=True,
    ).astype(jnp.float32)
    grad_residual = grad_two + whole_norm_back(residual, gain_one, grad_normed)
    patch_grad = grad_residual[:, lead_count:].astype(jnp.bfloat16)
    lead_grad = grad_residual[:, :lead_count].reshape(held_count, lead_count * feature_count)
    task_term = jnp.dot(
        chosen.astype(jnp.float32).T,
        lead_grad,
        precision=lax.Precision.HIGHEST,
        preferred_element_type=jnp.float32,
    )
    task_grad = lax.psum_scatter(task_term, ("dp", "mp"), scatter_dimension=1, tiled=True)
    square = jnp.sum(task_grad * task_grad)
    square, square_sums, live_count = lax.psum((square, square_sums, live_count), ("dp", "mp"))
    grad_norm = jnp.sqrt(square)
    prompt_grad = task_grad * (clip_level / jnp.maximum(grad_norm, clip_level))
    new_first = beta_one * first_moment + (1.0 - beta_one) * prompt_grad
    new_second = beta_two * second_moment + (1.0 - beta_two) * prompt_grad * prompt_grad
    step_size = (
        new_first
        / (1.0 - beta_one**STEP)
        / (jnp.sqrt(new_second / (1.0 - beta_two**STEP)) + adam_eps)
    )
    new_master = prompt_master - learn_rate * (step_size + decay_rate * prompt_master)
    rms_stats = jnp.sqrt(square_sums / (live_count * feature_count))
    return (
        block_sum.astype(jnp.bfloat16),
        patch_grad,
        prompt_grad,
        grad_norm,
        new_first,
        new_second,
        new_master,
        new_master.astype(jnp.bfloat16),
        rms_stats,
    )


def solution(mesh):
    small = mesh.shape["dp"] == 8 and mesh.shape["mp"] == 4
    return jax.shard_map(
        fast_body if small else body,
        mesh=mesh,
        in_specs=(
            P(("dp", "mp"), None, None),
            P(("dp", "mp")),
            P(("dp", "mp"), None),
            P(None, ("dp", "mp")),
            P(None, ("dp", "mp")),
            P(None, ("dp", "mp")),
            P(),
            P(),
            P("dp", None, "mp"),
            P("mp", "dp"),
            P("dp", "mp"),
            P("mp", "dp"),
            P("dp", None, None),
        ),
        out_specs=(
            P(("dp", "mp"), None, None),
            P(("dp", "mp"), None, None),
            P(None, ("dp", "mp")),
            P(),
            P(None, ("dp", "mp")),
            P(None, ("dp", "mp")),
            P(None, ("dp", "mp")),
            P(None, ("dp", "mp")),
            P(),
        ),
        check_vma=False,
    )
```

```python
import functools
import math

import jax
import jax.numpy as jnp
from jax import lax
from jax.experimental import pallas as pl
from jax.experimental.pallas import tpu as pltpu
from jax.sharding import PartitionSpec as P

HEAD_DIM = 64
STEP = 10
MESH = pl.DeviceIdType.MESH
F32 = jnp.float32
BF16 = jnp.bfloat16

eps_norm = 1e-06
clip_level = 1.0
beta_one = 0.9
beta_two = 0.999
learn_rate = 3.0
decay_rate = 0.05
adam_eps = 1e-08

D = 768
ROWS = 256
LEAD = 50
PATCH = 206
IMGS = 2
TASKS = 8
PART = 1200
PADP = 1280
NDEV = 32
DOWNS = (512, 256)
UPS = (512, 256)
SPLITS = ((16, 48, 80, 96), (32, 48, 64, 96), (16, 48, 48, 96), (32, 48, 64, 96), (16, 32, 64, 96))
ORDER = (
    28, 56, 0, 1000, 112, 32, 84, 44, 4, 16, 37, 140, 13, 41, 17, 38, 14, 18, 48, 60,
    45, 42, 144, 121, 65, 21, 22, 39, 15, 19, 46, 156, 20, 23, 43, 47, 69, 72, 116, 149,
    49, 27, 1001, 93, 66, 50, 1002, 51, 128, 70, 160, 73, 125, 122, 76, 88, 150, 74, 55, 1003,
    1004, 1005, 67, 129, 1006, 94, 1007, 126, 71, 153, 132, 77, 123, 75, 1008, 78, 130, 1009, 97, 157,
    1010, 79, 127, 131, 1011, 1012, 95, 133, 154, 100, 151, 158, 83, 98, 102, 101, 1013, 134, 1014, 135,
    161, 1017, 99, 155, 104, 103, 159, 139, 1018, 162, 106, 1019, 105, 107, 1020, 111, 163, 1015, 1016, 1021,
    167, 1022, 1023, 1024,
)


def run_if(cond, f):
    if cond is None:
        f()
    else:
        pl.when(cond())(f)


class Net:
    def __init__(self, send_sem, recv_sem):
        self.send_sem, self.recv_sem = send_sem, recv_sem
        self.sends = self.recvs = 0
        dp, mp = lax.axis_index("dp"), lax.axis_index("mp")
        z, x, y, c = dp // 2, dp % 2, mp // 2, mp % 2
        self.z, self.x, self.y, self.c = z, x, y, c
        self.dp, self.mp = dp, mp
        self.peer = {
            "x": (2 * z + 1 - x, mp),
            "y": (dp, (1 - y) * 2 + c),
            "c": (dp, 2 * y + 1 - c),
            "u": (jnp.minimum(2 * z + 2 + x, 6 + x), mp),
            "d": (jnp.maximum(2 * z - 2 + x, x), mp),
        }

    def send(self, way, view, sem, landed):
        pltpu.make_async_remote_copy(
            src_ref=view,
            dst_ref=view,
            send_sem=self.send_sem.at[sem],
            recv_sem=self.recv_sem.at[landed],
            device_id=self.peer[way],
            device_id_type=MESH,
        ).start()

    def recv(self, view, landed):
        pltpu.make_async_copy(view, view, self.recv_sem.at[landed]).wait()

    def wait_sent(self, view, sem):
        pltpu.make_async_copy(view, view, self.send_sem.at[sem]).wait()


def gather_events(net, G, W, split):
    z, x, y, c = net.z, net.x, net.y, net.c
    r1, r2, r3, rows = split
    some = 4 if r3 > r1 else 0
    f_sem = net.recvs
    zs_sem, zp_sem, m_sem = f_sem + 1, f_sem + 1 + some, f_sem + 5 + some
    l_sem, c_sem = f_sem + 5 + 2 * some, f_sem + 9 + 2 * some
    net.recvs = c_sem + 1
    start_sent, single_sent, pair_sent, middle_sent, last_sent, core_sent = range(net.sends, net.sends + 6)
    net.sends += 6
    every = slice(None)
    ends = r1 + rows - r3

    def V(yy, d, first, last, other=False):
        core = (1 - c) if other else c
        cols = pl.ds(pl.multiple_of(core * W, 128), W)
        return G.at[:, yy, d, pl.ds(first, last - first), cols]

    def two(p):
        return pl.ds(2 * p, 2)

    def one(p):
        return 2 * p + x

    def send(way, yy, d, first, last, sem, landed):
        if last > first:
            net.send(way, V(yy, d, first, last), sem, landed)

    def sides(k, f):
        if k == 0:
            f(z, None, None)
        else:
            pl.when(z >= k)(lambda: f(z - k, "u", z < 3))
            pl.when(z + k <= 3)(lambda: f(z + k, "d", z > 0))

    def middle(p):
        send("x", y, one(p), r1, r2, middle_sent, m_sem + p)
        send("y", y, one(p), r2, r3, middle_sent, m_sem + p)

    def start():
        send("x", y, one(z), 0, r1, start_sent, f_sem)
        send("y", y, one(z), r3, rows, start_sent, f_sem)
        if r3 > r1:
            pl.when(z < 3)(lambda: send("u", y, one(z), r1, r3, single_sent, zs_sem + z))
            pl.when(z > 0)(lambda: send("d", y, one(z), r1, r3, single_sent, zs_sem + z))
            middle(z)

    def pair(way, p):
        send(way, y, two(p), 0, r1, pair_sent, zp_sem + p)
        send(way, every, one(p), r3, rows, pair_sent, zp_sem + p)

    def first_hop():
        net.recv(V(y, one(z), 0, ends), f_sem)
        pl.when(z < 3)(lambda: pair("u", z))
        pl.when(z > 0)(lambda: pair("d", z))

    def single_hop(k):
        def hop(p, way, more):
            net.recv(V(y, one(p), r1, r3), zs_sem + p)
            if k < 3:
                pl.when(more)(lambda: send(way, y, one(p), r1, r3, single_sent, zs_sem + p))
            middle(p)

        sides(k, hop)

    def pair_hop(k):
        def hop(p, way, more):
            net.recv(V(y, two(p), 0, ends), zp_sem + p)
            if k < 3:
                pl.when(more)(lambda: pair(way, p))

        sides(k, hop)

    def last_hop(k):
        def hop(p, way, more):
            if r3 > r1:
                net.recv(V(y, one(p), r1, r3), m_sem + p)
            send("y", y, two(p), 0, r2, last_sent, l_sem + p)
            send("x", every, one(p), r2, rows, last_sent, l_sem + p)

        sides(k, hop)

    def to_core(k):
        def hop(p, way, more):
            net.recv(V(y, two(p), 0, rows), l_sem + p)
            send("c", every, two(p), 0, rows, core_sent, c_sem)

        sides(k, hop)

    def from_core(k):
        if k == 3:
            net.recv(V(every, every, 0, rows, other=True), c_sem)

    def finish():
        net.wait_sent(V(y, one(z), 0, ends), start_sent)
        net.wait_sent(V(y, every, 0, rows), last_sent)
        net.wait_sent(V(every, every, 0, rows), core_sent)
        if r3 > r1:
            net.wait_sent(V(y, pl.ds(0, 4), r1, r3), middle_sent)

        def along(count):
            if r3 > r1:
                net.wait_sent(V(y, pl.ds(0, count), r1, r3), single_sent)
            total = 2 * ends * count
            yy, blocks = min(
                (yy, n) for yy in (1, 2) for n in range(1, 9) if total % (yy * n * 16) == 0 and total // (yy * n) <= rows
            )
            net.wait_sent(V(y if yy == 1 else every, pl.ds(0, blocks), 0, total // (yy * blocks)), pair_sent)

        inner = jnp.logical_and(z > 0, z < 3)
        pl.when(inner)(lambda: along(5))
        pl.when(jnp.logical_not(inner))(lambda: along(1))

    kinds = (start, first_hop, single_hop, pair_hop, last_hop, to_core, from_core)
    return [f if i < 2 else functools.partial(f, k) for i, f in enumerate(kinds) for k in range(4)], finish


def nn(a, b):
    return lax.dot_general(a, b, (((1,), (0,)), ((), ())), preferred_element_type=F32)


def nt(a, b):
    return lax.dot_general(a, b, (((1,), (1,)), ((), ())), preferred_element_type=F32)


def tn(a, b):
    return lax.dot_general(a, b, (((0,), (0,)), ((), ())), preferred_element_type=F32)


def norm_parts(v):
    centre = jnp.mean(v, axis=-1, keepdims=True)
    shifted = v - centre
    spread = jnp.mean(shifted * shifted, axis=-1, keepdims=True)
    scaled = lax.rsqrt(spread + eps_norm)
    return shifted * scaled, scaled


def norm_back(normal, scaled, gain, upstream):
    weighted = upstream * gain
    return scaled * (
        weighted
        - jnp.mean(weighted, axis=-1, keepdims=True)
        - normal * jnp.mean(weighted * normal, axis=-1, keepdims=True)
    )


def keep(lanes, low, high):
    return jnp.where(lanes, low, high)


def layer_kernel(
    patches, lengths_in, tasks_in, master, first_moment, second_moment, gain_one, gain_two, qkv_in, out_in, u_in, d_in,
    cot_hbm, out_block, out_patch, out_task, out_stats, MIN, FIRST, SECOND,
    GP, GA, GDS, GUS, LOC, SEL, RES, N1, QKV, PT, CTX, RES2, N2, NRM1, NRM2, SC1, SC2, COT, BACK, ACT, GU, MACC, GACC, G2, G2B, DM, DC, LEADR,
    PAIR, PIN, SEND, RECV, ONEHOT, SREC, STSUM, QIN, OIN, GIN, lengths, tasks, own_sem, local_sem, send_sem, recv_sem, all_sem,
):
    net = Net(send_sem, recv_sem)
    z, x, y, c, dp, mp = net.z, net.x, net.y, net.c, net.dp, net.mp
    device = dp * 4 + mp

    barrier = pltpu.get_barrier_semaphore()
    for way, cond in (("x", None), ("y", None), ("c", None), ("u", lambda: z < 3), ("d", lambda: z > 0)):
        run_if(
            cond,
            lambda way=way: pl.semaphore_signal(
                barrier, inc=1, device_id=net.peer[way], device_id_type=MESH
            ),
        )

    def own_cols(w):
        return pl.ds(pl.multiple_of(c * w, 128), w)

    cot_copy = pltpu.make_async_copy(cot_hbm.at[pl.ds(mp * IMGS, IMGS)], COT, local_sem.at[0])
    copies = []
    for refs, widths, weight_in in ((GDS, DOWNS, d_in), (GUS, UPS, u_in)):
        first = 0
        for ref, w in zip(refs, widths):
            copies.append(
                pltpu.make_async_copy(
                    weight_in.at[:, pl.ds(first, w)], ref.at[0, y, dp, :, own_cols(w)], own_sem.at[len(copies)]
                )
            )
            first += w
    for copy in copies:
        copy.start()
    patch_copy = pltpu.make_async_copy(patches, PIN, local_sem.at[1])
    small = [
        pltpu.make_async_copy(src, dst, own_sem.at[len(copies) + i])
        for i, (src, dst) in enumerate(
            ((qkv_in, QIN), (out_in, OIN), (master, MIN), (gain_one, GIN.at[0]), (gain_two, GIN.at[1]),
             (lengths_in, lengths), (tasks_in, tasks))
        )
    ]
    for copy in small:
        copy.start()
    patch_copy.start()
    cot_copy.start()
    moments = [
        pltpu.make_async_copy(first_moment, FIRST, local_sem.at[2]),
        pltpu.make_async_copy(second_moment, SECOND, local_sem.at[3]),
    ]
    for copy in moments:
        copy.start()
    for copy in small:
        copy.wait()

    qkv = [QIN[i].astype(F32) for i in range(3)]
    outs = OIN[...].astype(F32).T
    low = lax.broadcasted_iota(jnp.int32, (96, 128), 1) < HEAD_DIM

    def tail(v, high):
        v = jnp.concatenate([v[:, 128:192], v[:, 128:192]], axis=1)
        return v

    tiles = [qkv[0][:, 0:128], qkv[1][:, 0:128], qkv[2][:, 0:128]]
    tiles.append(jnp.where(low, tail(qkv[0], 0), tail(qkv[2], 1)))
    tiles.append(jnp.where(low, tail(qkv[1], 0), tail(outs, 1)))
    tiles.append(outs[:, 0:128])
    GA[0, pl.ds(y, 1), pl.ds(dp, 1), :, own_cols(D)] = (
        jnp.concatenate(tiles, axis=1).astype(BF16)[None, None]
    )

    LOC[:, 0:PART] = MIN[...]
    lane = lax.broadcasted_iota(jnp.int32, (TASKS, PADP - PART), 1)
    LOC[:, PART:PADP] = jnp.where(
        lane == 0, tasks[0, 0].astype(F32), jnp.where(lane == 1, tasks[0, 1].astype(F32), 0.0)
    )
    half = PADP // 2
    GP[0, pl.ds(y, 1), pl.ds(dp, 1), :, own_cols(half)] = (
        jnp.concatenate([LOC[:, 0:half], LOC[:, half:PADP]], axis=0).astype(BF16)[None, None]
    )
    for copy in copies:
        copy.wait()
    inner = jnp.logical_and(z > 0, z < 3)
    run_if(lambda: inner, lambda: pl.semaphore_wait(barrier, 5))
    run_if(lambda: jnp.logical_not(inner), lambda: pl.semaphore_wait(barrier, 4))

    gathers = [gather_events(net, GP, half, (16, 16, 16, 16))]
    for ref, w, split in zip((GA, *GDS, *GUS), (D, *DOWNS, *UPS), SPLITS):
        gathers.append(gather_events(net, ref, w, split))

    g1 = GIN[0].reshape(1, D)
    g2 = GIN[1].reshape(1, D)
    limits = [lengths[b] + LEAD for b in range(IMGS)]
    live = [
        (lax.broadcasted_iota(jnp.int32, (ROWS, 1), 0) < limits[b]).astype(F32) for b in range(IMGS)
    ]

    def place_rows():
        patch_copy.wait()
        cot_copy.wait()
        for copy in moments:
            copy.wait()
        for b in range(IMGS):
            RES[b, LEAD:ROWS, :] = PIN[:, b, :].astype(F32)

    task_rows = lax.broadcasted_iota(jnp.int32, (TASKS, 1), 0)

    columns = lax.broadcasted_iota(jnp.int32, (TASKS, 128), 1)

    def pick(d, _):
        dd, mm = d // 4, d % 4
        raw = GP[0, mm // 2, dd, :, pl.ds(pl.multiple_of((mm % 2) * half, 128), half)].astype(F32)
        low, high = raw[0:8], raw[8:16]
        rep, j = d // 16, d % 16
        for b in range(IMGS):
            hot = (task_rows == tasks[0, b]).astype(F32)
            row = 2 * rep + b
            SEL[j, pl.ds(row, 1), 0:half] = jnp.sum(low * hot, axis=0, keepdims=True)
            SEL[j, pl.ds(row, 1), half:PADP] = jnp.sum(high * hot, axis=0, keepdims=True)
        base = PART - half
        for b in range(IMGS):
            which = high[0:1, base + b : base + b + 1]
            hot = (lax.broadcasted_iota(jnp.int32, (TASKS, 128), 0).astype(F32) == which).astype(F32)
            for h in range(2):
                ONEHOT[h] += jnp.where(columns == 2 * IMGS * d + 2 * b + h, hot, 0.0)
        return 0

    def place_prompts():
        ONEHOT[...] = jnp.zeros_like(ONEHOT)
        lax.fori_loop(0, NDEV, pick, 0)
        wide = lax.broadcasted_iota(jnp.int32, (4, D), 1)
        for r in range(25):
            j, off = (D * r) // PART, (D * r) % PART
            first = min(D, PART - off)
            low = SEL[j, 0:4, :]
            seg = (pltpu.roll(low, PADP - off, 1) if off else low)[:, 0:D]
            if first < D:
                seg = jnp.where(wide < first, seg, pltpu.roll(SEL[j + 1, 0:4, :], first, 1)[:, 0:D])
            for rep in range(2):
                for b in range(IMGS):
                    RES[b, 25 * rep + r : 25 * rep + r + 1, :] = seg[2 * rep + b : 2 * rep + b + 1]

    def norm_one():
        for b in range(IMGS):
            normal, SC1[b] = norm_parts(RES[b])
            NRM1[b] = normal
            N1[b] = (normal * g1).astype(BF16)

    def weight(ref, core, first, width, span):
        cols = pl.ds(pl.multiple_of(core * span + first, 128), width)
        return ref[:, :, cols].reshape(D, width)

    left = lax.broadcasted_iota(jnp.int32, (ROWS, 128), 1) < HEAD_DIM
    scale = 1.0 / math.sqrt(HEAD_DIM)
    wide = lax.broadcasted_iota(jnp.int32, (1, 640), 1)
    q_scale = jnp.where((wide < 128) | ((wide >= 384) & (wide < 448)), scale, 1.0)

    def project(m):
        w = weight(GA.at[0, m // 2], m % 2, 0, 640, D)
        mixed = nn(N1[...].reshape(IMGS * ROWS, D), w) * q_scale
        QKV[m] = mixed.astype(BF16).reshape(IMGS, ROWS, 640)

    key_rows = lax.broadcasted_iota(jnp.int32, (ROWS, ROWS), 0)
    zero = jnp.zeros((), BF16)

    def attend(t):
        b, m = t // 4, t % 4
        tile = lambda i: QKV[m, b, :, 128 * i : 128 * i + 128]
        q01, k01, v01, q2v2, k2 = (tile(i) for i in range(5))
        mask = key_rows < (lengths[b] + LEAD)

        def soft(keys, queries):
            s = jnp.where(mask, nt(keys, queries), -1e30)
            e = jnp.exp(s - jnp.max(s, axis=0, keepdims=True))
            return (e * (1.0 / jnp.sum(e, axis=0, keepdims=True))).astype(BF16)

        p0 = soft(k01, keep(left, q01, zero))
        p1 = soft(k01, keep(left, zero, q01))
        p2 = soft(k2, keep(left, q2v2, zero))
        PT[t, 0], PT[t, 1], PT[t, 2] = p0, p1, p2
        CTX[b, :, m * 256 : m * 256 + 128] = keep(left, 0.0, tn(p2, q2v2)).astype(BF16)
        CTX[b, :, m * 256 + 128 : m * 256 + 256] = keep(
            left, tn(p0, v01), tn(p1, v01)
        ).astype(BF16)

    def attend_two(t):
        attend(2 * t)
        attend(2 * t + 1)

    sums = [jnp.zeros((1, 1), F32) for _ in range(3)]

    def total(v):
        return jnp.sum(jnp.sum(v, axis=0, keepdims=True), axis=1, keepdims=True)

    def project_out(b):
        attn = jnp.zeros((ROWS, D), F32)
        for m in range(4):
            attn += nt(CTX[b, :, 256 * m : 256 * m + 256], weight(GA.at[0, m // 2], m % 2, 512, 256, D))
        sums[1] += total(attn * attn * live[b])
        res2 = RES[b] + attn
        RES2[b] = res2
        normal, SC2[b] = norm_parts(res2)
        NRM2[b] = normal
        N2[b] = (normal * g2).astype(BF16)

    def back_units(i, yy):
        w, first = DOWNS[i], sum(DOWNS[:i])
        cot = COT[...].reshape(IMGS * ROWS, D)
        for core in range(2):
            back = nn(cot, weight(GDS[i].at[0, yy], core, 0, w, w))
            BACK[yy, :, core * D + first : core * D + first + w] = back.astype(BF16)

    def up_units(i, core):
        w, first = UPS[i], sum(UPS[:i])
        rows2 = N2[...].reshape(IMGS * ROWS, D)
        here = pl.ds(pl.multiple_of(core * w, 128), w)
        for yy in range(2):
            up = nn(rows2, weight(GUS[i].at[0, yy], core, 0, w, w))
            back = BACK[yy, :, pl.ds(pl.multiple_of(core * D + first, 128), w)].astype(F32)
            cumul = 0.5 * (1.0 + lax.erf(up * 0.7071067811865476))
            density = jnp.exp(-0.5 * up * up) * 0.3989422804014327
            ACT[yy, :, here] = (up * cumul).astype(BF16)
            GU[yy, :, here] = (back * (cumul + up * density)).astype(BF16)

    def add_grad(i, yy):
        w = UPS[i]
        grad = nt(GU[yy, :, 0 : 2 * w], weight(GUS[i].at[0, yy], 0, 0, 2 * w, w)).reshape(IMGS, ROWS, D)
        if i == 0 and yy == 0:
            GACC[...] = grad
        else:
            GACC[...] += grad

    def add_mlp(i, yy):
        w, first = UPS[i], sum(UPS[:i])
        d = max(d for d in range(len(DOWNS)) if sum(DOWNS[:d]) <= first)
        inside = first - sum(DOWNS[:d])
        if w == DOWNS[d]:
            mlp = nt(ACT[yy, :, 0 : 2 * w], weight(GDS[d].at[0, yy], 0, 0, 2 * w, w))
        else:
            mlp = sum(
                nt(ACT[yy, :, w * core : w * (core + 1)], weight(GDS[d].at[0, yy], core, inside, w, DOWNS[d]))
                for core in range(2)
            )
        mlp = mlp.reshape(IMGS, ROWS, D)
        if i == 0 and yy == 0:
            MACC[...] = mlp
        else:
            MACC[...] += mlp

    def add_units(i, yy):
        add_grad(i, yy)
        if i < len(UPS) - 1:
            add_mlp(i, yy)

    steps = [place_rows, place_prompts, norm_one]
    steps += [functools.partial(project, m) for m in range(4)]
    steps += [functools.partial(attend_two, t) for t in range(4)]
    steps += [functools.partial(project_out, b) for b in range(IMGS)]
    steps += [functools.partial(back_units, i, yy) for i in range(len(DOWNS)) for yy in range(2)]
    for i in range(len(UPS)):
        steps += [functools.partial(up_units, i, c), functools.partial(up_units, i, 1 - c)]
        steps += [functools.partial(add_units, i, yy) for yy in range(2)]
    for item in ORDER:
        if item < 1000:
            gathers[item // 28][0][item % 28]()
        else:
            steps[item - 1000]()

    for b in range(IMGS):
        g = COT[b].astype(F32) + norm_back(NRM2[b], SC2[b], g2, GACC[b])
        G2[b] = g
        G2B[b] = g.astype(BF16)

    for m in range(4):
        cols = pl.ds(pl.multiple_of((m % 2) * D + 512, 128), 256)
        w = GA[0, m // 2, :, :, cols].reshape(D, 256)
        DC[m] = nn(G2B[...].reshape(IMGS * ROWS, D), w).astype(BF16).reshape(IMGS, ROWS, 256)

    def attend_back(b):
        tiles, grad_probs, grad_scores = [], [], []
        for m in range(4):
            tiles.append(
                [QKV[m, b, :, 128 * i : 128 * i + 128] for i in range(5)]
                + [DC[m, b, :, 0:128], DC[m, b, :, 128:256]]
            )
            q01, k01, v01, q2v2, k2, c2, c01 = tiles[m]
            grad_probs.append(
                [nt(keep(left, v01, zero), c01), nt(keep(left, zero, v01), c01), nt(keep(left, zero, q2v2), c2)]
            )
        for m in range(4):
            out = []
            for h in range(3):
                pf, dp_ = PT[4 * b + m, h].astype(F32), grad_probs[m][h]
                inner = jnp.sum(pf * dp_, axis=0, keepdims=True)
                out.append((pf * (dp_ - inner)).astype(BF16))
            grad_scores.append(out)
        for m in range(4):
            q01, k01, v01, q2v2, k2, c2, c01 = tiles[m]
            s0, s1, s2 = grad_scores[m]
            p0, p1, p2 = (PT[4 * b + m, h] for h in range(3))
            DM[m, b, :, 0:128] = (keep(left, tn(s0, k01), tn(s1, k01)) * scale).astype(BF16)
            DM[m, b, :, 128:256] = keep(left, nn(s0, q01), nn(s1, q01)).astype(BF16)
            DM[m, b, :, 256:384] = keep(left, nn(p0, c01), nn(p1, c01)).astype(BF16)
            DM[m, b, :, 384:512] = keep(left, tn(s2, k2) * scale, nn(p2, c2)).astype(BF16)
            DM[m, b, :, 512:640] = keep(left, nn(s2, q2v2), 0.0).astype(BF16)

    def grad_rows(rows, first, last):
        count = last - first
        grad = jnp.zeros((len(rows) * count, D), F32)
        for m in range(4):
            mixed = jnp.concatenate([DM[m, b, first:last] for b in rows], axis=0)
            grad += nt(mixed, weight(GA.at[0, m // 2], m % 2, 0, 640, D))
        for i, b in enumerate(rows):
            part = grad[count * i : count * (i + 1)]
            GACC[b, first:last] = G2[b, first:last] + norm_back(NRM1[b, first:last], SC1[b, first:last], g1, part)

    def to_others(src, dst, sems):
        for step in (4, 5, 3, 6, 2, 7, 1, 0):
            to_dp = (dp + step) & 7
            for turn in range(4):
                if step or turn:
                    to_mp = (mp + turn) & 3
                    pltpu.make_async_remote_copy(
                        src_ref=src(to_dp * 4 + to_mp),
                        dst_ref=dst,
                        send_sem=all_sem.at[sems],
                        recv_sem=all_sem.at[sems + 1],
                        device_id=(to_dp, to_mp),
                        device_id_type=MESH,
                    ).start()

    wide = lax.broadcasted_iota(jnp.int32, (4, PADP), 1)

    def to_owners():
        for rep in range(2):
            for b in range(IMGS):
                LEADR[:, 2 * rep + b : 2 * rep + b + 1, :] = GACC[b, 25 * rep : 25 * rep + 25, :][:, None, :]
        for q in range(16):
            r, off = (PART * q) // D, (PART * q) % D
            msg, have = None, -off
            while have < PART:
                row = LEADR[r]
                moved = pltpu.roll(row, have % D, 1) if have % D else row
                moved = jnp.concatenate([moved, moved[:, 0 : PADP - D]], axis=1)
                msg = moved if msg is None else jnp.where(wide < have, msg, moved)
                have += D
                r += 1
            msg = jnp.where(wide < PART, msg, 0.0).astype(BF16)
            for rep in range(2):
                SEND[16 * rep + q] = jnp.concatenate(
                    [msg[2 * rep + b : 2 * rep + b + 1, half * h : half * h + half] for b in range(IMGS) for h in range(2)],
                    axis=0,
                )
        to_others(lambda other: SEND.at[other], RECV.at[device], 0)
        RECV[pl.ds(device, 1)] = SEND[pl.ds(device, 1)]

    def others(ref):
        return ref.at[pl.ds(0, NDEV - 1)]

    def wait_all(ref, sem):
        pltpu.make_async_copy(others(ref), others(ref), all_sem.at[sem]).wait()

    some = 64
    for b in range(IMGS):
        attend_back(b)
    grad_rows((0, 1), 0, some)
    to_owners()

    grad_rows((0, 1), some, ROWS)
    for yy in range(2):
        add_mlp(len(UPS) - 1, yy)
    for b in range(IMGS):
        mlp = MACC[b]
        block = RES2[b] + mlp
        out_block[b] = block.astype(BF16)
        sums[0] += total(block * block * live[b])
        sums[2] += total(mlp * mlp * live[b])

    wait_all(RECV, 1)

    came = RECV[...].reshape(2 * IMGS * NDEV, half)
    acc = [nn(ONEHOT[h].astype(BF16), came) for h in range(2)]
    square = total(acc[0] * acc[0]) + total(acc[1] * acc[1])
    lane = lax.broadcasted_iota(jnp.int32, (1, 128), 1)
    count = (limits[0] + limits[1]).astype(F32)
    stats = jnp.zeros((1, 128), F32)
    for i, v in enumerate((square, sums[0], sums[1], sums[2], count)):
        stats = jnp.where(lane == i, v, stats)
    STSUM[...] = stats
    SREC[pl.ds(device, 1)] = stats[None]
    to_others(lambda other: STSUM, SREC.at[device], 2)

    out_task[...] = jnp.concatenate(acc, axis=1)[:, 0:PART]
    for b in range(IMGS):
        PAIR[:, b : b + 1, :] = GACC[b, LEAD:ROWS, :][:, None, :]
    out_patch[...] = PAIR[...].astype(BF16)
    wait_all(RECV, 0)
    for gather in gathers:
        gather[1]()
    wait_all(SREC, 3)
    out_stats[...] = jnp.sum(SREC[...], axis=0)
    wait_all(SREC, 2)


def update_kernel(
    task_grad, stats, master, first_moment, second_moment, block_in, patch_in,
    out_grad, out_first, out_second, out_master, out_copy, out_norm, out_rms, block_out, patch_out, sem,
):
    copies = [
        pltpu.make_async_copy(block_in, block_out, sem.at[0]),
        pltpu.make_async_copy(patch_in, patch_out, sem.at[1]),
    ]
    for copy in copies:
        copy.start()
    st = stats[0:1, :]
    norm = jnp.sqrt(st[0:1, 0:1])
    grad = task_grad[...] * (clip_level / jnp.maximum(norm, clip_level))
    first = beta_one * first_moment[...] + (1.0 - beta_one) * grad
    second = beta_two * second_moment[...] + (1.0 - beta_two) * grad * grad
    step_size = (
        first / (1.0 - beta_one**STEP) / (jnp.sqrt(second / (1.0 - beta_two**STEP)) + adam_eps)
    )
    old = master[...]
    new = old - learn_rate * (step_size + decay_rate * old)
    out_grad[...] = grad
    out_first[...] = first
    out_second[...] = second
    out_master[...] = new
    out_copy[...] = new.astype(BF16)
    out_norm[0] = norm[0, 0]
    rms = jnp.sqrt(st / (st[0:1, 4:5] * D))
    for i in range(3):
        out_rms[i] = rms[0, i + 1]
    for copy in copies:
        copy.wait()


def fast_body(
    patches, lengths, tasks, prompt_master, first_moment, second_moment,
    gain_one, gain_two, w_qkv, w_out, w_up, w_down, cotangent,
):
    vmem = pl.BlockSpec(memory_space=pltpu.VMEM)
    smem = pl.BlockSpec(memory_space=pltpu.SMEM)
    anywhere = pl.BlockSpec(memory_space=pl.ANY)
    V = pltpu.VMEM
    block, patch, *states = pl.pallas_call(
        layer_kernel,
        out_shape=[
            V((IMGS, ROWS, D), BF16),
            V((PATCH, IMGS, D), BF16),
            V((TASKS, PART), F32),
            V((1, 128), F32),
        ]
        + [V((TASKS, PART), F32)] * 3,
        in_specs=[anywhere] * 13,
        out_specs=[vmem] * 7,
        scratch_shapes=[
            V((1, 2, 8, 16, PADP), BF16),
            V((1, 2, 8, 96, 2 * D), BF16),
            [V((1, 2, 8, 96, 2 * w), BF16) for w in DOWNS],
            [V((1, 2, 8, 96, 2 * w), BF16) for w in UPS],
            V((TASKS, PADP), F32),
            V((16, 4, PADP), F32),
            V((IMGS, ROWS, D), F32),
            V((IMGS, ROWS, D), BF16),
            V((4, IMGS, ROWS, 640), BF16),
            V((8, 3, ROWS, ROWS), BF16),
            V((IMGS, ROWS, 1024), BF16),
            V((IMGS, ROWS, D), F32),
            V((IMGS, ROWS, D), BF16),
            V((IMGS, ROWS, D), F32),
            V((IMGS, ROWS, D), F32),
            V((IMGS, ROWS, 1), F32),
            V((IMGS, ROWS, 1), F32),
            V((IMGS, ROWS, D), BF16),
            V((2, IMGS * ROWS, 2 * D), BF16),
            V((2, IMGS * ROWS, 2 * max(UPS)), BF16),
            V((2, IMGS * ROWS, 2 * max(UPS)), BF16),
            V((IMGS, ROWS, D), F32),
            V((IMGS, ROWS, D), F32),
            V((IMGS, ROWS, D), F32),
            V((IMGS, ROWS, D), BF16),
            V((4, IMGS, ROWS, 640), BF16),
            V((4, IMGS, ROWS, 256), BF16),
            V((25, 4, D), F32),
            V((PATCH, IMGS, D), F32),
            V((PATCH, IMGS, D), BF16),
            V((NDEV, 2 * IMGS, PADP // 2), BF16),
            V((NDEV, 2 * IMGS, PADP // 2), BF16),
            V((2, TASKS, 128), F32),
            V((NDEV, 1, 128), F32),
            V((1, 128), F32),
            V((3, 96, 192), BF16),
            V((192, 96), BF16),
            V((2, D), F32),
            pltpu.SMEM((IMGS,), jnp.int32),
            pltpu.SMEM((1, IMGS), jnp.int32),
            pltpu.SemaphoreType.DMA((7 + len(DOWNS) + len(UPS),)),
            pltpu.SemaphoreType.DMA((4,)),
            pltpu.SemaphoreType.DMA((6 * (2 + len(DOWNS) + len(UPS)),)),
            pltpu.SemaphoreType.DMA((10 + 18 * (1 + len(DOWNS) + len(UPS)),)),
            pltpu.SemaphoreType.DMA((4,)),
        ],
        compiler_params=pltpu.CompilerParams(
            collective_id=0, has_side_effects=True, vmem_limit_bytes=58 << 20
        ),
    )(
        patches.transpose(1, 0, 2), lengths, tasks.T, prompt_master, first_moment, second_moment, gain_one, gain_two,
        w_qkv.transpose(1, 0, 2), w_out, w_up, w_down.T, cotangent,
    )
    state = jax.ShapeDtypeStruct((TASKS, PART), F32)

    def keep_near(v):
        return pltpu.with_memory_space_constraint(v, pltpu.VMEM)

    grad, first, second, master, copy, norm, rms, block_out, patch_out = pl.pallas_call(
        update_kernel,
        out_shape=[state] * 4
        + [
            jax.ShapeDtypeStruct((TASKS, PART), BF16),
            jax.ShapeDtypeStruct((1,), F32),
            jax.ShapeDtypeStruct((3,), F32),
            jax.ShapeDtypeStruct((IMGS, ROWS, D), BF16),
            jax.ShapeDtypeStruct((PATCH, IMGS, D), BF16),
        ],
        in_specs=[vmem] * 7,
        out_specs=[vmem] * 5 + [smem] * 2 + [anywhere] * 2,
        scratch_shapes=[pltpu.SemaphoreType.DMA((2,))],
    )(*(keep_near(v) for v in (*states, block, patch)))
    return (
        block_out, patch_out.transpose(1, 0, 2), grad, norm.reshape(()), first, second, master, copy, rms,
    )


def layer_norm(values, gain):
    centre = jnp.mean(values, axis=-1, keepdims=True)
    shifted = values - centre
    spread = jnp.mean(shifted * shifted, axis=-1, keepdims=True)
    return shifted * lax.rsqrt(spread + eps_norm) * gain


def whole_norm_back(values, gain, upstream):
    centre = jnp.mean(values, axis=-1, keepdims=True)
    shifted = values - centre
    spread = jnp.mean(shifted * shifted, axis=-1, keepdims=True)
    scaled = lax.rsqrt(spread + eps_norm)
    normal_part = shifted * scaled
    weighted = upstream * gain
    return scaled * (
        weighted
        - jnp.mean(weighted, axis=-1, keepdims=True)
        - normal_part * jnp.mean(weighted * normal_part, axis=-1, keepdims=True)
    )


def gelu_slope(upward):
    cumul = 0.5 * (1.0 + lax.erf(upward * 0.7071067811865476))
    density = jnp.exp(-0.5 * upward * upward) * 0.3989422804014327
    return cumul + upward * density


def attend_forward(group_normed, group_limit, w_mix, block_images):
    group_size, row_count, feature_count = group_normed.shape
    lane_width = w_mix.shape[2]
    head_count = lane_width // HEAD_DIM
    scale = 1.0 / math.sqrt(HEAD_DIM)
    mask_all = jnp.arange(row_count, dtype=jnp.int32)[None, :] < group_limit[:, None]

    def one_block(block_index):
        first_row = block_index * block_images
        block_in = lax.dynamic_slice_in_dim(group_normed, first_row, block_images, 0)
        key_mask = lax.dynamic_slice_in_dim(mask_all, first_row, block_images, 0)
        mixed_qkv = jnp.einsum(
            "brd,dce->brce", block_in, w_mix, preferred_element_type=jnp.float32
        ).astype(jnp.bfloat16)
        split_heads = mixed_qkv.reshape(block_images, row_count, 3, head_count, HEAD_DIM)
        scores = (
            jnp.einsum(
                "bqhe,bkhe->bhqk",
                split_heads[:, :, 0],
                split_heads[:, :, 1],
                preferred_element_type=jnp.float32,
            )
            * scale
        )
        scores = jnp.where(key_mask[:, None, None, :], scores, -1e30)
        row_top = jnp.max(scores, axis=-1, keepdims=True)
        exponent = jnp.exp(scores - row_top)
        row_total = jnp.sum(exponent, axis=-1, keepdims=True)
        attend_weights = (exponent / row_total).astype(jnp.bfloat16)
        context = jnp.einsum(
            "bhqk,bkhe->bqhe",
            attend_weights,
            split_heads[:, :, 2],
            preferred_element_type=jnp.float32,
        )
        context = context.astype(jnp.bfloat16).reshape(block_images, row_count, lane_width)
        return (mixed_qkv, context, (row_top + jnp.log(row_total))[..., 0])

    mixed_qkv, context, logsums = lax.map(
        one_block, jnp.arange(group_size // block_images, dtype=jnp.int32)
    )
    return (
        mixed_qkv.reshape(group_size, row_count, 3, lane_width),
        context.reshape(group_size, row_count, lane_width),
        logsums.reshape(group_size, head_count, row_count),
    )


def attend_back(mixed_qkv, logsums, group_limit, grad_context, block_images):
    group_size, row_count, three_parts, lane_width = mixed_qkv.shape
    head_count = lane_width // HEAD_DIM
    scale = 1.0 / math.sqrt(HEAD_DIM)
    mask_all = jnp.arange(row_count, dtype=jnp.int32)[None, :] < group_limit[:, None]

    def one_block(block_index):
        first_row = block_index * block_images
        split_heads = lax.dynamic_slice_in_dim(mixed_qkv, first_row, block_images, 0).reshape(
            block_images, row_count, 3, head_count, HEAD_DIM
        )
        queries = split_heads[:, :, 0]
        keys_all = split_heads[:, :, 1]
        values = split_heads[:, :, 2]
        key_mask = lax.dynamic_slice_in_dim(mask_all, first_row, block_images, 0)
        logsum = lax.dynamic_slice_in_dim(logsums, first_row, block_images, 0)
        grad_out = lax.dynamic_slice_in_dim(grad_context, first_row, block_images, 0).reshape(
            block_images, row_count, head_count, HEAD_DIM
        )
        scores = (
            jnp.einsum("bqhe,bkhe->bhqk", queries, keys_all, preferred_element_type=jnp.float32)
            * scale
        )
        scores = jnp.where(key_mask[:, None, None, :], scores, -1e30)
        attend_weights = jnp.exp(scores - logsum[..., None])
        grad_weights = jnp.einsum(
            "bqhe,bkhe->bhqk", grad_out, values, preferred_element_type=jnp.float32
        )
        row_inner = jnp.sum(attend_weights * grad_weights, axis=-1, keepdims=True)
        grad_scores = (attend_weights * (grad_weights - row_inner)).astype(jnp.bfloat16)
        grad_query = (
            jnp.einsum("bhqk,bkhe->bqhe", grad_scores, keys_all, preferred_element_type=jnp.float32)
            * scale
        )
        grad_key = (
            jnp.einsum("bhqk,bqhe->bkhe", grad_scores, queries, preferred_element_type=jnp.float32)
            * scale
        )
        grad_value = jnp.einsum(
            "bhqk,bqhe->bkhe",
            attend_weights.astype(jnp.bfloat16),
            grad_out,
            preferred_element_type=jnp.float32,
        )
        stacked = jnp.stack([grad_query, grad_key, grad_value], axis=2).astype(jnp.bfloat16)
        return stacked.reshape(block_images, row_count, 3, lane_width)

    grad_mixed = lax.map(one_block, jnp.arange(group_size // block_images, dtype=jnp.int32))
    return grad_mixed.reshape(group_size, row_count, 3, lane_width)


def expand_units(group_two, w_expand, block_images):
    group_size, row_count, feature_count = group_two.shape

    def one_block(block_index):
        block_in = lax.dynamic_slice_in_dim(group_two, block_index * block_images, block_images, 0)
        upward = jnp.einsum("brd,df->brf", block_in, w_expand, preferred_element_type=jnp.float32)
        return jax.nn.gelu(upward, approximate=False).astype(jnp.bfloat16)

    act_units = lax.map(one_block, jnp.arange(group_size // block_images, dtype=jnp.int32))
    return act_units.reshape(group_size, row_count, w_expand.shape[1])


def units_back(grad_group, group_two, w_expand, w_reduce, block_images):
    group_size, row_count, feature_count = group_two.shape

    def one_block(block_index):
        first_row = block_index * block_images
        grad_in = lax.dynamic_slice_in_dim(grad_group, first_row, block_images, 0)
        norm_in = lax.dynamic_slice_in_dim(group_two, first_row, block_images, 0)
        back_units = jnp.einsum(
            "brd,fd->brf", grad_in, w_reduce, preferred_element_type=jnp.float32
        )
        upward = jnp.einsum("brd,df->brf", norm_in, w_expand, preferred_element_type=jnp.float32)
        return (back_units * gelu_slope(upward)).astype(jnp.bfloat16)

    grad_units = lax.map(one_block, jnp.arange(group_size // block_images, dtype=jnp.int32))
    return grad_units.reshape(group_size, row_count, w_expand.shape[1])


def rows_term(source, weight, form):
    return jnp.einsum(form, source, weight, preferred_element_type=jnp.float32)


def body(
    patches,
    lengths,
    tasks,
    prompt_master,
    first_moment,
    second_moment,
    gain_one,
    gain_two,
    w_qkv,
    w_out,
    w_up,
    w_down,
    cotangent,
):
    held_count, patch_count, feature_count = patches.shape
    row_count = cotangent.shape[1]
    lead_count = row_count - patch_count
    task_count = prompt_master.shape[0]
    prompt_table = lax.all_gather(
        prompt_master.astype(jnp.bfloat16), ("dp", "mp"), axis=1, tiled=True
    )
    chosen = tasks == jnp.arange(task_count, dtype=jnp.int32)[None, :]
    lead_part = jnp.dot(
        chosen.astype(jnp.bfloat16), prompt_table, preferred_element_type=jnp.float32
    )
    residual = jnp.concatenate(
        [lead_part.reshape(held_count, lead_count, feature_count), patches.astype(jnp.float32)],
        axis=1,
    )
    row_limit = lengths + lead_count
    w_mix, w_expand, w_reduce, w_rows = (
        lax.all_gather(w_qkv, "dp", axis=0, tiled=True),
        lax.all_gather(w_up, "dp", axis=0, tiled=True),
        lax.all_gather(w_down, "dp", axis=1, tiled=True),
        lax.all_gather(w_out, "dp", axis=1, tiled=True),
    )
    normed = layer_norm(residual, gain_one).astype(jnp.bfloat16)
    mp_rank = lax.axis_index("mp")
    group_normed, group_bound = (
        lax.all_gather(normed, "mp", axis=0, tiled=True),
        lax.all_gather(row_limit.astype(jnp.bfloat16), "mp", axis=0, tiled=True),
    )
    group_limit = group_bound.astype(jnp.int32)
    mixed_qkv, context, logsums = attend_forward(group_normed, group_limit, w_mix, held_count)
    attn_out = lax.psum_scatter(
        rows_term(context, w_rows, "brc,cd->brd"), "mp", scatter_dimension=0, tiled=True
    )
    residual_two = residual + attn_out
    normed_two = layer_norm(residual_two, gain_two).astype(jnp.bfloat16)
    group_two = lax.all_gather(normed_two, "mp", axis=0, tiled=True)
    act_units = expand_units(group_two, w_expand, held_count)
    mlp_out = lax.psum_scatter(
        rows_term(act_units, w_reduce, "brf,fd->brd").astype(jnp.bfloat16),
        "mp",
        scatter_dimension=0,
        tiled=True,
    ).astype(jnp.float32)
    block_sum = residual_two + mlp_out
    live_rows = (jnp.arange(row_count, dtype=jnp.int32)[None, :] < row_limit[:, None]).astype(
        jnp.float32
    )[:, :, None]
    square_sums = jnp.stack(
        [
            jnp.sum(block_sum * block_sum * live_rows),
            jnp.sum(attn_out * attn_out * live_rows),
            jnp.sum(mlp_out * mlp_out * live_rows),
        ]
    )
    live_count = jnp.sum(row_limit).astype(jnp.float32)
    w_mix, w_expand, w_reduce, w_rows = (
        lax.all_gather(w_qkv, "dp", axis=0, tiled=True),
        lax.all_gather(w_up, "dp", axis=0, tiled=True),
        lax.all_gather(w_down, "dp", axis=1, tiled=True),
        lax.all_gather(w_out, "dp", axis=1, tiled=True),
    )
    grad_held = lax.dynamic_slice_in_dim(cotangent, mp_rank * held_count, held_count, 0)
    grad_units = units_back(cotangent, group_two, w_expand, w_reduce, held_count)
    grad_normed_two = lax.psum_scatter(
        rows_term(grad_units, w_expand, "brf,df->brd"), "mp", scatter_dimension=0, tiled=True
    )
    grad_two = grad_held.astype(jnp.float32) + whole_norm_back(residual_two, gain_two, grad_normed_two)
    grad_low = grad_two.astype(jnp.bfloat16)
    grad_context = jnp.einsum(
        "brd,cd->brc",
        lax.all_gather(grad_low, "mp", axis=0, tiled=True),
        w_rows,
        preferred_element_type=jnp.float32,
    ).astype(jnp.bfloat16)
    grad_mixed = attend_back(mixed_qkv, logsums, group_limit, grad_context, held_count)
    grad_normed = lax.psum_scatter(
        rows_term(grad_mixed, w_mix, "brce,dce->brd").astype(jnp.bfloat16),
        "mp",
        scatter_dimension=0,
        tiled=True,
    ).astype(jnp.float32)
    grad_residual = grad_two + whole_norm_back(residual, gain_one, grad_normed)
    patch_grad = grad_residual[:, lead_count:].astype(jnp.bfloat16)
    lead_grad = grad_residual[:, :lead_count].reshape(held_count, lead_count * feature_count)
    task_term = jnp.dot(
        chosen.astype(jnp.float32).T,
        lead_grad,
        precision=lax.Precision.HIGHEST,
        preferred_element_type=jnp.float32,
    )
    task_grad = lax.psum_scatter(task_term, ("dp", "mp"), scatter_dimension=1, tiled=True)
    square = jnp.sum(task_grad * task_grad)
    square, square_sums, live_count = lax.psum((square, square_sums, live_count), ("dp", "mp"))
    grad_norm = jnp.sqrt(square)
    prompt_grad = task_grad * (clip_level / jnp.maximum(grad_norm, clip_level))
    new_first = beta_one * first_moment + (1.0 - beta_one) * prompt_grad
    new_second = beta_two * second_moment + (1.0 - beta_two) * prompt_grad * prompt_grad
    step_size = (
        new_first
        / (1.0 - beta_one**STEP)
        / (jnp.sqrt(new_second / (1.0 - beta_two**STEP)) + adam_eps)
    )
    new_master = prompt_master - learn_rate * (step_size + decay_rate * prompt_master)
    rms_stats = jnp.sqrt(square_sums / (live_count * feature_count))
    return (
        block_sum.astype(jnp.bfloat16),
        patch_grad,
        prompt_grad,
        grad_norm,
        new_first,
        new_second,
        new_master,
        new_master.astype(jnp.bfloat16),
        rms_stats,
    )


def solution(mesh):
    small = mesh.shape["dp"] == 8 and mesh.shape["mp"] == 4
    return jax.shard_map(
        fast_body if small else body,
        mesh=mesh,
        in_specs=(
            P(("dp", "mp"), None, None),
            P(("dp", "mp")),
            P(("dp", "mp"), None),
            P(None, ("dp", "mp")),
            P(None, ("dp", "mp")),
            P(None, ("dp", "mp")),
            P(),
            P(),
            P("dp", None, "mp"),
            P("mp", "dp"),
            P("dp", "mp"),
            P("mp", "dp"),
            P("dp", None, None),
        ),
        out_specs=(
            P(("dp", "mp"), None, None),
            P(("dp", "mp"), None, None),
            P(None, ("dp", "mp")),
            P(),
            P(None, ("dp", "mp")),
            P(None, ("dp", "mp")),
            P(None, ("dp", "mp")),
            P(None, ("dp", "mp")),
            P(),
        ),
        check_vma=False,
    )
```

```python
import functools
import math

import jax
import jax.numpy as jnp
from jax import lax
from jax.experimental import pallas as pl
from jax.experimental.pallas import tpu as pltpu
from jax.sharding import PartitionSpec as P

HEAD_DIM = 64
STEP = 10
MESH = pl.DeviceIdType.MESH
F32 = jnp.float32
BF16 = jnp.bfloat16

eps_norm = 1e-06
clip_level = 1.0
beta_one = 0.9
beta_two = 0.999
learn_rate = 3.0
decay_rate = 0.05
adam_eps = 1e-08

D = 768
ROWS = 256
LEAD = 50
PATCH = 206
IMGS = 2
TASKS = 8
PART = 1200
PADP = 1280
NDEV = 32
DOWNS = (512, 256)
UPS = (512, 256)
SPLITS = ((16, 48, 80, 96), (32, 48, 64, 96), (16, 48, 48, 96), (32, 48, 64, 96), (16, 32, 64, 96))
ORDER = (
    28, 56, 0, 1000, 112, 32, 84, 44, 4, 16, 37, 140, 13, 41, 17, 38, 14, 18, 48, 60,
    45, 42, 144, 121, 65, 21, 22, 39, 15, 19, 46, 156, 20, 23, 43, 47, 69, 72, 116, 149,
    49, 27, 1001, 93, 66, 50, 1002, 51, 128, 70, 160, 73, 125, 122, 76, 88, 150, 74, 55, 1003,
    1004, 1005, 67, 129, 1006, 94, 1007, 126, 71, 153, 132, 77, 123, 75, 1008, 78, 130, 1009, 97, 157,
    1010, 79, 127, 131, 1011, 1012, 95, 133, 154, 100, 151, 158, 83, 98, 102, 101, 1013, 134, 1014, 135,
    161, 1017, 99, 155, 104, 103, 159, 139, 1018, 162, 106, 1019, 105, 107, 1020, 111, 163, 1015, 1016, 1021,
    167, 1022, 1023, 1024,
)


def run_if(cond, f):
    if cond is None:
        f()
    else:
        pl.when(cond())(f)


class Net:
    def __init__(self, send_sem, recv_sem):
        self.send_sem, self.recv_sem = send_sem, recv_sem
        self.sends = self.recvs = 0
        dp, mp = lax.axis_index("dp"), lax.axis_index("mp")
        z, x, y, c = dp // 2, dp % 2, mp // 2, mp % 2
        self.z, self.x, self.y, self.c = z, x, y, c
        self.dp, self.mp = dp, mp
        self.peer = {
            "x": (2 * z + 1 - x, mp),
            "y": (dp, (1 - y) * 2 + c),
            "c": (dp, 2 * y + 1 - c),
            "u": (jnp.minimum(2 * z + 2 + x, 6 + x), mp),
            "d": (jnp.maximum(2 * z - 2 + x, x), mp),
        }

    def send(self, way, view, sem, landed):
        pltpu.make_async_remote_copy(
            src_ref=view,
            dst_ref=view,
            send_sem=self.send_sem.at[sem],
            recv_sem=self.recv_sem.at[landed],
            device_id=self.peer[way],
            device_id_type=MESH,
        ).start()

    def recv(self, view, landed):
        pltpu.make_async_copy(view, view, self.recv_sem.at[landed]).wait()

    def wait_sent(self, view, sem):
        pltpu.make_async_copy(view, view, self.send_sem.at[sem]).wait()


def gather_events(net, G, W, split):
    z, x, y, c = net.z, net.x, net.y, net.c
    r1, r2, r3, rows = split
    some = 1 if r3 > r1 else 0
    f_sem = net.recvs
    zp_sem, l_sem = f_sem + 1, f_sem + 4
    c_sem, zs_sem, m_sem = f_sem + 8, f_sem + 9, f_sem + 12
    net.recvs = f_sem + 9 + 7 * some
    start_sent, single_sent, pair_sent, middle_sent, last_sent, core_sent = range(net.sends, net.sends + 6)
    net.sends += 6
    every = slice(None)
    ends = r1 + rows - r3

    def V(yy, d, first, last, other=False):
        core = (1 - c) if other else c
        cols = pl.ds(pl.multiple_of(core * W, 128), W)
        return G.at[:, yy, d, pl.ds(first, last - first), cols]

    def two(p):
        return pl.ds(2 * p, 2)

    def one(p):
        return 2 * p + x

    def send(way, yy, d, first, last, sem, landed):
        if last > first:
            net.send(way, V(yy, d, first, last), sem, landed)

    def sides(k, f):
        if k == 0:
            f(z, None, None)
        else:
            pl.when(z >= k)(lambda: f(z - k, "u", z < 3))
            pl.when(z + k <= 3)(lambda: f(z + k, "d", z > 0))

    def along(sem, p, zz):
        return sem + p - (p > zz).astype(jnp.int32)

    def middle(p):
        send("x", y, one(p), r1, r2, middle_sent, m_sem + p)
        send("y", y, one(p), r2, r3, middle_sent, m_sem + p)

    def start():
        send("x", y, one(z), 0, r1, start_sent, f_sem)
        send("y", y, one(z), r3, rows, start_sent, f_sem)
        if r3 > r1:
            pl.when(z < 3)(lambda: send("u", y, one(z), r1, r3, single_sent, along(zs_sem, z, z + 1)))
            pl.when(z > 0)(lambda: send("d", y, one(z), r1, r3, single_sent, along(zs_sem, z, z - 1)))
            middle(z)

    def pair(way, p):
        landed = along(zp_sem, p, z + 1 if way == "u" else z - 1)
        send(way, y, two(p), 0, r1, pair_sent, landed)
        send(way, every, one(p), r3, rows, pair_sent, landed)

    def first_hop():
        net.recv(V(y, one(z), 0, ends), f_sem)
        pl.when(z < 3)(lambda: pair("u", z))
        pl.when(z > 0)(lambda: pair("d", z))

    def single_hop(k):
        def hop(p, way, more):
            net.recv(V(y, one(p), r1, r3), along(zs_sem, p, z))
            if k < 3:
                on = z + 1 if way == "u" else z - 1
                pl.when(more)(lambda: send(way, y, one(p), r1, r3, single_sent, along(zs_sem, p, on)))
            middle(p)

        sides(k, hop)

    def pair_hop(k):
        def hop(p, way, more):
            net.recv(V(y, two(p), 0, ends), along(zp_sem, p, z))
            if k < 3:
                pl.when(more)(lambda: pair(way, p))

        sides(k, hop)

    def last_hop(k):
        def hop(p, way, more):
            if r3 > r1:
                net.recv(V(y, one(p), r1, r3), m_sem + p)
            send("y", y, two(p), 0, r2, last_sent, l_sem + p)
            send("x", every, one(p), r2, rows, last_sent, l_sem + p)

        sides(k, hop)

    def to_core(k):
        def hop(p, way, more):
            net.recv(V(y, two(p), 0, rows), l_sem + p)
            send("c", every, two(p), 0, rows, core_sent, c_sem)

        sides(k, hop)

    def from_core(k):
        if k == 3:
            net.recv(V(every, every, 0, rows, other=True), c_sem)

    def finish():
        net.wait_sent(V(y, one(z), 0, ends), start_sent)
        net.wait_sent(V(y, every, 0, rows), last_sent)
        net.wait_sent(V(every, every, 0, rows), core_sent)
        if r3 > r1:
            net.wait_sent(V(y, pl.ds(0, 4), r1, r3), middle_sent)

        def chain(count):
            if r3 > r1:
                net.wait_sent(V(y, pl.ds(0, count), r1, r3), single_sent)
            total = 2 * ends * count
            yy, blocks = min(
                (yy, n) for yy in (1, 2) for n in range(1, 9) if total % (yy * n * 16) == 0 and total // (yy * n) <= rows
            )
            net.wait_sent(V(y if yy == 1 else every, pl.ds(0, blocks), 0, total // (yy * blocks)), pair_sent)

        inner = jnp.logical_and(z > 0, z < 3)
        pl.when(inner)(lambda: chain(5))
        pl.when(jnp.logical_not(inner))(lambda: chain(1))

    kinds = (start, first_hop, single_hop, pair_hop, last_hop, to_core, from_core)
    return [f if i < 2 else functools.partial(f, k) for i, f in enumerate(kinds) for k in range(4)], finish


def nn(a, b):
    return lax.dot_general(a, b, (((1,), (0,)), ((), ())), preferred_element_type=F32)


def nt(a, b):
    return lax.dot_general(a, b, (((1,), (1,)), ((), ())), preferred_element_type=F32)


def tn(a, b):
    return lax.dot_general(a, b, (((0,), (0,)), ((), ())), preferred_element_type=F32)


def norm_parts(v):
    centre = jnp.mean(v, axis=-1, keepdims=True)
    shifted = v - centre
    spread = jnp.mean(shifted * shifted, axis=-1, keepdims=True)
    scaled = lax.rsqrt(spread + eps_norm)
    return shifted * scaled, scaled


def norm_back(normal, scaled, gain, upstream):
    weighted = upstream * gain
    return scaled * (
        weighted
        - jnp.mean(weighted, axis=-1, keepdims=True)
        - normal * jnp.mean(weighted * normal, axis=-1, keepdims=True)
    )


def keep(lanes, low, high):
    return jnp.where(lanes, low, high)


def layer_kernel(
    patches, lengths_in, tasks_in, master, first_moment, second_moment, gain_one, gain_two, qkv_in, out_in, u_in, d_in,
    cot_hbm, out_block, out_patch, out_task, out_stats, MIN, FIRST, SECOND,
    GP, GA, GDS, GUS, LOC, SEL, RES, N1, QKV, PT, CTX, RES2, N2, NRM1, NRM2, SC1, SC2, COT, BACK, ACT, GU, MACC, GACC, G2, G2B, DM, DC, LEADR,
    PAIR, PIN, SEND, RECV, ONEHOT, SREC, STSUM, QIN, OIN, GIN, lengths, tasks, own_sem, local_sem, send_sem, recv_sem, all_sem,
):
    net = Net(send_sem, recv_sem)
    z, x, y, c, dp, mp = net.z, net.x, net.y, net.c, net.dp, net.mp
    device = dp * 4 + mp

    barrier = pltpu.get_barrier_semaphore()
    for way, cond in (("x", None), ("y", None), ("c", None), ("u", lambda: z < 3), ("d", lambda: z > 0)):
        run_if(
            cond,
            lambda way=way: pl.semaphore_signal(
                barrier, inc=1, device_id=net.peer[way], device_id_type=MESH
            ),
        )

    def own_cols(w):
        return pl.ds(pl.multiple_of(c * w, 128), w)

    cot_copy = pltpu.make_async_copy(cot_hbm.at[pl.ds(mp * IMGS, IMGS)], COT, local_sem.at[0])
    copies = []
    for refs, widths, weight_in in ((GDS, DOWNS, d_in), (GUS, UPS, u_in)):
        first = 0
        for ref, w in zip(refs, widths):
            copies.append(
                pltpu.make_async_copy(
                    weight_in.at[:, pl.ds(first, w)], ref.at[0, y, dp, :, own_cols(w)], own_sem.at[len(copies)]
                )
            )
            first += w
    for copy in copies:
        copy.start()
    patch_copy = pltpu.make_async_copy(patches, PIN, local_sem.at[1])
    small = [
        pltpu.make_async_copy(src, dst, own_sem.at[len(copies) + i])
        for i, (src, dst) in enumerate(
            ((qkv_in, QIN), (out_in, OIN), (master, MIN), (gain_one, GIN.at[0]), (gain_two, GIN.at[1]),
             (lengths_in, lengths), (tasks_in, tasks))
        )
    ]
    for copy in small:
        copy.start()
    patch_copy.start()
    cot_copy.start()
    moments = [
        pltpu.make_async_copy(first_moment, FIRST, local_sem.at[2]),
        pltpu.make_async_copy(second_moment, SECOND, local_sem.at[3]),
    ]
    for copy in moments:
        copy.start()
    for copy in small:
        copy.wait()

    qkv = [QIN[i].astype(F32) for i in range(3)]
    outs = OIN[...].astype(F32).T
    low = lax.broadcasted_iota(jnp.int32, (96, 128), 1) < HEAD_DIM

    def tail(v, high):
        v = jnp.concatenate([v[:, 128:192], v[:, 128:192]], axis=1)
        return v

    tiles = [qkv[0][:, 0:128], qkv[1][:, 0:128], qkv[2][:, 0:128]]
    tiles.append(jnp.where(low, tail(qkv[0], 0), tail(qkv[2], 1)))
    tiles.append(jnp.where(low, tail(qkv[1], 0), tail(outs, 1)))
    tiles.append(outs[:, 0:128])
    GA[0, pl.ds(y, 1), pl.ds(dp, 1), :, own_cols(D)] = (
        jnp.concatenate(tiles, axis=1).astype(BF16)[None, None]
    )

    LOC[:, 0:PART] = MIN[...]
    lane = lax.broadcasted_iota(jnp.int32, (TASKS, PADP - PART), 1)
    LOC[:, PART:PADP] = jnp.where(
        lane == 0, tasks[0, 0].astype(F32), jnp.where(lane == 1, tasks[0, 1].astype(F32), 0.0)
    )
    half = PADP // 2
    GP[0, pl.ds(y, 1), pl.ds(dp, 1), :, own_cols(half)] = (
        jnp.concatenate([LOC[:, 0:half], LOC[:, half:PADP]], axis=0).astype(BF16)[None, None]
    )
    for copy in copies:
        copy.wait()
    inner = jnp.logical_and(z > 0, z < 3)
    run_if(lambda: inner, lambda: pl.semaphore_wait(barrier, 5))
    run_if(lambda: jnp.logical_not(inner), lambda: pl.semaphore_wait(barrier, 4))

    gathers = [gather_events(net, GP, half, (16, 16, 16, 16))]
    for ref, w, split in zip((GA, *GDS, *GUS), (D, *DOWNS, *UPS), SPLITS):
        gathers.append(gather_events(net, ref, w, split))

    g1 = GIN[0].reshape(1, D)
    g2 = GIN[1].reshape(1, D)
    limits = [lengths[b] + LEAD for b in range(IMGS)]
    live = [
        (lax.broadcasted_iota(jnp.int32, (ROWS, 1), 0) < limits[b]).astype(F32) for b in range(IMGS)
    ]

    def place_rows():
        patch_copy.wait()
        cot_copy.wait()
        for copy in moments:
            copy.wait()
        for b in range(IMGS):
            RES[b, LEAD:ROWS, :] = PIN[:, b, :].astype(F32)

    task_rows = lax.broadcasted_iota(jnp.int32, (TASKS, 1), 0)

    columns = lax.broadcasted_iota(jnp.int32, (TASKS, 128), 1)

    def pick(d, _):
        dd, mm = d // 4, d % 4
        raw = GP[0, mm // 2, dd, :, pl.ds(pl.multiple_of((mm % 2) * half, 128), half)].astype(F32)
        low, high = raw[0:8], raw[8:16]
        rep, j = d // 16, d % 16
        for b in range(IMGS):
            hot = (task_rows == tasks[0, b]).astype(F32)
            row = 2 * rep + b
            SEL[j, pl.ds(row, 1), 0:half] = jnp.sum(low * hot, axis=0, keepdims=True)
            SEL[j, pl.ds(row, 1), half:PADP] = jnp.sum(high * hot, axis=0, keepdims=True)
        base = PART - half
        for b in range(IMGS):
            which = high[0:1, base + b : base + b + 1]
            hot = (lax.broadcasted_iota(jnp.int32, (TASKS, 128), 0).astype(F32) == which).astype(F32)
            for h in range(2):
                ONEHOT[h] += jnp.where(columns == 2 * IMGS * d + 2 * b + h, hot, 0.0)
        return 0

    def place_prompts():
        ONEHOT[...] = jnp.zeros_like(ONEHOT)
        lax.fori_loop(0, NDEV, pick, 0)
        wide = lax.broadcasted_iota(jnp.int32, (4, D), 1)
        for r in range(25):
            j, off = (D * r) // PART, (D * r) % PART
            first = min(D, PART - off)
            low = SEL[j, 0:4, :]
            seg = (pltpu.roll(low, PADP - off, 1) if off else low)[:, 0:D]
            if first < D:
                seg = jnp.where(wide < first, seg, pltpu.roll(SEL[j + 1, 0:4, :], first, 1)[:, 0:D])
            for rep in range(2):
                for b in range(IMGS):
                    RES[b, 25 * rep + r : 25 * rep + r + 1, :] = seg[2 * rep + b : 2 * rep + b + 1]

    def norm_one():
        for b in range(IMGS):
            normal, SC1[b] = norm_parts(RES[b])
            NRM1[b] = normal
            N1[b] = (normal * g1).astype(BF16)

    def weight(ref, core, first, width, span):
        cols = pl.ds(pl.multiple_of(core * span + first, 128), width)
        return ref[:, :, cols].reshape(D, width)

    left = lax.broadcasted_iota(jnp.int32, (ROWS, 128), 1) < HEAD_DIM
    scale = 1.0 / math.sqrt(HEAD_DIM)
    wide = lax.broadcasted_iota(jnp.int32, (1, 640), 1)
    q_scale = jnp.where((wide < 128) | ((wide >= 384) & (wide < 448)), scale, 1.0)

    def project(m):
        w = weight(GA.at[0, m // 2], m % 2, 0, 640, D)
        mixed = nn(N1[...].reshape(IMGS * ROWS, D), w) * q_scale
        QKV[m] = mixed.astype(BF16).reshape(IMGS, ROWS, 640)

    key_rows = lax.broadcasted_iota(jnp.int32, (ROWS, ROWS), 0)
    zero = jnp.zeros((), BF16)

    def attend(t):
        b, m = t // 4, t % 4
        tile = lambda i: QKV[m, b, :, 128 * i : 128 * i + 128]
        q01, k01, v01, q2v2, k2 = (tile(i) for i in range(5))
        mask = key_rows < (lengths[b] + LEAD)

        def soft(keys, queries):
            s = jnp.where(mask, nt(keys, queries), -1e30)
            e = jnp.exp(s - jnp.max(s, axis=0, keepdims=True))
            return (e * (1.0 / jnp.sum(e, axis=0, keepdims=True))).astype(BF16)

        p0 = soft(k01, keep(left, q01, zero))
        p1 = soft(k01, keep(left, zero, q01))
        p2 = soft(k2, keep(left, q2v2, zero))
        PT[t, 0], PT[t, 1], PT[t, 2] = p0, p1, p2
        CTX[b, :, m * 256 : m * 256 + 128] = keep(left, 0.0, tn(p2, q2v2)).astype(BF16)
        CTX[b, :, m * 256 + 128 : m * 256 + 256] = keep(
            left, tn(p0, v01), tn(p1, v01)
        ).astype(BF16)

    def attend_two(t):
        attend(2 * t)
        attend(2 * t + 1)

    sums = [jnp.zeros((1, 1), F32) for _ in range(3)]

    def total(v):
        return jnp.sum(jnp.sum(v, axis=0, keepdims=True), axis=1, keepdims=True)

    def project_out(b):
        attn = jnp.zeros((ROWS, D), F32)
        for m in range(4):
            attn += nt(CTX[b, :, 256 * m : 256 * m + 256], weight(GA.at[0, m // 2], m % 2, 512, 256, D))
        sums[1] += total(attn * attn * live[b])
        res2 = RES[b] + attn
        RES2[b] = res2
        normal, SC2[b] = norm_parts(res2)
        NRM2[b] = normal
        N2[b] = (normal * g2).astype(BF16)

    def back_units(i, yy):
        w, first = DOWNS[i], sum(DOWNS[:i])
        cot = COT[...].reshape(IMGS * ROWS, D)
        for core in range(2):
            back = nn(cot, weight(GDS[i].at[0, yy], core, 0, w, w))
            BACK[yy, :, core * D + first : core * D + first + w] = back.astype(BF16)

    def up_units(i, core):
        w, first = UPS[i], sum(UPS[:i])
        rows2 = N2[...].reshape(IMGS * ROWS, D)
        here = pl.ds(pl.multiple_of(core * w, 128), w)
        for yy in range(2):
            up = nn(rows2, weight(GUS[i].at[0, yy], core, 0, w, w))
            back = BACK[yy, :, pl.ds(pl.multiple_of(core * D + first, 128), w)].astype(F32)
            cumul = 0.5 * (1.0 + lax.erf(up * 0.7071067811865476))
            density = jnp.exp(-0.5 * up * up) * 0.3989422804014327
            ACT[yy, :, here] = (up * cumul).astype(BF16)
            GU[yy, :, here] = (back * (cumul + up * density)).astype(BF16)

    def add_grad(i, yy):
        w = UPS[i]
        grad = nt(GU[yy, :, 0 : 2 * w], weight(GUS[i].at[0, yy], 0, 0, 2 * w, w)).reshape(IMGS, ROWS, D)
        if i == 0 and yy == 0:
            GACC[...] = grad
        else:
            GACC[...] += grad

    def add_mlp(i, yy):
        w, first = UPS[i], sum(UPS[:i])
        d = max(d for d in range(len(DOWNS)) if sum(DOWNS[:d]) <= first)
        inside = first - sum(DOWNS[:d])
        if w == DOWNS[d]:
            mlp = nt(ACT[yy, :, 0 : 2 * w], weight(GDS[d].at[0, yy], 0, 0, 2 * w, w))
        else:
            mlp = sum(
                nt(ACT[yy, :, w * core : w * (core + 1)], weight(GDS[d].at[0, yy], core, inside, w, DOWNS[d]))
                for core in range(2)
            )
        mlp = mlp.reshape(IMGS, ROWS, D)
        if i == 0 and yy == 0:
            MACC[...] = mlp
        else:
            MACC[...] += mlp

    def add_units(i, yy):
        add_grad(i, yy)
        if i < len(UPS) - 1:
            add_mlp(i, yy)

    steps = [place_rows, place_prompts, norm_one]
    steps += [functools.partial(project, m) for m in range(4)]
    steps += [functools.partial(attend_two, t) for t in range(4)]
    steps += [functools.partial(project_out, b) for b in range(IMGS)]
    steps += [functools.partial(back_units, i, yy) for i in range(len(DOWNS)) for yy in range(2)]
    for i in range(len(UPS)):
        steps += [functools.partial(up_units, i, c), functools.partial(up_units, i, 1 - c)]
        steps += [functools.partial(add_units, i, yy) for yy in range(2)]
    for item in ORDER:
        if item < 1000:
            gathers[item // 28][0][item % 28]()
        else:
            steps[item - 1000]()

    for b in range(IMGS):
        g = COT[b].astype(F32) + norm_back(NRM2[b], SC2[b], g2, GACC[b])
        G2[b] = g
        G2B[b] = g.astype(BF16)

    for m in range(4):
        cols = pl.ds(pl.multiple_of((m % 2) * D + 512, 128), 256)
        w = GA[0, m // 2, :, :, cols].reshape(D, 256)
        DC[m] = nn(G2B[...].reshape(IMGS * ROWS, D), w).astype(BF16).reshape(IMGS, ROWS, 256)

    def attend_back(b):
        tiles, grad_probs, grad_scores = [], [], []
        for m in range(4):
            tiles.append(
                [QKV[m, b, :, 128 * i : 128 * i + 128] for i in range(5)]
                + [DC[m, b, :, 0:128], DC[m, b, :, 128:256]]
            )
            q01, k01, v01, q2v2, k2, c2, c01 = tiles[m]
            grad_probs.append(
                [nt(keep(left, v01, zero), c01), nt(keep(left, zero, v01), c01), nt(keep(left, zero, q2v2), c2)]
            )
        for m in range(4):
            out = []
            for h in range(3):
                pf, dp_ = PT[4 * b + m, h].astype(F32), grad_probs[m][h]
                inner = jnp.sum(pf * dp_, axis=0, keepdims=True)
                out.append((pf * (dp_ - inner)).astype(BF16))
            grad_scores.append(out)
        for m in range(4):
            q01, k01, v01, q2v2, k2, c2, c01 = tiles[m]
            s0, s1, s2 = grad_scores[m]
            p0, p1, p2 = (PT[4 * b + m, h] for h in range(3))
            DM[m, b, :, 0:128] = (keep(left, tn(s0, k01), tn(s1, k01)) * scale).astype(BF16)
            DM[m, b, :, 128:256] = keep(left, nn(s0, q01), nn(s1, q01)).astype(BF16)
            DM[m, b, :, 256:384] = keep(left, nn(p0, c01), nn(p1, c01)).astype(BF16)
            DM[m, b, :, 384:512] = keep(left, tn(s2, k2) * scale, nn(p2, c2)).astype(BF16)
            DM[m, b, :, 512:640] = keep(left, nn(s2, q2v2), 0.0).astype(BF16)

    def grad_rows(rows, first, last):
        count = last - first
        grad = jnp.zeros((len(rows) * count, D), F32)
        for m in range(4):
            mixed = jnp.concatenate([DM[m, b, first:last] for b in rows], axis=0)
            grad += nt(mixed, weight(GA.at[0, m // 2], m % 2, 0, 640, D))
        for i, b in enumerate(rows):
            part = grad[count * i : count * (i + 1)]
            GACC[b, first:last] = G2[b, first:last] + norm_back(NRM1[b, first:last], SC1[b, first:last], g1, part)

    def to_others(src, dst, sems, mirror=False):
        for step in (7, 6, 5, 4, 3, 2, 1, 0) if mirror else (4, 5, 3, 6, 2, 7, 1, 0):
            to_dp = dp ^ step if mirror else (dp + step) & 7
            for turn in range(4):
                if step or turn:
                    to_mp = (mp + turn) & 3
                    pltpu.make_async_remote_copy(
                        src_ref=src(to_dp * 4 + to_mp),
                        dst_ref=dst,
                        send_sem=all_sem.at[sems],
                        recv_sem=all_sem.at[sems + 1],
                        device_id=(to_dp, to_mp),
                        device_id_type=MESH,
                    ).start()

    wide = lax.broadcasted_iota(jnp.int32, (4, PADP), 1)

    def to_owners():
        for rep in range(2):
            for b in range(IMGS):
                LEADR[:, 2 * rep + b : 2 * rep + b + 1, :] = GACC[b, 25 * rep : 25 * rep + 25, :][:, None, :]
        for q in range(16):
            r, off = (PART * q) // D, (PART * q) % D
            msg, have = None, -off
            while have < PART:
                row = LEADR[r]
                moved = pltpu.roll(row, have % D, 1) if have % D else row
                moved = jnp.concatenate([moved, moved[:, 0 : PADP - D]], axis=1)
                msg = moved if msg is None else jnp.where(wide < have, msg, moved)
                have += D
                r += 1
            msg = jnp.where(wide < PART, msg, 0.0).astype(BF16)
            for rep in range(2):
                SEND[16 * rep + q] = jnp.concatenate(
                    [msg[2 * rep + b : 2 * rep + b + 1, half * h : half * h + half] for b in range(IMGS) for h in range(2)],
                    axis=0,
                )
        to_others(lambda other: SEND.at[other], RECV.at[device], 0)
        RECV[pl.ds(device, 1)] = SEND[pl.ds(device, 1)]

    def others(ref):
        return ref.at[pl.ds(0, NDEV - 1)]

    def wait_all(ref, sem):
        pltpu.make_async_copy(others(ref), others(ref), all_sem.at[sem]).wait()

    some = 64
    for b in range(IMGS):
        attend_back(b)
    grad_rows((0, 1), 0, some)
    to_owners()

    grad_rows((0, 1), some, ROWS)
    for yy in range(2):
        add_mlp(len(UPS) - 1, yy)
    for b in range(IMGS):
        mlp = MACC[b]
        block = RES2[b] + mlp
        out_block[b] = block.astype(BF16)
        sums[0] += total(block * block * live[b])
        sums[2] += total(mlp * mlp * live[b])

    wait_all(RECV, 1)

    came = RECV[...].reshape(2 * IMGS * NDEV, half)
    acc = [nn(ONEHOT[h].astype(BF16), came) for h in range(2)]
    square = total(acc[0] * acc[0]) + total(acc[1] * acc[1])
    lane = lax.broadcasted_iota(jnp.int32, (1, 128), 1)
    count = (limits[0] + limits[1]).astype(F32)
    stats = jnp.zeros((1, 128), F32)
    for i, v in enumerate((square, sums[0], sums[1], sums[2], count)):
        stats = jnp.where(lane == i, v, stats)
    STSUM[...] = stats
    SREC[pl.ds(device, 1)] = stats[None]
    to_others(lambda other: STSUM, SREC.at[device], 2, mirror=True)

    out_task[...] = jnp.concatenate(acc, axis=1)[:, 0:PART]
    for b in range(IMGS):
        PAIR[:, b : b + 1, :] = GACC[b, LEAD:ROWS, :][:, None, :]
    out_patch[...] = PAIR[...].astype(BF16)
    wait_all(RECV, 0)
    for gather in gathers:
        gather[1]()
    wait_all(SREC, 3)
    out_stats[...] = jnp.sum(SREC[...], axis=0)
    wait_all(SREC, 2)


def update_kernel(
    task_grad, stats, master, first_moment, second_moment, block_in, patch_in,
    out_grad, out_first, out_second, out_master, out_copy, out_norm, out_rms, block_out, patch_out, sem,
):
    copies = [
        pltpu.make_async_copy(block_in, block_out, sem.at[0]),
        pltpu.make_async_copy(patch_in, patch_out, sem.at[1]),
    ]
    for copy in copies:
        copy.start()
    st = stats[0:1, :]
    norm = jnp.sqrt(st[0:1, 0:1])
    grad = task_grad[...] * (clip_level / jnp.maximum(norm, clip_level))
    first = beta_one * first_moment[...] + (1.0 - beta_one) * grad
    second = beta_two * second_moment[...] + (1.0 - beta_two) * grad * grad
    step_size = (
        first / (1.0 - beta_one**STEP) / (jnp.sqrt(second / (1.0 - beta_two**STEP)) + adam_eps)
    )
    old = master[...]
    new = old - learn_rate * (step_size + decay_rate * old)
    out_grad[...] = grad
    out_first[...] = first
    out_second[...] = second
    out_master[...] = new
    out_copy[...] = new.astype(BF16)
    out_norm[0] = norm[0, 0]
    rms = jnp.sqrt(st / (st[0:1, 4:5] * D))
    for i in range(3):
        out_rms[i] = rms[0, i + 1]
    for copy in copies:
        copy.wait()


def fast_body(
    patches, lengths, tasks, prompt_master, first_moment, second_moment,
    gain_one, gain_two, w_qkv, w_out, w_up, w_down, cotangent,
):
    vmem = pl.BlockSpec(memory_space=pltpu.VMEM)
    smem = pl.BlockSpec(memory_space=pltpu.SMEM)
    anywhere = pl.BlockSpec(memory_space=pl.ANY)
    V = pltpu.VMEM
    block, patch, *states = pl.pallas_call(
        layer_kernel,
        out_shape=[
            V((IMGS, ROWS, D), BF16),
            V((PATCH, IMGS, D), BF16),
            V((TASKS, PART), F32),
            V((1, 128), F32),
        ]
        + [V((TASKS, PART), F32)] * 3,
        in_specs=[anywhere] * 13,
        out_specs=[vmem] * 7,
        scratch_shapes=[
            V((1, 2, 8, 16, PADP), BF16),
            V((1, 2, 8, 96, 2 * D), BF16),
            [V((1, 2, 8, 96, 2 * w), BF16) for w in DOWNS],
            [V((1, 2, 8, 96, 2 * w), BF16) for w in UPS],
            V((TASKS, PADP), F32),
            V((16, 4, PADP), F32),
            V((IMGS, ROWS, D), F32),
            V((IMGS, ROWS, D), BF16),
            V((4, IMGS, ROWS, 640), BF16),
            V((8, 3, ROWS, ROWS), BF16),
            V((IMGS, ROWS, 1024), BF16),
            V((IMGS, ROWS, D), F32),
            V((IMGS, ROWS, D), BF16),
            V((IMGS, ROWS, D), F32),
            V((IMGS, ROWS, D), F32),
            V((IMGS, ROWS, 1), F32),
            V((IMGS, ROWS, 1), F32),
            V((IMGS, ROWS, D), BF16),
            V((2, IMGS * ROWS, 2 * D), BF16),
            V((2, IMGS * ROWS, 2 * max(UPS)), BF16),
            V((2, IMGS * ROWS, 2 * max(UPS)), BF16),
            V((IMGS, ROWS, D), F32),
            V((IMGS, ROWS, D), F32),
            V((IMGS, ROWS, D), F32),
            V((IMGS, ROWS, D), BF16),
            V((4, IMGS, ROWS, 640), BF16),
            V((4, IMGS, ROWS, 256), BF16),
            V((25, 4, D), F32),
            V((PATCH, IMGS, D), F32),
            V((PATCH, IMGS, D), BF16),
            V((NDEV, 2 * IMGS, PADP // 2), BF16),
            V((NDEV, 2 * IMGS, PADP // 2), BF16),
            V((2, TASKS, 128), F32),
            V((NDEV, 1, 128), F32),
            V((1, 128), F32),
            V((3, 96, 192), BF16),
            V((192, 96), BF16),
            V((2, D), F32),
            pltpu.SMEM((IMGS,), jnp.int32),
            pltpu.SMEM((1, IMGS), jnp.int32),
            pltpu.SemaphoreType.DMA((7 + len(DOWNS) + len(UPS),)),
            pltpu.SemaphoreType.DMA((4,)),
            pltpu.SemaphoreType.DMA((6 * (2 + len(DOWNS) + len(UPS)),)),
            pltpu.SemaphoreType.DMA((9 + 16 * (1 + len(DOWNS) + len(UPS)),)),
            pltpu.SemaphoreType.DMA((4,)),
        ],
        compiler_params=pltpu.CompilerParams(
            collective_id=0, has_side_effects=True, vmem_limit_bytes=58 << 20
        ),
    )(
        patches.transpose(1, 0, 2), lengths, tasks.T, prompt_master, first_moment, second_moment, gain_one, gain_two,
        w_qkv.transpose(1, 0, 2), w_out, w_up, w_down.T, cotangent,
    )
    state = jax.ShapeDtypeStruct((TASKS, PART), F32)

    def keep_near(v):
        return pltpu.with_memory_space_constraint(v, pltpu.VMEM)

    grad, first, second, master, copy, norm, rms, block_out, patch_out = pl.pallas_call(
        update_kernel,
        out_shape=[state] * 4
        + [
            jax.ShapeDtypeStruct((TASKS, PART), BF16),
            jax.ShapeDtypeStruct((1,), F32),
            jax.ShapeDtypeStruct((3,), F32),
            jax.ShapeDtypeStruct((IMGS, ROWS, D), BF16),
            jax.ShapeDtypeStruct((PATCH, IMGS, D), BF16),
        ],
        in_specs=[vmem] * 7,
        out_specs=[vmem] * 5 + [smem] * 2 + [anywhere] * 2,
        scratch_shapes=[pltpu.SemaphoreType.DMA((2,))],
    )(*(keep_near(v) for v in (*states, block, patch)))
    return (
        block_out, patch_out.transpose(1, 0, 2), grad, norm.reshape(()), first, second, master, copy, rms,
    )


def layer_norm(values, gain):
    centre = jnp.mean(values, axis=-1, keepdims=True)
    shifted = values - centre
    spread = jnp.mean(shifted * shifted, axis=-1, keepdims=True)
    return shifted * lax.rsqrt(spread + eps_norm) * gain


def whole_norm_back(values, gain, upstream):
    centre = jnp.mean(values, axis=-1, keepdims=True)
    shifted = values - centre
    spread = jnp.mean(shifted * shifted, axis=-1, keepdims=True)
    scaled = lax.rsqrt(spread + eps_norm)
    normal_part = shifted * scaled
    weighted = upstream * gain
    return scaled * (
        weighted
        - jnp.mean(weighted, axis=-1, keepdims=True)
        - normal_part * jnp.mean(weighted * normal_part, axis=-1, keepdims=True)
    )


def gelu_slope(upward):
    cumul = 0.5 * (1.0 + lax.erf(upward * 0.7071067811865476))
    density = jnp.exp(-0.5 * upward * upward) * 0.3989422804014327
    return cumul + upward * density


def attend_forward(group_normed, group_limit, w_mix, block_images):
    group_size, row_count, feature_count = group_normed.shape
    lane_width = w_mix.shape[2]
    head_count = lane_width // HEAD_DIM
    scale = 1.0 / math.sqrt(HEAD_DIM)
    mask_all = jnp.arange(row_count, dtype=jnp.int32)[None, :] < group_limit[:, None]

    def one_block(block_index):
        first_row = block_index * block_images
        block_in = lax.dynamic_slice_in_dim(group_normed, first_row, block_images, 0)
        key_mask = lax.dynamic_slice_in_dim(mask_all, first_row, block_images, 0)
        mixed_qkv = jnp.einsum(
            "brd,dce->brce", block_in, w_mix, preferred_element_type=jnp.float32
        ).astype(jnp.bfloat16)
        split_heads = mixed_qkv.reshape(block_images, row_count, 3, head_count, HEAD_DIM)
        scores = (
            jnp.einsum(
                "bqhe,bkhe->bhqk",
                split_heads[:, :, 0],
                split_heads[:, :, 1],
                preferred_element_type=jnp.float32,
            )
            * scale
        )
        scores = jnp.where(key_mask[:, None, None, :], scores, -1e30)
        row_top = jnp.max(scores, axis=-1, keepdims=True)
        exponent = jnp.exp(scores - row_top)
        row_total = jnp.sum(exponent, axis=-1, keepdims=True)
        attend_weights = (exponent / row_total).astype(jnp.bfloat16)
        context = jnp.einsum(
            "bhqk,bkhe->bqhe",
            attend_weights,
            split_heads[:, :, 2],
            preferred_element_type=jnp.float32,
        )
        context = context.astype(jnp.bfloat16).reshape(block_images, row_count, lane_width)
        return (mixed_qkv, context, (row_top + jnp.log(row_total))[..., 0])

    mixed_qkv, context, logsums = lax.map(
        one_block, jnp.arange(group_size // block_images, dtype=jnp.int32)
    )
    return (
        mixed_qkv.reshape(group_size, row_count, 3, lane_width),
        context.reshape(group_size, row_count, lane_width),
        logsums.reshape(group_size, head_count, row_count),
    )


def attend_back(mixed_qkv, logsums, group_limit, grad_context, block_images):
    group_size, row_count, three_parts, lane_width = mixed_qkv.shape
    head_count = lane_width // HEAD_DIM
    scale = 1.0 / math.sqrt(HEAD_DIM)
    mask_all = jnp.arange(row_count, dtype=jnp.int32)[None, :] < group_limit[:, None]

    def one_block(block_index):
        first_row = block_index * block_images
        split_heads = lax.dynamic_slice_in_dim(mixed_qkv, first_row, block_images, 0).reshape(
            block_images, row_count, 3, head_count, HEAD_DIM
        )
        queries = split_heads[:, :, 0]
        keys_all = split_heads[:, :, 1]
        values = split_heads[:, :, 2]
        key_mask = lax.dynamic_slice_in_dim(mask_all, first_row, block_images, 0)
        logsum = lax.dynamic_slice_in_dim(logsums, first_row, block_images, 0)
        grad_out = lax.dynamic_slice_in_dim(grad_context, first_row, block_images, 0).reshape(
            block_images, row_count, head_count, HEAD_DIM
        )
        scores = (
            jnp.einsum("bqhe,bkhe->bhqk", queries, keys_all, preferred_element_type=jnp.float32)
            * scale
        )
        scores = jnp.where(key_mask[:, None, None, :], scores, -1e30)
        attend_weights = jnp.exp(scores - logsum[..., None])
        grad_weights = jnp.einsum(
            "bqhe,bkhe->bhqk", grad_out, values, preferred_element_type=jnp.float32
        )
        row_inner = jnp.sum(attend_weights * grad_weights, axis=-1, keepdims=True)
        grad_scores = (attend_weights * (grad_weights - row_inner)).astype(jnp.bfloat16)
        grad_query = (
            jnp.einsum("bhqk,bkhe->bqhe", grad_scores, keys_all, preferred_element_type=jnp.float32)
            * scale
        )
        grad_key = (
            jnp.einsum("bhqk,bqhe->bkhe", grad_scores, queries, preferred_element_type=jnp.float32)
            * scale
        )
        grad_value = jnp.einsum(
            "bhqk,bqhe->bkhe",
            attend_weights.astype(jnp.bfloat16),
            grad_out,
            preferred_element_type=jnp.float32,
        )
        stacked = jnp.stack([grad_query, grad_key, grad_value], axis=2).astype(jnp.bfloat16)
        return stacked.reshape(block_images, row_count, 3, lane_width)

    grad_mixed = lax.map(one_block, jnp.arange(group_size // block_images, dtype=jnp.int32))
    return grad_mixed.reshape(group_size, row_count, 3, lane_width)


def expand_units(group_two, w_expand, block_images):
    group_size, row_count, feature_count = group_two.shape

    def one_block(block_index):
        block_in = lax.dynamic_slice_in_dim(group_two, block_index * block_images, block_images, 0)
        upward = jnp.einsum("brd,df->brf", block_in, w_expand, preferred_element_type=jnp.float32)
        return jax.nn.gelu(upward, approximate=False).astype(jnp.bfloat16)

    act_units = lax.map(one_block, jnp.arange(group_size // block_images, dtype=jnp.int32))
    return act_units.reshape(group_size, row_count, w_expand.shape[1])


def units_back(grad_group, group_two, w_expand, w_reduce, block_images):
    group_size, row_count, feature_count = group_two.shape

    def one_block(block_index):
        first_row = block_index * block_images
        grad_in = lax.dynamic_slice_in_dim(grad_group, first_row, block_images, 0)
        norm_in = lax.dynamic_slice_in_dim(group_two, first_row, block_images, 0)
        back_units = jnp.einsum(
            "brd,fd->brf", grad_in, w_reduce, preferred_element_type=jnp.float32
        )
        upward = jnp.einsum("brd,df->brf", norm_in, w_expand, preferred_element_type=jnp.float32)
        return (back_units * gelu_slope(upward)).astype(jnp.bfloat16)

    grad_units = lax.map(one_block, jnp.arange(group_size // block_images, dtype=jnp.int32))
    return grad_units.reshape(group_size, row_count, w_expand.shape[1])


def rows_term(source, weight, form):
    return jnp.einsum(form, source, weight, preferred_element_type=jnp.float32)


def body(
    patches,
    lengths,
    tasks,
    prompt_master,
    first_moment,
    second_moment,
    gain_one,
    gain_two,
    w_qkv,
    w_out,
    w_up,
    w_down,
    cotangent,
):
    held_count, patch_count, feature_count = patches.shape
    row_count = cotangent.shape[1]
    lead_count = row_count - patch_count
    task_count = prompt_master.shape[0]
    prompt_table = lax.all_gather(
        prompt_master.astype(jnp.bfloat16), ("dp", "mp"), axis=1, tiled=True
    )
    chosen = tasks == jnp.arange(task_count, dtype=jnp.int32)[None, :]
    lead_part = jnp.dot(
        chosen.astype(jnp.bfloat16), prompt_table, preferred_element_type=jnp.float32
    )
    residual = jnp.concatenate(
        [lead_part.reshape(held_count, lead_count, feature_count), patches.astype(jnp.float32)],
        axis=1,
    )
    row_limit = lengths + lead_count
    w_mix, w_expand, w_reduce, w_rows = (
        lax.all_gather(w_qkv, "dp", axis=0, tiled=True),
        lax.all_gather(w_up, "dp", axis=0, tiled=True),
        lax.all_gather(w_down, "dp", axis=1, tiled=True),
        lax.all_gather(w_out, "dp", axis=1, tiled=True),
    )
    normed = layer_norm(residual, gain_one).astype(jnp.bfloat16)
    mp_rank = lax.axis_index("mp")
    group_normed, group_bound = (
        lax.all_gather(normed, "mp", axis=0, tiled=True),
        lax.all_gather(row_limit.astype(jnp.bfloat16), "mp", axis=0, tiled=True),
    )
    group_limit = group_bound.astype(jnp.int32)
    mixed_qkv, context, logsums = attend_forward(group_normed, group_limit, w_mix, held_count)
    attn_out = lax.psum_scatter(
        rows_term(context, w_rows, "brc,cd->brd"), "mp", scatter_dimension=0, tiled=True
    )
    residual_two = residual + attn_out
    normed_two = layer_norm(residual_two, gain_two).astype(jnp.bfloat16)
    group_two = lax.all_gather(normed_two, "mp", axis=0, tiled=True)
    act_units = expand_units(group_two, w_expand, held_count)
    mlp_out = lax.psum_scatter(
        rows_term(act_units, w_reduce, "brf,fd->brd").astype(jnp.bfloat16),
        "mp",
        scatter_dimension=0,
        tiled=True,
    ).astype(jnp.float32)
    block_sum = residual_two + mlp_out
    live_rows = (jnp.arange(row_count, dtype=jnp.int32)[None, :] < row_limit[:, None]).astype(
        jnp.float32
    )[:, :, None]
    square_sums = jnp.stack(
        [
            jnp.sum(block_sum * block_sum * live_rows),
            jnp.sum(attn_out * attn_out * live_rows),
            jnp.sum(mlp_out * mlp_out * live_rows),
        ]
    )
    live_count = jnp.sum(row_limit).astype(jnp.float32)
    w_mix, w_expand, w_reduce, w_rows = (
        lax.all_gather(w_qkv, "dp", axis=0, tiled=True),
        lax.all_gather(w_up, "dp", axis=0, tiled=True),
        lax.all_gather(w_down, "dp", axis=1, tiled=True),
        lax.all_gather(w_out, "dp", axis=1, tiled=True),
    )
    grad_held = lax.dynamic_slice_in_dim(cotangent, mp_rank * held_count, held_count, 0)
    grad_units = units_back(cotangent, group_two, w_expand, w_reduce, held_count)
    grad_normed_two = lax.psum_scatter(
        rows_term(grad_units, w_expand, "brf,df->brd"), "mp", scatter_dimension=0, tiled=True
    )
    grad_two = grad_held.astype(jnp.float32) + whole_norm_back(residual_two, gain_two, grad_normed_two)
    grad_low = grad_two.astype(jnp.bfloat16)
    grad_context = jnp.einsum(
        "brd,cd->brc",
        lax.all_gather(grad_low, "mp", axis=0, tiled=True),
        w_rows,
        preferred_element_type=jnp.float32,
    ).astype(jnp.bfloat16)
    grad_mixed = attend_back(mixed_qkv, logsums, group_limit, grad_context, held_count)
    grad_normed = lax.psum_scatter(
        rows_term(grad_mixed, w_mix, "brce,dce->brd").astype(jnp.bfloat16),
        "mp",
        scatter_dimension=0,
        tiled=True,
    ).astype(jnp.float32)
    grad_residual = grad_two + whole_norm_back(residual, gain_one, grad_normed)
    patch_grad = grad_residual[:, lead_count:].astype(jnp.bfloat16)
    lead_grad = grad_residual[:, :lead_count].reshape(held_count, lead_count * feature_count)
    task_term = jnp.dot(
        chosen.astype(jnp.float32).T,
        lead_grad,
        precision=lax.Precision.HIGHEST,
        preferred_element_type=jnp.float32,
    )
    task_grad = lax.psum_scatter(task_term, ("dp", "mp"), scatter_dimension=1, tiled=True)
    square = jnp.sum(task_grad * task_grad)
    square, square_sums, live_count = lax.psum((square, square_sums, live_count), ("dp", "mp"))
    grad_norm = jnp.sqrt(square)
    prompt_grad = task_grad * (clip_level / jnp.maximum(grad_norm, clip_level))
    new_first = beta_one * first_moment + (1.0 - beta_one) * prompt_grad
    new_second = beta_two * second_moment + (1.0 - beta_two) * prompt_grad * prompt_grad
    step_size = (
        new_first
        / (1.0 - beta_one**STEP)
        / (jnp.sqrt(new_second / (1.0 - beta_two**STEP)) + adam_eps)
    )
    new_master = prompt_master - learn_rate * (step_size + decay_rate * prompt_master)
    rms_stats = jnp.sqrt(square_sums / (live_count * feature_count))
    return (
        block_sum.astype(jnp.bfloat16),
        patch_grad,
        prompt_grad,
        grad_norm,
        new_first,
        new_second,
        new_master,
        new_master.astype(jnp.bfloat16),
        rms_stats,
    )


def solution(mesh):
    small = mesh.shape["dp"] == 8 and mesh.shape["mp"] == 4
    return jax.shard_map(
        fast_body if small else body,
        mesh=mesh,
        in_specs=(
            P(("dp", "mp"), None, None),
            P(("dp", "mp")),
            P(("dp", "mp"), None),
            P(None, ("dp", "mp")),
            P(None, ("dp", "mp")),
            P(None, ("dp", "mp")),
            P(),
            P(),
            P("dp", None, "mp"),
            P("mp", "dp"),
            P("dp", "mp"),
            P("mp", "dp"),
            P("dp", None, None),
        ),
        out_specs=(
            P(("dp", "mp"), None, None),
            P(("dp", "mp"), None, None),
            P(None, ("dp", "mp")),
            P(),
            P(None, ("dp", "mp")),
            P(None, ("dp", "mp")),
            P(None, ("dp", "mp")),
            P(None, ("dp", "mp")),
            P(),
        ),
        check_vma=False,
    )
```
